32 devices in a mesh: fsdp: 4 (over y, x), ctx: 8 (over z, core).
Axes of the slice: x: 2, y: 2, z: 4, core: 2. Of those that a mesh axis runs over, the one named last changes fastest.
Arguments:
- tokens: bfloat16 [4096, 2048], P(('fsdp', 'ctx')), may hold values from -6 to 6
- cotangent: bfloat16 [4096, 2048], P(('fsdp', 'ctx')), may hold values from -6 to 6
- doc_lengths: int32 [4, 4], P('fsdp'), may hold values from 1 to 1021, as said below
- gain_attn: bfloat16 [2048], P(('fsdp', 'ctx')), may hold values from 0.5 to 1.5
- w_query: bfloat16 [2048, 2048], P(('fsdp', 'ctx')), may hold values from -0.125 to 0.125
- w_key: bfloat16 [2048, 2048], P(('fsdp', 'ctx')), may hold values from -0.125 to 0.125
- w_value: bfloat16 [2048, 2048], P(('fsdp', 'ctx')), may hold values from -0.125 to 0.125
- w_out: bfloat16 [2048, 2048], P(('fsdp', 'ctx')), may hold values from -1 to 1
- gain_mlp: bfloat16 [2048], P(('fsdp', 'ctx')), may hold values from 0.5 to 1.5
- w_gate: bfloat16 [2048, 8192], P(('fsdp', 'ctx')), may hold values from -0.125 to 0.125
- w_up: bfloat16 [2048, 8192], P(('fsdp', 'ctx')), may hold values from -0.125 to 0.125
- w_down: bfloat16 [2048, 8192], P(('fsdp', 'ctx')), may hold values from -0.0625 to 0.0625
Outputs:
- layer_out: bfloat16 [4096, 2048], P(('fsdp', 'ctx'))
- grad_tokens: float32 [4096, 2048], P(('fsdp', 'ctx'))
- grad_gain_attn: float32 [2048], P(('fsdp', 'ctx'))
- grad_query: float32 [2048, 2048], P(('fsdp', 'ctx'))
- grad_key: float32 [2048, 2048], P(('fsdp', 'ctx'))
- grad_value: float32 [2048, 2048], P(('fsdp', 'ctx'))
- grad_out: float32 [2048, 2048], P(('fsdp', 'ctx'))
- grad_gain_mlp: float32 [2048], P(('fsdp', 'ctx'))
- grad_gate: float32 [2048, 8192], P(('fsdp', 'ctx'))
- grad_up: float32 [2048, 8192], P(('fsdp', 'ctx'))
- grad_down: float32 [2048, 8192], P(('fsdp', 'ctx'))
The draws below stay inside these ranges and needn't reach their ends.
Inputs may be any that keep to these rules, and one draw needn't show every extreme that they name: `doc_lengths`: row g holds the lengths of the 4 documents packed in order into the g-th group of 1024 rows of tokens; each row sums to 1024.
All inputs are finite; a program needn't handle non-finite values.
Results may differ from the reference program's by a relative error of at most 0.014.
Values may be sent and summed in bfloat16 or wider, within the bound.
No kernel may reach another device: no remote copies, remote signals or barrier semaphores. Data moves between devices by JAX's collectives and lax.ppermute only.
A program may use at most 320 MiB of HBM per device.

```python
import jax
import jax.numpy as jnp
from jax import lax

D = 2048
H = 32
HD = 64
FF = 8192
TOK_DEV = 128
DOCS = 4
GROUP = 1024
TOKENS = 4096
N_FSDP = 4


def draw_doc_lengths(key, part):
    key = jax.random.fold_in(key, 11)
    pick_key, size_key, row_key = jax.random.split(key, 3)
    longest = jax.random.randint(pick_key, (N_FSDP, 1), 0, DOCS)
    short_sizes = jax.random.randint(size_key, (N_FSDP, DOCS), 1, TOK_DEV // DOCS + 1)
    single_row = jax.random.randint(row_key, (), 0, N_FSDP)
    rows = jnp.arange(N_FSDP, dtype=jnp.int32)[:, None]
    short_sizes = jnp.where(rows == single_row, 1, short_sizes)
    slots = jnp.arange(DOCS, dtype=jnp.int32)[None, :]
    chosen = slots == longest
    others = jnp.sum(jnp.where(chosen, 0, short_sizes), axis=1, keepdims=True)
    return jnp.where(chosen, GROUP - others, short_sizes).astype(jnp.int32)


def with_spikes(drawn, key, source, target, parts, factor):
    owner, partner = [(jnp.arange(drawn.shape[axis_at]) // (drawn.shape[axis_at] // parts)).reshape([-1 if axis == axis_at else 1 for axis in range(drawn.ndim)]) for axis_at in (source, target)]
    chosen = jax.random.permutation(key, parts)[partner]
    strong = (owner == chosen) | (owner == (partner + parts // 2) % parts)
    return jnp.where(strong, factor * drawn, drawn)


def levels(own_key, dims, cuts, low, largest):
    gain = 1.0
    for dim, blocks in cuts:
        draws = jax.random.uniform(jax.random.fold_in(jax.random.fold_in(own_key, 6), dim), (blocks,), jnp.float32, low / len(cuts), largest / len(cuts))
        gain = gain * jnp.repeat(jnp.exp(draws), dims[dim] // blocks).reshape((-1,) + (1,) * (len(dims) - 1 - dim))
    return gain


def noise(rng, shape, scale, limit, cuts=(), kind=jnp.bfloat16):
    entries = scale * jax.random.normal(rng, shape, jnp.float32)
    if cuts:
        entries = entries * levels(rng, shape, cuts, -0.22, 0.18)
    return jnp.clip(entries, -limit, limit).astype(kind)


def noise_with(rng, dims, spread, bound, cuts, heavy, kind=jnp.bfloat16):
    entries = spread * jax.random.normal(rng, dims, jnp.float32)
    if cuts:
        entries = entries * levels(rng, dims, cuts, -0.22, 0.18)
    return jnp.clip(with_spikes(entries, jax.random.fold_in(rng, 3), *heavy), -bound, bound).astype(kind)


def setup_inputs(seed: int = 0) -> dict:
    seeds = jax.random.split(jax.random.key(seed), 13)
    return {
        "tokens": noise_with(seeds[0], (TOKENS, D), 1.0, 6.0, ((0, 32),), (0, 1, 32, 2.75)),
        "cotangent": noise(seeds[1], (TOKENS, D), 1.0, 6.0, ((0, 32),)),
        "doc_lengths": draw_doc_lengths(jax.random.fold_in(seeds[12], 71), 0),
        "gain_attn": jnp.clip(1.0 + 0.1 * jax.random.normal(seeds[3], (D,), jnp.float32), 0.5, 1.5).astype(jnp.bfloat16),
        "w_query": noise(seeds[4], (D, D), D ** -0.5, 0.125, ((0, 32),)),
        "w_key": noise(seeds[5], (D, D), D ** -0.5, 0.125, ((0, 32),)),
        "w_value": noise(seeds[6], (D, D), D ** -0.5, 0.125, ((0, 32),)),
        "w_out": noise(seeds[7], (D, D), (D // 64) ** -0.5, 1.0, ((0, 32),)),
        "gain_mlp": jnp.clip(1.0 + 0.1 * jax.random.normal(seeds[8], (D,), jnp.float32), 0.5, 1.5).astype(jnp.bfloat16),
        "w_gate": noise(seeds[9], (D, FF), D ** -0.5, 0.125, ((0, 32),)),
        "w_up": noise(seeds[10], (D, FF), D ** -0.5, 0.125, ((0, 32),)),
        "w_down": noise(seeds[11], (D, FF), FF ** -0.5, 0.0625, ((0, 32),)),
    }


EPSILON = 1e-05
ROPE_BASE = 130000.0

@jax.custom_vjp
def low(v):
    return lax.optimization_barrier(v.astype(jnp.bfloat16)).astype(jnp.float32)

@jax.custom_vjp
def low_back(v):
    return v

def low_keep(v):
    return (low(v), None)

def low_pass(kept, grad):
    return (grad,)

def back_keep(v):
    return (v, None)

def back_low(kept, grad):
    return (low(grad),)
low.defvjp(low_keep, low_pass)
low_back.defvjp(back_keep, back_low)

def doc_layout(doc_sizes, position):
    doc_ends = jnp.cumsum(doc_sizes).astype(jnp.int32)
    doc_starts = (doc_ends - doc_sizes).astype(jnp.int32)
    doc_index = lax.optimization_barrier(jnp.sum((position[:, None] >= doc_ends[None, :]).astype(jnp.int32), axis=1)).astype(jnp.int32)
    numbers = jnp.arange(doc_sizes.shape[0], dtype=jnp.int32)
    doc_match = (doc_index[:, None] == numbers[None, :]).astype(jnp.int32)
    begins = lax.optimization_barrier(jnp.sum(doc_match * doc_starts[None, :], axis=1)).astype(jnp.int32)
    return (doc_index, (position - begins).astype(jnp.int32))

def rotate(values, places, direction, head_size):
    half_size = head_size // 2
    inv_freq = ROPE_BASE ** (-2.0 * jnp.arange(half_size).astype(values.dtype) / head_size)
    angles = places.astype(values.dtype)[:, None] * inv_freq[None, :]
    cosine = jnp.cos(angles)[:, None, :]
    sine_part = direction * jnp.sin(angles)[:, None, :]
    shaped = values.reshape(values.shape[0], -1, head_size)
    lower_half = shaped[..., :half_size]
    upper_half = shaped[..., half_size:]
    turned = jnp.concatenate([lower_half * cosine - upper_half * sine_part, upper_half * cosine + lower_half * sine_part], axis=-1)
    return turned.reshape(values.shape)

def project(left_rows, right_rows):
    return jnp.dot(left_rows, right_rows, precision=lax.Precision.HIGHEST)

def project_back(left_rows, right_rows):
    return lax.dot_general(left_rows, right_rows, (((1,), (1,)), ((), ())), precision=lax.Precision.HIGHEST)

def group_attention(query_rot, key_rot, value_low, doc_index):
    token_count = query_rot.shape[0]
    block_rows = min(512, token_count)
    factor = HD ** (-0.5)
    key_heads = key_rot.reshape(token_count, H, HD)
    value_heads = value_low.reshape(token_count, H, HD)
    position = jnp.arange(token_count, dtype=jnp.int32)

    def query_block(pieces):
        query_heads, query_doc, query_place = pieces
        raw_scores = jnp.einsum('qhd,khd->hqk', query_heads, key_heads, precision=lax.Precision.HIGHEST)
        scores = low_back(raw_scores * factor)
        allowed = (query_doc[:, None] == doc_index[None, :]) & (position[None, :] <= query_place[:, None])
        scores = jnp.where(allowed[None], scores, -1e+30)
        weights = jax.nn.softmax(scores, axis=-1)
        return jnp.einsum('hqk,khd->qhd', weights, value_heads, precision=lax.Precision.HIGHEST)
    blocks = token_count // block_rows
    attended = lax.map(jax.checkpoint(query_block), (query_rot.reshape(blocks, block_rows, H, HD), doc_index.reshape(blocks, block_rows), position.reshape(blocks, block_rows)))
    return attended.reshape(token_count, H * HD)

def block_layer(tokens_f, gain_attn, w_query, w_key, w_value, w_out, gain_mlp, w_gate, w_up, w_down, doc_lengths):

    def one_group(pieces):
        group_rows, doc_sizes = pieces
        position = jnp.arange(GROUP, dtype=jnp.int32)
        doc_index, places = doc_layout(doc_sizes, position)
        inverse = lax.rsqrt(lax.optimization_barrier(jnp.mean(group_rows * group_rows, axis=-1, keepdims=True)) + EPSILON)
        normed = low(group_rows * inverse * gain_attn)
        query_proj = low_back(project(normed, w_query))
        key_proj = low_back(project(normed, w_key))
        value_proj = low_back(project(normed, w_value))
        query_rot = low(rotate(query_proj, places, 1.0, HD))
        key_rot = low(rotate(key_proj, places, 1.0, HD))
        value_low = low(value_proj)
        attended = low(low_back(group_attention(query_rot, key_rot, value_low, doc_index)))
        mixed = group_rows + low_back(project_back(attended, w_out))
        inverse_mlp = lax.rsqrt(lax.optimization_barrier(jnp.mean(mixed * mixed, axis=-1, keepdims=True)) + EPSILON)
        normed_mlp = low(mixed * inverse_mlp * gain_mlp)
        gate = low_back(project(normed_mlp, w_gate))
        up_proj = low_back(project(normed_mlp, w_up))
        hidden = low(jax.nn.silu(gate) * up_proj)
        return mixed + low_back(project_back(hidden, w_down))
    output = lax.map(jax.checkpoint(one_group), (tokens_f.reshape(N_FSDP, GROUP, D), doc_lengths))
    return output.reshape(TOKENS, D)

def reference(tokens, cotangent, doc_lengths, gain_attn, w_query, w_key, w_value, w_out, gain_mlp, w_gate, w_up, w_down):
    as_floats = [array.astype(jnp.float32) for array in (tokens, gain_attn, w_query, w_key, w_value, w_out, gain_mlp, w_gate, w_up, w_down)]

    def forward(*values):
        return block_layer(*values, doc_lengths)
    result, pull_back = jax.vjp(forward, *as_floats)
    gradients = pull_back(cotangent.astype(jnp.float32))
    return (result.astype(jnp.bfloat16), gradients[0], gradients[1], gradients[2], gradients[3], gradients[4], gradients[5], gradients[6], gradients[7], gradients[8], gradients[9])
```

```python
import functools

import jax
import jax.numpy as jnp
from jax import lax
from jax.experimental import pallas as pl
from jax.experimental.pallas import tpu as pltpu
from jax.sharding import PartitionSpec as P

H = 32
HD = 64
EPSILON = 1e-05
ROPE_BASE = 130000.0
BLOCK = 256
VMEM_LIMIT = 56 * 1024 * 1024
LOW = jnp.bfloat16
F32 = jnp.float32


def dot(left, right, left_dim, right_dim):
    return lax.dot_general(
        left, right, (((left_dim,), (right_dim,)), ((), ())), preferred_element_type=F32
    )


def flip(axis, size, bit):
    return [(i, i ^ bit) for i in range(size)]


def same_core_groups(size):
    return [[2 * i + core for i in range(size // 2)] for core in (0, 1)]


def gather_fsdp(block):
    size = lax.axis_size("fsdp")
    if size != 4:
        return lax.all_gather(block, "fsdp", axis=0, tiled=True)
    me = lax.axis_index("fsdp")
    rows = block.shape[0]
    half = rows // 2
    from_x = lax.ppermute(block, "fsdp", flip("fsdp", 4, 1))
    from_y = lax.ppermute(block, "fsdp", flip("fsdp", 4, 2))
    far_top = lax.ppermute(from_x[:half], "fsdp", flip("fsdp", 4, 2))
    far_low = lax.ppermute(from_y[half:], "fsdp", flip("fsdp", 4, 1))
    out = jnp.zeros((4 * rows, block.shape[1]), block.dtype)
    for piece, place in (
        (block, me * rows),
        (from_x, (me ^ 1) * rows),
        (from_y, (me ^ 2) * rows),
        (far_top, (me ^ 3) * rows),
        (far_low, (me ^ 3) * rows + half),
    ):
        out = lax.dynamic_update_slice_in_dim(out, piece, place, 0)
    return out


def scatter_fsdp(part):
    size = lax.axis_size("fsdp")
    if size != 4:
        return lax.psum_scatter(part, "fsdp", scatter_dimension=0, tiled=True).astype(F32)
    me = lax.axis_index("fsdp")
    rows = part.shape[0] // 4
    half = rows // 2

    def piece(bits, low):
        return lax.dynamic_slice_in_dim(part, (me ^ bits) * rows + low * half, half, 0)

    over_x = lax.ppermute(
        jnp.concatenate([piece(3, 0), piece(1, 0)]), "fsdp", flip("fsdp", 4, 1)
    )
    over_y = lax.ppermute(
        jnp.concatenate([piece(3, 1), piece(2, 1)]), "fsdp", flip("fsdp", 4, 2)
    )
    send_y = (piece(2, 0).astype(F32) + over_x[:half].astype(F32)).astype(part.dtype)
    send_x = (piece(1, 1).astype(F32) + over_y[:half].astype(F32)).astype(part.dtype)
    last_y = lax.ppermute(send_y, "fsdp", flip("fsdp", 4, 2))
    last_x = lax.ppermute(send_x, "fsdp", flip("fsdp", 4, 1))
    top = piece(0, 0).astype(F32) + over_x[half:].astype(F32) + last_y.astype(F32)
    low = piece(0, 1).astype(F32) + over_y[half:].astype(F32) + last_x.astype(F32)
    return jnp.concatenate([top, low])


def gather_ctx(block):
    size = lax.axis_size("ctx")
    pairs = size // 2
    core = lax.axis_index("ctx") % 2
    mine = lax.all_to_all(
        jnp.broadcast_to(block[None], (pairs,) + block.shape),
        "ctx",
        0,
        0,
        axis_index_groups=same_core_groups(size),
        tiled=True,
    )
    other = lax.ppermute(mine, "ctx", flip("ctx", size, 1))
    first = jnp.where(core == 0, mine, other)
    second = jnp.where(core == 0, other, mine)
    return jnp.stack([first, second], axis=1).reshape((size,) + block.shape)


def scatter_ctx(part):
    size = lax.axis_size("ctx")
    pairs = size // 2
    core = lax.axis_index("ctx") % 2
    shaped = part.reshape(pairs, 2, part.shape[0] // size, part.shape[1])
    mine = lax.dynamic_index_in_dim(shaped, core, 1, keepdims=False)
    theirs = lax.dynamic_index_in_dim(shaped, 1 - core, 1, keepdims=False)
    got = lax.ppermute(theirs, "ctx", flip("ctx", size, 1))
    pair_sum = (mine.astype(F32) + got.astype(F32)).astype(part.dtype)
    landed = lax.all_to_all(
        pair_sum, "ctx", 0, 0, axis_index_groups=same_core_groups(size), tiled=True
    )
    return jnp.sum(landed.astype(F32), axis=0)


def to_columns(rows_block):
    return lax.all_to_all(rows_block, "ctx", split_axis=1, concat_axis=0, tiled=True)


def swap_halves(values):
    width = values.shape[1]
    lane = lax.broadcasted_iota(jnp.int32, values.shape, 1)
    down = pltpu.roll(values, width - HD // 2, 1)
    up = pltpu.roll(values, HD // 2, 1)
    return jnp.where(lane % HD < HD // 2, down, up)


def project_kernel(width, x_ref, w_ref, cos_ref, sin_ref, unit_ref, out_ref):
    x = x_ref[...].astype(F32)
    inverse = lax.rsqrt(jnp.mean(x * x, axis=-1, keepdims=True) + EPSILON)
    unit = (x * inverse).astype(LOW)
    unit_ref[...] = unit
    cos, sin = cos_ref[...], sin_ref[...]
    for part in range(3):
        columns = slice(part * width, (part + 1) * width)
        value = dot(unit, w_ref[:, columns], 1, 0)
        if part < 2:
            value = value * cos + swap_halves(value) * sin
        out_ref[:, columns] = value.astype(LOW)


def project(x_all, w_qkv, cos, sin):
    count, features = x_all.shape
    width = w_qkv.shape[1] // 3
    return pl.pallas_call(
        functools.partial(project_kernel, width),
        grid=(count // BLOCK,),
        in_specs=[
            pl.BlockSpec((BLOCK, features), lambda i: (i, 0)),
            pl.BlockSpec((features, 3 * width), lambda i: (0, 0)),
            pl.BlockSpec((BLOCK, width), lambda i: (i, 0)),
            pl.BlockSpec((BLOCK, width), lambda i: (i, 0)),
        ],
        out_specs=[
            pl.BlockSpec((BLOCK, features), lambda i: (i, 0)),
            pl.BlockSpec((BLOCK, 3 * width), lambda i: (i, 0)),
        ],
        out_shape=[
            jax.ShapeDtypeStruct((count, features), LOW),
            jax.ShapeDtypeStruct((count, 3 * width), LOW),
        ],
        compiler_params=pltpu.CompilerParams(vmem_limit_bytes=VMEM_LIMIT),
        name="project",
    )(x_all, w_qkv, cos, sin)


def masked_scores(key, query, key_block, query_block, starts):
    scores = dot(key, query, 1, 1) * (HD**-0.5)
    at_key = key_block * BLOCK + lax.broadcasted_iota(jnp.int32, scores.shape, 0)
    at_query = query_block * BLOCK + lax.broadcasted_iota(jnp.int32, scores.shape, 1)
    return jnp.where((at_key <= at_query) & (at_key >= starts), scores, -1e30)


def attend_kernel(heads, lo_ref, start_ref, q_ref, k_ref, v_ref, out_ref, score_ref):
    block = pl.program_id(0)
    starts = start_ref[...]
    lanes = [slice(h * HD, (h + 1) * HD) for h in range(heads)]
    queries = [q_ref[:, lane] for lane in lanes]

    def score(key_block, tops):
        rows = pl.ds(pl.multiple_of(key_block * BLOCK, BLOCK), BLOCK)
        fresh = []
        for h in range(heads):
            s = masked_scores(k_ref[rows, lanes[h]], queries[h], key_block, block, starts)
            score_ref[h, rows, :] = s
            fresh.append(jnp.maximum(tops[h], jnp.max(s, axis=0, keepdims=True)))
        return tuple(fresh)

    lo = lo_ref[block]
    tops = lax.fori_loop(lo, block + 1, score, (jnp.full((1, BLOCK), -1e30, F32),) * heads)

    def weigh(key_block, carried):
        sums, totals = carried
        rows = pl.ds(pl.multiple_of(key_block * BLOCK, BLOCK), BLOCK)
        new_sums, new_totals = [], []
        for h in range(heads):
            p = jnp.exp(score_ref[h, rows, :] - tops[h])
            new_sums.append(sums[h] + jnp.sum(p, axis=0, keepdims=True))
            new_totals.append(totals[h] + dot(v_ref[rows, lanes[h]], p.astype(LOW), 0, 0))
        return tuple(new_sums), tuple(new_totals)

    sums, totals = lax.fori_loop(
        lo,
        block + 1,
        weigh,
        ((jnp.zeros((1, BLOCK), F32),) * heads, (jnp.zeros((HD, BLOCK), F32),) * heads),
    )
    turned = jnp.concatenate([totals[h] / sums[h] for h in range(heads)], axis=0)
    out_ref[...] = turned.T.astype(LOW)


def attend(lows, starts, qkv):
    count = qkv.shape[0]
    width = qkv.shape[1] // 3
    heads = width // HD
    return pl.pallas_call(
        functools.partial(attend_kernel, heads),
        grid_spec=pltpu.PrefetchScalarGridSpec(
            num_scalar_prefetch=1,
            grid=(count // BLOCK,),
            in_specs=[
                pl.BlockSpec((1, BLOCK), lambda i, lo: (0, i)),
                pl.BlockSpec((BLOCK, width), lambda i, lo: (i, 0)),
                pl.BlockSpec((count, width), lambda i, lo: (0, 1)),
                pl.BlockSpec((count, width), lambda i, lo: (0, 2)),
            ],
            out_specs=pl.BlockSpec((BLOCK, width), lambda i, lo: (i, 0)),
            scratch_shapes=[pltpu.VMEM((heads, count, BLOCK), F32)],
        ),
        out_shape=jax.ShapeDtypeStruct((count, width), LOW),
        compiler_params=pltpu.CompilerParams(vmem_limit_bytes=VMEM_LIMIT),
        name="attend",
    )(lows, starts, qkv, qkv, qkv)


def attend_back_kernel(
    heads,
    lo_ref,
    start_ref,
    q_ref,
    k_ref,
    v_ref,
    back_ref,
    cos_ref,
    sin_ref,
    out_ref,
    weight_ref,
    slope_ref,
    dk_ref,
    dv_ref,
):
    block = pl.program_id(0)
    width = heads * HD
    starts = start_ref[...]
    lanes = [slice(h * HD, (h + 1) * HD) for h in range(heads)]
    queries = [q_ref[:, lane] for lane in lanes]
    backs = [back_ref[:, lane] for lane in lanes]

    @pl.when(block == 0)
    def _():
        dk_ref[...] = jnp.zeros_like(dk_ref)
        dv_ref[...] = jnp.zeros_like(dv_ref)

    def score(key_block, tops):
        rows = pl.ds(pl.multiple_of(key_block * BLOCK, BLOCK), BLOCK)
        fresh = []
        for h in range(heads):
            s = masked_scores(k_ref[rows, lanes[h]], queries[h], key_block, block, starts)
            weight_ref[h, rows, :] = s
            slope_ref[h, rows, :] = dot(v_ref[rows, lanes[h]], backs[h], 1, 1)
            fresh.append(jnp.maximum(tops[h], jnp.max(s, axis=0, keepdims=True)))
        return tuple(fresh)

    lo = lo_ref[block]
    tops = lax.fori_loop(lo, block + 1, score, (jnp.full((1, BLOCK), -1e30, F32),) * heads)

    def weigh(key_block, carried):
        sums, deltas = carried
        rows = pl.ds(pl.multiple_of(key_block * BLOCK, BLOCK), BLOCK)
        new_sums, new_deltas = [], []
        for h in range(heads):
            p = jnp.exp(weight_ref[h, rows, :] - tops[h])
            weight_ref[h, rows, :] = p
            new_sums.append(sums[h] + jnp.sum(p, axis=0, keepdims=True))
            new_deltas.append(
                deltas[h] + jnp.sum(p * slope_ref[h, rows, :], axis=0, keepdims=True)
            )
        return tuple(new_sums), tuple(new_deltas)

    zero_row = (jnp.zeros((1, BLOCK), F32),) * heads
    sums, deltas = lax.fori_loop(lo, block + 1, weigh, (zero_row, zero_row))
    inverses = [1.0 / sums[h] for h in range(heads)]
    deltas = [deltas[h] * inverses[h] for h in range(heads)]

    def spread(key_block, totals):
        rows = pl.ds(pl.multiple_of(key_block * BLOCK, BLOCK), BLOCK)
        fresh, dks, dvs = [], [], []
        for h in range(heads):
            p = weight_ref[h, rows, :] * inverses[h]
            ds = (p * (slope_ref[h, rows, :] - deltas[h])).astype(LOW)
            dvs.append(dot(p.astype(LOW), backs[h], 1, 0))
            dks.append(dot(ds, queries[h], 1, 0))
            fresh.append(totals[h] + dot(k_ref[rows, lanes[h]], ds, 0, 0))
        dk_ref[rows, :] += jnp.concatenate(dks, axis=1)
        dv_ref[rows, :] += jnp.concatenate(dvs, axis=1)
        return tuple(fresh)

    totals = lax.fori_loop(lo, block + 1, spread, (jnp.zeros((HD, BLOCK), F32),) * heads)
    here = pl.ds(pl.multiple_of(block * BLOCK, BLOCK), BLOCK)
    dq = jnp.concatenate(totals, axis=0).T * (HD**-0.5)
    dq = dq * cos_ref[here, :] - swap_halves(dq) * sin_ref[here, :]
    out_ref[here, 0:width] = dq.astype(LOW)

    @pl.when(block == pl.num_programs(0) - 1)
    def _():
        def finish(index, carried):
            rows = pl.ds(pl.multiple_of(index * BLOCK, BLOCK), BLOCK)
            dk = dk_ref[rows, :] * (HD**-0.5)
            dk = dk * cos_ref[rows, :] - swap_halves(dk) * sin_ref[rows, :]
            out_ref[rows, width : 2 * width] = dk.astype(LOW)
            out_ref[rows, 2 * width : 3 * width] = dv_ref[rows, :].astype(LOW)
            return carried

        lax.fori_loop(0, dk_ref.shape[0] // BLOCK, finish, 0)


def attend_back(lows, starts, qkv, back, cos, sin):
    count = qkv.shape[0]
    width = qkv.shape[1] // 3
    heads = width // HD
    return pl.pallas_call(
        functools.partial(attend_back_kernel, heads),
        grid_spec=pltpu.PrefetchScalarGridSpec(
            num_scalar_prefetch=1,
            grid=(count // BLOCK,),
            in_specs=[
                pl.BlockSpec((1, BLOCK), lambda i, lo: (0, i)),
                pl.BlockSpec((BLOCK, width), lambda i, lo: (i, 0)),
                pl.BlockSpec((count, width), lambda i, lo: (0, 1)),
                pl.BlockSpec((count, width), lambda i, lo: (0, 2)),
                pl.BlockSpec((BLOCK, width), lambda i, lo: (i, 0)),
                pl.BlockSpec((count, width), lambda i, lo: (0, 0)),
                pl.BlockSpec((count, width), lambda i, lo: (0, 0)),
            ],
            out_specs=pl.BlockSpec((count, 3 * width), lambda i, lo: (0, 0)),
            scratch_shapes=[
                pltpu.VMEM((heads, count, BLOCK), F32),
                pltpu.VMEM((heads, count, BLOCK), F32),
                pltpu.VMEM((count, width), F32),
                pltpu.VMEM((count, width), F32),
            ],
        ),
        out_shape=jax.ShapeDtypeStruct((count, 3 * width), LOW),
        compiler_params=pltpu.CompilerParams(vmem_limit_bytes=VMEM_LIMIT),
        name="attend_back",
    )(lows, starts, qkv, qkv, qkv, back, cos, sin)


def local(
    tokens,
    cotangent,
    doc_lengths,
    gain_attn,
    w_query,
    w_key,
    w_value,
    w_out,
    gain_mlp,
    w_gate,
    w_up,
    w_down,
):
    rows, features = tokens.shape
    n_c = lax.axis_size("ctx")
    group = rows * n_c
    width = features // n_c
    here = lax.axis_index("ctx") * rows
    share = w_query.shape[0]

    gain_a = gain_attn.astype(F32)[:, None]
    gain_m = gain_mlp.astype(F32)[:, None]

    def scaled(weight, gain):
        return (weight.astype(F32) * gain).astype(LOW)

    x_all = lax.all_gather(tokens, "ctx", axis=0, tiled=True)
    out_all = lax.all_gather(w_out, ("fsdp", "ctx"), axis=0, tiled=True)
    back_all = lax.all_gather(cotangent, "ctx", axis=0, tiled=True)

    stacked = jnp.concatenate(
        [
            scaled(w, gain_a).reshape(share, n_c, width)
            for w in (w_query, w_key, w_value)
        ],
        axis=2,
    ).reshape(share, 3 * features)
    w_qkv = gather_fsdp(to_columns(stacked))
    col_gate = gather_fsdp(to_columns(scaled(w_gate, gain_m)))
    col_up = gather_fsdp(to_columns(scaled(w_up, gain_m)))
    col_down = gather_fsdp(to_columns(w_down))

    position = jnp.arange(group, dtype=jnp.int32)
    doc_ends = jnp.cumsum(doc_lengths[0])
    doc_starts = doc_ends - doc_lengths[0]
    starts = jnp.max(
        jnp.where(position[:, None] >= doc_starts[None, :], doc_starts[None, :], 0), axis=1
    ).astype(jnp.int32)
    places = (position - starts).astype(F32)
    half = HD // 2
    lane = jnp.arange(128, dtype=jnp.int32)
    inv_freq = ROPE_BASE ** (-2.0 * (lane % half).astype(F32) / HD)
    angles = places[:, None] * inv_freq[None, :]
    sign = jnp.where(lane % HD < half, -1.0, 1.0).astype(F32)
    cos = jnp.tile(jnp.cos(angles), (1, width // 128))
    sin = jnp.tile(jnp.sin(angles) * sign[None, :], (1, width // 128))
    lows = starts[::BLOCK] // BLOCK
    starts_row = starts[None, :]

    unit, qkv = project(x_all, w_qkv, cos, sin)
    attended = attend(lows, starts_row, qkv)
    attended_all = (
        jnp.swapaxes(gather_ctx(attended), 0, 1).reshape(group, features)
    )
    mixed = x_all.astype(F32) + dot(attended_all, out_all, 1, 1)
    inverse_mlp = lax.rsqrt(jnp.mean(mixed * mixed, axis=-1, keepdims=True) + EPSILON)
    unit_mlp = (mixed * inverse_mlp).astype(LOW)

    gate = dot(unit_mlp, col_gate, 1, 0)
    up = dot(unit_mlp, col_up, 1, 0)
    sigmoid = jax.nn.sigmoid(gate)
    silu = gate * sigmoid
    hidden = (silu * up).astype(LOW)
    d_hidden = dot(back_all, col_down, 1, 0)
    d_gate = (d_hidden * up * sigmoid * (1.0 + gate * (1.0 - sigmoid))).astype(LOW)
    d_up = (d_hidden * silu).astype(LOW)
    branch = dot(hidden, col_down, 1, 1).astype(LOW)
    d_unit_part = (dot(d_gate, col_gate, 1, 1) + dot(d_up, col_up, 1, 1)).astype(LOW)
    d_unit = scatter_ctx(d_unit_part)
    branch_own = lax.psum_scatter(branch, "ctx", scatter_dimension=0, tiled=True).astype(F32)
    mixed_own = lax.dynamic_slice_in_dim(mixed, here, rows, 0)
    layer_out = (mixed_own + branch_own).astype(LOW)

    inverse_own = lax.dynamic_slice_in_dim(inverse_mlp, here, rows, 0)
    unit_own = mixed_own * inverse_own
    d_mixed = cotangent.astype(F32) + inverse_own * (
        d_unit - unit_own * jnp.mean(d_unit * unit_own, axis=-1, keepdims=True)
    )
    d_mixed_low = d_mixed.astype(LOW)
    d_att = dot(d_mixed_low, out_all, 1, 0).astype(LOW)
    d_att_own = lax.all_to_all(d_att, "ctx", split_axis=1, concat_axis=0, tiled=True)
    d_qkv = attend_back(lows, starts_row, qkv, d_att_own, cos, sin)

    d_first = scatter_ctx(dot(d_qkv, w_qkv, 1, 1).astype(LOW))
    x_own = tokens.astype(F32)
    inverse = lax.rsqrt(jnp.mean(x_own * x_own, axis=-1, keepdims=True) + EPSILON)
    first_own = x_own * inverse
    grad_tokens = d_mixed + inverse * (
        d_first - first_own * jnp.mean(d_first * first_own, axis=-1, keepdims=True)
    )

    def weight_grad(left, right):
        part = dot(left, right, 0, 0).astype(LOW)
        mine = scatter_fsdp(part).astype(LOW)
        return lax.all_to_all(mine, "ctx", split_axis=0, concat_axis=1, tiled=True).astype(F32)

    raw_gate = weight_grad(unit_mlp, d_gate)
    raw_up = weight_grad(unit_mlp, d_up)
    grad_down = weight_grad(back_all, hidden)
    attended_own = lax.dynamic_slice_in_dim(attended_all, here, rows, 0)
    grad_out = lax.psum_scatter(
        dot(d_mixed_low, attended_own, 0, 0).astype(LOW),
        ("fsdp", "ctx"),
        scatter_dimension=0,
        tiled=True,
    ).astype(F32)
    raw_qkv = weight_grad(unit, d_qkv).reshape(share, n_c, 3, width)
    raw_query, raw_key, raw_value = (
        raw_qkv[:, :, part].reshape(share, features) for part in range(3)
    )
    grad_gain_attn = jnp.sum(
        raw_query * w_query.astype(F32)
        + raw_key * w_key.astype(F32)
        + raw_value * w_value.astype(F32),
        axis=1,
    )
    grad_gain_mlp = jnp.sum(
        raw_gate * w_gate.astype(F32) + raw_up * w_up.astype(F32), axis=1
    )
    return (
        layer_out,
        grad_tokens,
        grad_gain_attn,
        raw_query * gain_a,
        raw_key * gain_a,
        raw_value * gain_a,
        grad_out,
        grad_gain_mlp,
        raw_gate * gain_m,
        raw_up * gain_m,
        grad_down,
    )


def solution(mesh):
    split = P(("fsdp", "ctx"))
    rows = P(("fsdp", "ctx"), None)
    in_specs = (rows, rows, P("fsdp", None), split, rows, rows, rows, rows, split, rows, rows, rows)
    out_specs = (rows, rows, split, rows, rows, rows, rows, split, rows, rows, rows)
    return jax.shard_map(local, mesh=mesh, in_specs=in_specs, out_specs=out_specs, check_vma=False)
```

```python
import functools

import jax
import jax.numpy as jnp
from jax import lax
from jax.experimental import pallas as pl
from jax.experimental.pallas import tpu as pltpu
from jax.sharding import PartitionSpec as P

H = 32
HD = 64
EPSILON = 1e-05
ROPE_BASE = 130000.0
BLOCK = 256
UNIT = 256
VMEM_LIMIT = 56 * 1024 * 1024
GIGA = 1000 * 1000 * 1000
LOW = jnp.bfloat16
F32 = jnp.float32


def dot(left, right, left_dim, right_dim):
    return lax.dot_general(
        left, right, (((left_dim,), (right_dim,)), ((), ())), preferred_element_type=F32
    )


def flip(axis, size, bit):
    return [(i, i ^ bit) for i in range(size)]


def same_core_groups(size):
    return [[2 * i + core for i in range(size // 2)] for core in (0, 1)]


def after(value, *others):
    return lax.optimization_barrier((value,) + others)[0]


def near(block):
    return (
        lax.ppermute(block, "fsdp", flip("fsdp", 4, 1)),
        lax.ppermute(block, "fsdp", flip("fsdp", 4, 2)),
    )


def far(pieces):
    from_x, from_y = pieces
    half = from_x.shape[0] // 2
    return (
        lax.ppermute(from_x[:half], "fsdp", flip("fsdp", 4, 2)),
        lax.ppermute(from_y[half:], "fsdp", flip("fsdp", 4, 1)),
    )


def reduce_near(part):
    return (
        lax.ppermute(part[0], "fsdp", flip("fsdp", 4, 1)),
        lax.ppermute(part[1], "fsdp", flip("fsdp", 4, 2)),
    )


def reduce_far(part, landed):
    over_x, over_y = landed
    unit = over_x.shape[0] // 2
    send_y = (part[2][:unit].astype(F32) + over_x[:unit].astype(F32)).astype(LOW)
    send_x = (part[2][unit : 2 * unit].astype(F32) + over_y[:unit].astype(F32)).astype(LOW)
    return (
        lax.ppermute(send_y, "fsdp", flip("fsdp", 4, 2)),
        lax.ppermute(send_x, "fsdp", flip("fsdp", 4, 1)),
    )


def reduce_own(part, landed, last):
    over_x, over_y = landed
    unit = over_x.shape[0] // 2
    top = part[2][2 * unit : 3 * unit].astype(F32) + over_x[unit:].astype(F32)
    low = part[2][3 * unit :].astype(F32) + over_y[unit:].astype(F32)
    return jnp.concatenate([top + last[0].astype(F32), low + last[1].astype(F32)])


def spread_cores(block):
    size = lax.axis_size("ctx")
    pairs = size // 2
    return lax.all_to_all(
        jnp.broadcast_to(block[None], (pairs,) + block.shape),
        "ctx",
        0,
        0,
        axis_index_groups=same_core_groups(size),
        tiled=True,
    )


def other_core(value):
    return lax.ppermute(value, "ctx", flip("ctx", lax.axis_size("ctx"), 1))


def pair_sums(part):
    size = lax.axis_size("ctx")
    core = lax.axis_index("ctx") % 2
    shaped = part.reshape(size // 2, 2, part.shape[0] // size, part.shape[1])
    mine = lax.dynamic_index_in_dim(shaped, core, 1, keepdims=False)
    theirs = lax.dynamic_index_in_dim(shaped, 1 - core, 1, keepdims=False)
    got = other_core(theirs)
    return (mine.astype(F32) + got.astype(F32)).astype(part.dtype)


def swap_chips(sums):
    return lax.all_to_all(
        sums,
        "ctx",
        0,
        0,
        axis_index_groups=same_core_groups(lax.axis_size("ctx")),
        tiled=True,
    )


def total(landed):
    return jnp.sum(landed.astype(F32), axis=0)


def to_columns(rows_block):
    return lax.all_to_all(rows_block, "ctx", split_axis=1, concat_axis=0, tiled=True)


def swap_halves(values):
    width = values.shape[1]
    lane = lax.broadcasted_iota(jnp.int32, values.shape, 1)
    down = pltpu.roll(values, width - HD // 2, 1)
    up = pltpu.roll(values, HD // 2, 1)
    return jnp.where(lane % HD < HD // 2, down, up)


def units_of(pieces):
    return [
        (index, unit)
        for index, piece in enumerate(pieces)
        for unit in range(piece.shape[0] // UNIT)
    ]


def gather_units(places_ref, pieces, out_ref):
    for step, (index, unit) in enumerate(units_of(pieces)):
        rows = pl.ds(pl.multiple_of(places_ref[step] * UNIT, UNIT), UNIT)
        out_ref[rows, :] = pieces[index][unit * UNIT : (unit + 1) * UNIT, :]


def project_kernel(count, places_ref, x_ref, cos_ref, sin_ref, *refs):
    pieces = refs[:count]
    unit_ref, out_ref, w_ref = refs[count:]
    width = out_ref.shape[1] // 3

    @pl.when(pl.program_id(0) == 0)
    def _():
        gather_units(places_ref, pieces, w_ref)

    x = x_ref[...].astype(F32)
    inverse = lax.rsqrt(jnp.mean(x * x, axis=-1, keepdims=True) + EPSILON)
    unit = (x * inverse).astype(LOW)
    unit_ref[...] = unit
    cos, sin = cos_ref[...], sin_ref[...]
    for part in range(3):
        columns = slice(part * width, (part + 1) * width)
        value = dot(unit, w_ref[:, columns], 1, 0)
        if part < 2:
            value = value * cos + swap_halves(value) * sin
        out_ref[:, columns] = value.astype(LOW)


def project(places, x_all, pieces, cos, sin):
    count, features = x_all.shape
    wide = pieces[0].shape[1]
    width = wide // 3
    return pl.pallas_call(
        functools.partial(project_kernel, len(pieces)),
        grid_spec=pltpu.PrefetchScalarGridSpec(
            num_scalar_prefetch=1,
            grid=(count // BLOCK,),
            in_specs=[
                pl.BlockSpec((BLOCK, features), lambda i, p: (i, 0)),
                pl.BlockSpec((BLOCK, width), lambda i, p: (i, 0)),
                pl.BlockSpec((BLOCK, width), lambda i, p: (i, 0)),
            ]
            + [pl.BlockSpec(piece.shape, lambda i, p: (0, 0)) for piece in pieces],
            out_specs=[
                pl.BlockSpec((BLOCK, features), lambda i, p: (i, 0)),
                pl.BlockSpec((BLOCK, wide), lambda i, p: (i, 0)),
            ],
            scratch_shapes=[pltpu.VMEM((features, wide), LOW)],
        ),
        out_shape=[
            jax.ShapeDtypeStruct((count, features), LOW),
            jax.ShapeDtypeStruct((count, wide), LOW),
        ],
        compiler_params=pltpu.CompilerParams(vmem_limit_bytes=VMEM_LIMIT),
        cost_estimate=pl.CostEstimate(flops=9 * GIGA, bytes_accessed=0, transcendentals=0),
        name="project",
    )(places, x_all, cos, sin, *pieces)


def open_kernel(count, places_ref, left_ref, *refs):
    gate_pieces, up_pieces = refs[:count], refs[count : 2 * count]
    gate_ref, up_ref, hidden_ref, w_gate_ref, w_up_ref = refs[2 * count :]
    gather_units(places_ref, gate_pieces, w_gate_ref)
    gather_units(places_ref, up_pieces, w_up_ref)
    left = left_ref[...]
    gate = dot(left, w_gate_ref[...], 1, 0)
    gate_ref[...] = gate
    up = dot(left, w_up_ref[...], 1, 0)
    up_ref[...] = up
    hidden_ref[...] = (gate * jax.nn.sigmoid(gate) * up).astype(LOW)


def open_units(places, left, pieces):
    count, features = left.shape
    hidden = pieces[0].shape[1] // 2
    blocks = hidden // UNIT
    column = pl.BlockSpec((count, UNIT), lambda j, p: (0, j))
    return pl.pallas_call(
        functools.partial(open_kernel, len(pieces)),
        grid_spec=pltpu.PrefetchScalarGridSpec(
            num_scalar_prefetch=1,
            grid=(blocks,),
            in_specs=[pl.BlockSpec((count, features), lambda j, p: (0, 0))]
            + [pl.BlockSpec((w.shape[0], UNIT), lambda j, p: (0, j)) for w in pieces]
            + [pl.BlockSpec((w.shape[0], UNIT), lambda j, p: (0, j + blocks)) for w in pieces],
            out_specs=[column] * 3,
            scratch_shapes=[pltpu.VMEM((features, UNIT), LOW)] * 2,
        ),
        out_shape=[
            jax.ShapeDtypeStruct((count, hidden), F32),
            jax.ShapeDtypeStruct((count, hidden), F32),
            jax.ShapeDtypeStruct((count, hidden), LOW),
        ],
        compiler_params=pltpu.CompilerParams(vmem_limit_bytes=VMEM_LIMIT),
        cost_estimate=pl.CostEstimate(flops=12 * GIGA, bytes_accessed=0, transcendentals=0),
        name="open_units",
    )(places, left, *pieces, *pieces)


def close_kernel(count, places_ref, back_ref, gate_ref, up_ref, *refs):
    pieces = refs[:count]
    out_ref, w_ref = refs[count:]
    gather_units(places_ref, pieces, w_ref)
    d_hidden = dot(back_ref[...], w_ref[...], 1, 0)
    gate = gate_ref[...]
    sigmoid = jax.nn.sigmoid(gate)
    scaled = d_hidden * sigmoid
    out_ref[0] = (scaled * up_ref[...] * (1.0 + gate * (1.0 - sigmoid))).astype(LOW)
    out_ref[1] = (scaled * gate).astype(LOW)


def close_units(places, back, gate, up, pieces):
    count, features = back.shape
    hidden = gate.shape[1]
    column = pl.BlockSpec((count, UNIT), lambda j, p: (0, j))
    return pl.pallas_call(
        functools.partial(close_kernel, len(pieces)),
        grid_spec=pltpu.PrefetchScalarGridSpec(
            num_scalar_prefetch=1,
            grid=(hidden // UNIT,),
            in_specs=[pl.BlockSpec((count, features), lambda j, p: (0, 0)), column, column]
            + [pl.BlockSpec((w.shape[0], UNIT), lambda j, p: (0, j)) for w in pieces],
            out_specs=pl.BlockSpec((2, count, UNIT), lambda j, p: (0, 0, j)),
            scratch_shapes=[pltpu.VMEM((features, UNIT), LOW)],
        ),
        out_shape=jax.ShapeDtypeStruct((2, count, hidden), LOW),
        compiler_params=pltpu.CompilerParams(vmem_limit_bytes=VMEM_LIMIT),
        cost_estimate=pl.CostEstimate(flops=7 * GIGA, bytes_accessed=0, transcendentals=0),
        name="close_units",
    )(places, back, gate, up, *pieces)


def times_rows_kernel(pieces, places_ref, left_ref, *refs):
    out_ref, w_ref = refs[len(pieces) :]
    step = pl.program_id(0)
    first = 0
    for ref, units in zip(refs, pieces):

        @pl.when((step >= first) & (step < first + units))
        def _():
            w_ref[...] = ref[...]

        first += units
    parts, unused, width = left_ref.shape
    total_ = dot(left_ref[0], w_ref[:, :width], 1, 1)
    for part in range(1, parts):
        total_ += dot(left_ref[part], w_ref[:, part * width : (part + 1) * width], 1, 1)
    out_ref[...] = total_.astype(LOW)


def times_rows(places, left, pieces):
    parts, count, width = left.shape
    units = [piece.shape[0] // UNIT for piece in pieces]
    firsts = [sum(units[:index]) for index in range(len(units))]

    def spec(first, held):
        return pl.BlockSpec(
            (UNIT, parts * width), lambda s, p: (jnp.clip(s - first, 0, held - 1), 0)
        )

    return pl.pallas_call(
        functools.partial(times_rows_kernel, units),
        grid_spec=pltpu.PrefetchScalarGridSpec(
            num_scalar_prefetch=1,
            grid=(sum(units),),
            in_specs=[pl.BlockSpec(left.shape, lambda s, p: (0, 0, 0))]
            + [spec(first, held) for first, held in zip(firsts, units)],
            out_specs=pl.BlockSpec((count, UNIT), lambda s, p: (0, p[s])),
            scratch_shapes=[pltpu.VMEM((UNIT, parts * width), LOW)],
        ),
        out_shape=jax.ShapeDtypeStruct((count, sum(units) * UNIT), LOW),
        compiler_params=pltpu.CompilerParams(vmem_limit_bytes=VMEM_LIMIT),
        cost_estimate=pl.CostEstimate(
            flops=2 * parts * count * width * sum(units) * UNIT, bytes_accessed=0, transcendentals=0
        ),
        name="times_rows",
    )(places, left, *pieces)


def weight_grad_kernel(outs, pairs, order_ref, *refs):
    step = pl.program_id(0)
    values = []
    for left_ref, right_ref in zip(refs[:pairs], refs[pairs : 2 * pairs]):
        left = left_ref[...]
        for part in range(right_ref.shape[0]):
            values.append(dot(left, right_ref[part], 0, 0).astype(LOW))
    value = values[0] if len(values) == 1 else jnp.concatenate(values, axis=1)
    first = 0
    for ref, units in zip(refs[2 * pairs :], outs):

        @pl.when((step >= first) & (step < first + units))
        def _():
            ref[...] = value

        first += units


def weight_grad(order, outs, *pairs):
    lefts = [left for left, unused in pairs]
    rights = [right for unused, right in pairs]
    count, features = lefts[0].shape
    wide = sum(right.shape[0] * right.shape[2] for right in rights)
    firsts = [sum(outs[:index]) for index in range(len(outs))]

    def spec(first, held):
        return pl.BlockSpec((UNIT, wide), lambda s, p: (jnp.clip(s - first, 0, held - 1), 0))

    return pl.pallas_call(
        functools.partial(weight_grad_kernel, outs, len(pairs)),
        grid_spec=pltpu.PrefetchScalarGridSpec(
            num_scalar_prefetch=1,
            grid=(features // UNIT,),
            in_specs=[pl.BlockSpec((count, UNIT), lambda s, p: (0, p[s]))] * len(pairs)
            + [pl.BlockSpec(right.shape, lambda s, p: (0, 0, 0)) for right in rights],
            out_specs=[spec(first, held) for first, held in zip(firsts, outs)],
        ),
        out_shape=[jax.ShapeDtypeStruct((held * UNIT, wide), LOW) for held in outs],
        compiler_params=pltpu.CompilerParams(vmem_limit_bytes=VMEM_LIMIT),
        cost_estimate=pl.CostEstimate(
            flops=2 * count * wide * features, bytes_accessed=0, transcendentals=0
        ),
        name="weight_grad",
    )(order, *lefts, *rights)


def masked_scores(key, query, key_block, query_block, starts):
    scores = dot(key, query, 1, 1) * (HD**-0.5)
    at_key = key_block * BLOCK + lax.broadcasted_iota(jnp.int32, scores.shape, 0)
    at_query = query_block * BLOCK + lax.broadcasted_iota(jnp.int32, scores.shape, 1)
    return jnp.where((at_key <= at_query) & (at_key >= starts), scores, -1e30)


def attend_kernel(heads, lo_ref, start_ref, q_ref, k_ref, v_ref, out_ref, score_ref):
    block = pl.program_id(0)
    starts = start_ref[...]
    lanes = [slice(h * HD, (h + 1) * HD) for h in range(heads)]
    queries = [q_ref[:, lane] for lane in lanes]

    def score(key_block, tops):
        rows = pl.ds(pl.multiple_of(key_block * BLOCK, BLOCK), BLOCK)
        fresh = []
        for h in range(heads):
            s = masked_scores(k_ref[rows, lanes[h]], queries[h], key_block, block, starts)
            score_ref[h, rows, :] = s
            fresh.append(jnp.maximum(tops[h], jnp.max(s, axis=0, keepdims=True)))
        return tuple(fresh)

    lo = lo_ref[block]
    tops = lax.fori_loop(lo, block + 1, score, (jnp.full((1, BLOCK), -1e30, F32),) * heads)

    def weigh(key_block, carried):
        sums, totals = carried
        rows = pl.ds(pl.multiple_of(key_block * BLOCK, BLOCK), BLOCK)
        new_sums, new_totals = [], []
        for h in range(heads):
            p = jnp.exp(score_ref[h, rows, :] - tops[h])
            new_sums.append(sums[h] + jnp.sum(p, axis=0, keepdims=True))
            new_totals.append(totals[h] + dot(v_ref[rows, lanes[h]], p.astype(LOW), 0, 0))
        return tuple(new_sums), tuple(new_totals)

    sums, totals = lax.fori_loop(
        lo,
        block + 1,
        weigh,
        ((jnp.zeros((1, BLOCK), F32),) * heads, (jnp.zeros((HD, BLOCK), F32),) * heads),
    )
    turned = jnp.concatenate([totals[h] / sums[h] for h in range(heads)], axis=0)
    out_ref[...] = turned.T.astype(LOW)


def attend(lows, starts, qkv):
    count = qkv.shape[0]
    width = qkv.shape[1] // 3
    heads = width // HD
    return pl.pallas_call(
        functools.partial(attend_kernel, heads),
        grid_spec=pltpu.PrefetchScalarGridSpec(
            num_scalar_prefetch=1,
            grid=(count // BLOCK,),
            in_specs=[
                pl.BlockSpec((1, BLOCK), lambda i, lo: (0, i)),
                pl.BlockSpec((BLOCK, width), lambda i, lo: (i, 0)),
                pl.BlockSpec((count, width), lambda i, lo: (0, 1)),
                pl.BlockSpec((count, width), lambda i, lo: (0, 2)),
            ],
            out_specs=pl.BlockSpec((BLOCK, width), lambda i, lo: (i, 0)),
            scratch_shapes=[pltpu.VMEM((heads, count, BLOCK), F32)],
        ),
        out_shape=jax.ShapeDtypeStruct((count, width), LOW),
        compiler_params=pltpu.CompilerParams(vmem_limit_bytes=VMEM_LIMIT),
        cost_estimate=pl.CostEstimate(flops=10 * GIGA, bytes_accessed=0, transcendentals=0),
        name="attend",
    )(lows, starts, qkv, qkv, qkv)


def attend_back_kernel(
    heads,
    lo_ref,
    start_ref,
    q_ref,
    k_ref,
    v_ref,
    back_ref,
    cos_ref,
    sin_ref,
    out_ref,
    weight_ref,
    slope_ref,
    dk_ref,
    dv_ref,
):
    block = pl.program_id(0)
    width = heads * HD
    starts = start_ref[...]
    lanes = [slice(h * HD, (h + 1) * HD) for h in range(heads)]
    queries = [q_ref[:, lane] for lane in lanes]
    backs = [back_ref[:, lane] for lane in lanes]

    @pl.when(block == 0)
    def _():
        dk_ref[...] = jnp.zeros_like(dk_ref)
        dv_ref[...] = jnp.zeros_like(dv_ref)

    def score(key_block, tops):
        rows = pl.ds(pl.multiple_of(key_block * BLOCK, BLOCK), BLOCK)
        fresh = []
        for h in range(heads):
            s = masked_scores(k_ref[rows, lanes[h]], queries[h], key_block, block, starts)
            weight_ref[h, rows, :] = s
            slope_ref[h, rows, :] = dot(v_ref[rows, lanes[h]], backs[h], 1, 1)
            fresh.append(jnp.maximum(tops[h], jnp.max(s, axis=0, keepdims=True)))
        return tuple(fresh)

    lo = lo_ref[block]
    tops = lax.fori_loop(lo, block + 1, score, (jnp.full((1, BLOCK), -1e30, F32),) * heads)

    def weigh(key_block, carried):
        sums, deltas = carried
        rows = pl.ds(pl.multiple_of(key_block * BLOCK, BLOCK), BLOCK)
        new_sums, new_deltas = [], []
        for h in range(heads):
            p = jnp.exp(weight_ref[h, rows, :] - tops[h])
            weight_ref[h, rows, :] = p
            new_sums.append(sums[h] + jnp.sum(p, axis=0, keepdims=True))
            new_deltas.append(
                deltas[h] + jnp.sum(p * slope_ref[h, rows, :], axis=0, keepdims=True)
            )
        return tuple(new_sums), tuple(new_deltas)

    zero_row = (jnp.zeros((1, BLOCK), F32),) * heads
    sums, deltas = lax.fori_loop(lo, block + 1, weigh, (zero_row, zero_row))
    inverses = [1.0 / sums[h] for h in range(heads)]
    deltas = [deltas[h] * inverses[h] for h in range(heads)]

    def spread(key_block, totals):
        rows = pl.ds(pl.multiple_of(key_block * BLOCK, BLOCK), BLOCK)
        fresh, dks, dvs = [], [], []
        for h in range(heads):
            p = weight_ref[h, rows, :] * inverses[h]
            ds = (p * (slope_ref[h, rows, :] - deltas[h])).astype(LOW)
            dvs.append(dot(p.astype(LOW), backs[h], 1, 0))
            dks.append(dot(ds, queries[h], 1, 0))
            fresh.append(totals[h] + dot(k_ref[rows, lanes[h]], ds, 0, 0))
        dk_ref[rows, :] += jnp.concatenate(dks, axis=1)
        dv_ref[rows, :] += jnp.concatenate(dvs, axis=1)
        return tuple(fresh)

    totals = lax.fori_loop(lo, block + 1, spread, (jnp.zeros((HD, BLOCK), F32),) * heads)
    here = pl.ds(pl.multiple_of(block * BLOCK, BLOCK), BLOCK)
    dq = jnp.concatenate(totals, axis=0).T * (HD**-0.5)
    dq = dq * cos_ref[here, :] - swap_halves(dq) * sin_ref[here, :]
    out_ref[here, 0:width] = dq.astype(LOW)

    @pl.when(block == pl.num_programs(0) - 1)
    def _():
        def finish(index, carried):
            rows = pl.ds(pl.multiple_of(index * BLOCK, BLOCK), BLOCK)
            dk = dk_ref[rows, :] * (HD**-0.5)
            dk = dk * cos_ref[rows, :] - swap_halves(dk) * sin_ref[rows, :]
            out_ref[rows, width : 2 * width] = dk.astype(LOW)
            out_ref[rows, 2 * width : 3 * width] = dv_ref[rows, :].astype(LOW)
            return carried

        lax.fori_loop(0, dk_ref.shape[0] // BLOCK, finish, 0)


def attend_back(lows, starts, qkv, back, cos, sin):
    count = qkv.shape[0]
    width = qkv.shape[1] // 3
    heads = width // HD
    return pl.pallas_call(
        functools.partial(attend_back_kernel, heads),
        grid_spec=pltpu.PrefetchScalarGridSpec(
            num_scalar_prefetch=1,
            grid=(count // BLOCK,),
            in_specs=[
                pl.BlockSpec((1, BLOCK), lambda i, lo: (0, i)),
                pl.BlockSpec((BLOCK, width), lambda i, lo: (i, 0)),
                pl.BlockSpec((count, width), lambda i, lo: (0, 1)),
                pl.BlockSpec((count, width), lambda i, lo: (0, 2)),
                pl.BlockSpec((BLOCK, width), lambda i, lo: (i, 0)),
                pl.BlockSpec((count, width), lambda i, lo: (0, 0)),
                pl.BlockSpec((count, width), lambda i, lo: (0, 0)),
            ],
            out_specs=pl.BlockSpec((count, 3 * width), lambda i, lo: (0, 0)),
            scratch_shapes=[
                pltpu.VMEM((heads, count, BLOCK), F32),
                pltpu.VMEM((heads, count, BLOCK), F32),
                pltpu.VMEM((count, width), F32),
                pltpu.VMEM((count, width), F32),
            ],
        ),
        out_shape=jax.ShapeDtypeStruct((count, 3 * width), LOW),
        compiler_params=pltpu.CompilerParams(vmem_limit_bytes=VMEM_LIMIT),
        cost_estimate=pl.CostEstimate(flops=20 * GIGA, bytes_accessed=0, transcendentals=0),
        name="attend_back",
    )(lows, starts, qkv, qkv, qkv, back, cos, sin)


def blend_kernel(core_ref, x_ref, own_ref, other_ref, w_ref, unit_ref, mixed_ref):
    core = core_ref[0]
    pieces = []
    for chip in range(own_ref.shape[0]):
        own, other = own_ref[chip], other_ref[chip]
        pieces.append(jnp.where(core == 0, own, other))
        pieces.append(jnp.where(core == 0, other, own))
    attended = jnp.concatenate(pieces, axis=1)
    mixed = x_ref[...].astype(F32) + dot(attended, w_ref[...], 1, 1)
    mixed_ref[...] = mixed
    inverse = lax.rsqrt(jnp.mean(mixed * mixed, axis=-1, keepdims=True) + EPSILON)
    unit_ref[...] = (mixed * inverse).astype(LOW)


def blend(core, x_all, own, other, w_out):
    count, features = x_all.shape
    chips, unused, width = own.shape
    return pl.pallas_call(
        blend_kernel,
        grid_spec=pltpu.PrefetchScalarGridSpec(
            num_scalar_prefetch=1,
            grid=(count // BLOCK,),
            in_specs=[
                pl.BlockSpec((BLOCK, features), lambda i, core: (i, 0)),
                pl.BlockSpec((chips, BLOCK, width), lambda i, core: (0, i, 0)),
                pl.BlockSpec((chips, BLOCK, width), lambda i, core: (0, i, 0)),
                pl.BlockSpec((features, features), lambda i, core: (0, 0)),
            ],
            out_specs=[
                pl.BlockSpec((BLOCK, features), lambda i, core: (i, 0)),
                pl.BlockSpec((BLOCK, features), lambda i, core: (i, 0)),
            ],
        ),
        out_shape=[
            jax.ShapeDtypeStruct((count, features), LOW),
            jax.ShapeDtypeStruct((count, features), F32),
        ],
        compiler_params=pltpu.CompilerParams(vmem_limit_bytes=VMEM_LIMIT),
        cost_estimate=pl.CostEstimate(flops=15 * GIGA, bytes_accessed=0, transcendentals=0),
        name="blend",
    )(core, x_all, own, other, w_out)


def finish_kernel(parts, scaled_parts, rows_ref, gain_ref, *refs):
    weights = refs[:scaled_parts]
    grads = refs[scaled_parts : scaled_parts + parts]
    gain_grad_ref = refs[scaled_parts + parts]
    width = rows_ref.shape[2] // parts

    @pl.when(pl.program_id(0) == 0)
    def _():
        gain_grad_ref[...] = jnp.zeros_like(gain_grad_ref)

    gain = gain_ref[...]
    for part in range(parts):
        raw = rows_ref[0, :, part * width : (part + 1) * width].astype(F32)
        if part < scaled_parts:
            product = raw * weights[part][...].astype(F32)
            gain_grad_ref[...] += jnp.sum(product, axis=1, keepdims=True)
            raw = raw * gain
        grads[part][...] = raw


def finish(rows, gain, weights, parts):
    size, share, wide = rows.shape
    width = wide // parts
    column = pl.BlockSpec((share, 1), lambda i: (0, 0))
    block = pl.BlockSpec((share, width), lambda i: (0, i))
    out = pl.pallas_call(
        functools.partial(finish_kernel, parts, len(weights)),
        grid=(size,),
        in_specs=[pl.BlockSpec((1, share, wide), lambda i: (i, 0, 0)), column]
        + [block] * len(weights),
        out_specs=[block] * parts + [column],
        out_shape=[jax.ShapeDtypeStruct((share, size * width), F32)] * parts
        + [jax.ShapeDtypeStruct((share, 1), F32)],
        compiler_params=pltpu.CompilerParams(vmem_limit_bytes=VMEM_LIMIT),
        name="finish",
    )(rows, gain, *weights)
    return out[:parts], out[parts][:, 0]


def local(
    tokens,
    cotangent,
    doc_lengths,
    gain_attn,
    w_query,
    w_key,
    w_value,
    w_out,
    gain_mlp,
    w_gate,
    w_up,
    w_down,
):
    rows, features = tokens.shape
    n_c = lax.axis_size("ctx")
    group = rows * n_c
    width = features // n_c
    here = lax.axis_index("ctx") * rows
    share = w_query.shape[0]

    core = (lax.axis_index("ctx") % 2).astype(jnp.int32).reshape(1)
    square = lax.axis_size("fsdp") == 4

    def pull_near(block, *others):
        return near(after(block, *others)) if square else ()

    def pull_far(pieces):
        return far(pieces) if square else ()

    def pulled(block, near_pieces, far_pieces):
        if square:
            return (block,) + tuple(near_pieces) + tuple(far_pieces)
        return (lax.all_gather(block, "fsdp", axis=0, tiled=True),)

    def push_near(part):
        return reduce_near(part) if square else ()

    def push_far(part, landed):
        return reduce_far(part, landed) if square else ()

    def pushed(part, landed, last):
        if square:
            return reduce_own(part, landed, last).astype(LOW)
        return lax.psum_scatter(part[0], "fsdp", scatter_dimension=0, tiled=True)

    def to_rows(value):
        value = value.reshape(n_c, share, -1)
        return lax.all_to_all(value, "ctx", split_axis=0, concat_axis=0, tiled=True)

    me = lax.axis_index("fsdp")
    if square:
        places = [(me ^ bits) * 2 + low for bits in range(4) for low in range(2)]
        order = [
            (me ^ bits) * 2 + low
            for bits, low in ((3, 0), (1, 0), (3, 1), (2, 1), (2, 0), (1, 1), (0, 0), (0, 1))
        ]
        outs = (2, 2, 4)
    else:
        places = order = range(features // UNIT)
        outs = (features // UNIT,)
    places, order = (jnp.stack([jnp.int32(place) for place in p]) for p in (places, order))

    gain_a = gain_attn.astype(F32)[:, None]
    gain_m = gain_mlp.astype(F32)[:, None]

    def scaled(weight, gain):
        return (weight.astype(F32) * gain).astype(LOW)


    def paired(left, right):
        return jnp.concatenate(
            [left.reshape(share, n_c, -1), right.reshape(share, n_c, -1)], axis=2
        ).reshape(share, -1)

    x_all = lax.all_gather(tokens, "ctx", axis=0, tiled=True)
    stacked = jnp.concatenate(
        [
            scaled(w, gain_a).reshape(share, n_c, width)
            for w in (w_query, w_key, w_value)
        ],
        axis=2,
    ).reshape(share, 3 * features)
    out_all = lax.all_gather(after(w_out, stacked), ("fsdp", "ctx"), axis=0, tiled=True)
    qkv_rows = to_columns(stacked)
    qkv_near = pull_near(qkv_rows)
    two_rows = to_columns(after(paired(scaled(w_gate, gain_m), scaled(w_up, gain_m)), qkv_rows))
    qkv_far = pull_far(qkv_near)
    w_qkv = pulled(qkv_rows, qkv_near, qkv_far)

    position = jnp.arange(group, dtype=jnp.int32)
    doc_ends = jnp.cumsum(doc_lengths[0])
    doc_starts = doc_ends - doc_lengths[0]
    starts = jnp.max(
        jnp.where(position[:, None] >= doc_starts[None, :], doc_starts[None, :], 0), axis=1
    ).astype(jnp.int32)
    turns = (position - starts).astype(F32)
    half = HD // 2
    lane = jnp.arange(128, dtype=jnp.int32)
    inv_freq = ROPE_BASE ** (-2.0 * (lane % half).astype(F32) / HD)
    angles = turns[:, None] * inv_freq[None, :]
    sign = jnp.where(lane % HD < half, -1.0, 1.0).astype(F32)
    cos = jnp.tile(jnp.cos(angles), (1, width // 128))
    sin = jnp.tile(jnp.sin(angles) * sign[None, :], (1, width // 128))
    lows = starts[::BLOCK] // BLOCK
    starts_row = starts[None, :]

    unit, qkv = project(places, x_all, w_qkv, cos, sin)
    attended = attend(lows, starts_row, qkv)
    down_rows = to_columns(after(w_down, two_rows, attended))
    two_near = pull_near(two_rows)
    attended_mine = spread_cores(after(attended, down_rows))
    two_far = pull_far(two_near)
    down_near = pull_near(down_rows, *two_near)
    attended_mine = after(attended_mine, *two_far)
    back_all = lax.all_gather(after(cotangent, attended_mine), "ctx", axis=0, tiled=True)
    attended_other = other_core(attended_mine)
    unit_mlp, mixed = blend(core, x_all, attended_mine, attended_other, out_all)
    col_two = pulled(two_rows, two_near, two_far)
    down_near = tuple(after(piece, unit_mlp) for piece in down_near)
    down_far = pull_far(down_near)
    col_down = pulled(down_rows, down_near, down_far)

    gate, up, hidden = open_units(places, unit_mlp, col_two)
    d_both = close_units(places, back_all, gate, up, col_down)
    d_unit_sums = pair_sums(times_rows(places, d_both, col_two))
    d_unit_landed = swap_chips(d_unit_sums)
    part_down = weight_grad(order, outs, (after(back_all, d_unit_sums), hidden[None]))
    down_landed = push_near(part_down)
    part_gate = weight_grad(order, outs, (after(unit_mlp, part_down[0]), d_both[:1]))
    gate_landed = push_near(part_gate)
    part_up = weight_grad(order, outs, (after(unit_mlp, part_gate[0]), d_both[1:]))
    up_landed = push_near(part_up)
    mixed_own = lax.dynamic_slice_in_dim(mixed, here, rows, 0)
    d_unit = total(after(d_unit_landed, *down_landed, *gate_landed, part_up[0]))

    inverse_own = lax.rsqrt(jnp.mean(mixed_own * mixed_own, axis=-1, keepdims=True) + EPSILON)
    unit_own = mixed_own * inverse_own
    d_mixed = cotangent.astype(F32) + inverse_own * (
        d_unit - unit_own * jnp.mean(d_unit * unit_own, axis=-1, keepdims=True)
    )
    d_mixed_low = d_mixed.astype(LOW)
    d_att = dot(d_mixed_low, out_all, 1, 0).astype(LOW)
    d_mixed_all = lax.all_gather(d_mixed_low, "ctx", axis=0, tiled=True)
    d_att_own = lax.all_to_all(d_att, "ctx", split_axis=1, concat_axis=0, tiled=True)
    down_last = push_far(part_down, down_landed)
    gate_last = push_far(part_gate, gate_landed)
    d_att_own = after(d_att_own, *down_last, *gate_last)
    branch = times_rows(places, after(hidden, d_att_own)[None], col_down)
    branch_own = lax.psum_scatter(branch, "ctx", scatter_dimension=0, tiled=True).astype(F32)
    up_last = push_far(part_up, up_landed)
    rows_down = to_rows(after(pushed(part_down, down_landed, down_last), d_att_own))

    d_qkv = attend_back(lows, starts_row, qkv, d_att_own, cos, sin)
    first_part = after(times_rows(places, d_qkv[None], w_qkv), rows_down, *up_landed)
    first_landed = swap_chips(pair_sums(first_part))
    part_qkv = weight_grad(order, outs, (unit, d_qkv[None]), (d_mixed_all, attended[None]))
    qkv_landed = push_near(part_qkv)
    first_landed = after(first_landed, *qkv_landed, *up_last)
    two_mine = jnp.concatenate(
        [pushed(part_gate, gate_landed, gate_last), pushed(part_up, up_landed, up_last)], axis=1
    )
    rows_two = to_rows(after(two_mine, first_landed))
    qkv_last = push_far(part_qkv, qkv_landed)
    rows_qkv = to_rows(after(pushed(part_qkv, qkv_landed, qkv_last), rows_two))

    layer_out = (mixed_own + after(branch_own, rows_two)).astype(LOW)
    d_first = total(first_landed)
    x_own = tokens.astype(F32)
    inverse = lax.rsqrt(jnp.mean(x_own * x_own, axis=-1, keepdims=True) + EPSILON)
    first_own = x_own * inverse
    grad_tokens = d_mixed + inverse * (
        d_first - first_own * jnp.mean(d_first * first_own, axis=-1, keepdims=True)
    )

    (grad_down,), unused = finish(rows_down, gain_m, (), 1)
    (grad_gate, grad_up), grad_gain_mlp = finish(rows_two, gain_m, (w_gate, w_up), 2)
    (grad_query, grad_key, grad_value, grad_out), grad_gain_attn = finish(
        rows_qkv, gain_a, (w_query, w_key, w_value), 4
    )
    return (
        layer_out,
        grad_tokens,
        grad_gain_attn,
        grad_query,
        grad_key,
        grad_value,
        grad_out,
        grad_gain_mlp,
        grad_gate,
        grad_up,
        grad_down,
    )


def solution(mesh):
    split = P(("fsdp", "ctx"))
    rows = P(("fsdp", "ctx"), None)
    in_specs = (rows, rows, P("fsdp", None), split, rows, rows, rows, rows, split, rows, rows, rows)
    out_specs = (rows, rows, split, rows, rows, rows, rows, split, rows, rows, rows)
    return jax.shard_map(local, mesh=mesh, in_specs=in_specs, out_specs=out_specs, check_vma=False)
```

```python
import functools

import jax
import jax.numpy as jnp
from jax import lax
from jax.experimental import pallas as pl
from jax.experimental.pallas import tpu as pltpu
from jax.sharding import PartitionSpec as P

H = 32
HD = 64
EPSILON = 1e-05
ROPE_BASE = 130000.0
BLOCK = 256
UNIT = 256
VMEM_LIMIT = 56 * 1024 * 1024
GIGA = 1000 * 1000 * 1000
LOW = jnp.bfloat16
F32 = jnp.float32


def dot(left, right, left_dim, right_dim):
    return lax.dot_general(
        left, right, (((left_dim,), (right_dim,)), ((), ())), preferred_element_type=F32
    )


def flip(axis, size, bit):
    return [(i, i ^ bit) for i in range(size)]


def same_core_groups(size):
    return [[2 * i + core for i in range(size // 2)] for core in (0, 1)]


def after(value, *others):
    return lax.optimization_barrier((value,) + others)[0]


def near(block):
    return (
        lax.ppermute(block, "fsdp", flip("fsdp", 4, 1)),
        lax.ppermute(block, "fsdp", flip("fsdp", 4, 2)),
    )


def far(pieces):
    from_x, from_y = pieces
    half = from_x.shape[0] // 2
    return (
        lax.ppermute(from_x[:half], "fsdp", flip("fsdp", 4, 2)),
        lax.ppermute(from_y[half:], "fsdp", flip("fsdp", 4, 1)),
    )


def reduce_near(part):
    return (
        lax.ppermute(part[0], "fsdp", flip("fsdp", 4, 1)),
        lax.ppermute(part[1], "fsdp", flip("fsdp", 4, 2)),
    )


def reduce_far(part, landed):
    over_x, over_y = landed
    unit = over_x.shape[0] // 2
    send_y = (part[2][:unit].astype(F32) + over_x[:unit].astype(F32)).astype(LOW)
    send_x = (part[2][unit : 2 * unit].astype(F32) + over_y[:unit].astype(F32)).astype(LOW)
    return (
        lax.ppermute(send_y, "fsdp", flip("fsdp", 4, 2)),
        lax.ppermute(send_x, "fsdp", flip("fsdp", 4, 1)),
    )


def reduce_own(part, landed, last):
    over_x, over_y = landed
    unit = over_x.shape[0] // 2
    top = part[2][2 * unit : 3 * unit].astype(F32) + over_x[unit:].astype(F32)
    low = part[2][3 * unit :].astype(F32) + over_y[unit:].astype(F32)
    return jnp.concatenate([top + last[0].astype(F32), low + last[1].astype(F32)])


def spread_cores(block):
    size = lax.axis_size("ctx")
    pairs = size // 2
    return lax.all_to_all(
        jnp.broadcast_to(block[None], (pairs,) + block.shape),
        "ctx",
        0,
        0,
        axis_index_groups=same_core_groups(size),
        tiled=True,
    )


def other_core(value):
    return lax.ppermute(value, "ctx", flip("ctx", lax.axis_size("ctx"), 1))


def pair_sums(part):
    size = lax.axis_size("ctx")
    core = lax.axis_index("ctx") % 2
    shaped = part.reshape(size // 2, 2, part.shape[0] // size, part.shape[1])
    mine = lax.dynamic_index_in_dim(shaped, core, 1, keepdims=False)
    theirs = lax.dynamic_index_in_dim(shaped, 1 - core, 1, keepdims=False)
    got = other_core(theirs)
    return (mine.astype(F32) + got.astype(F32)).astype(part.dtype)


def swap_chips(sums):
    return lax.all_to_all(
        sums,
        "ctx",
        0,
        0,
        axis_index_groups=same_core_groups(lax.axis_size("ctx")),
        tiled=True,
    )


def total(landed):
    return jnp.sum(landed.astype(F32), axis=0)


def to_columns(rows_block):
    return lax.all_to_all(rows_block, "ctx", split_axis=1, concat_axis=0, tiled=True)


def swap_halves(values):
    width = values.shape[1]
    lane = lax.broadcasted_iota(jnp.int32, values.shape, 1)
    down = pltpu.roll(values, width - HD // 2, 1)
    up = pltpu.roll(values, HD // 2, 1)
    return jnp.where(lane % HD < HD // 2, down, up)


def units_of(pieces):
    return [
        (index, unit)
        for index, piece in enumerate(pieces)
        for unit in range(piece.shape[0] // UNIT)
    ]


def gather_units(places_ref, pieces, out_ref):
    for step, (index, unit) in enumerate(units_of(pieces)):
        rows = pl.ds(pl.multiple_of(places_ref[step] * UNIT, UNIT), UNIT)
        out_ref[rows, :] = pieces[index][unit * UNIT : (unit + 1) * UNIT, :]


def project_kernel(count, places_ref, x_ref, cos_ref, sin_ref, *refs):
    pieces = refs[:count]
    unit_ref, out_ref, w_ref = refs[count:]
    width = out_ref.shape[1] // 3

    @pl.when(pl.program_id(0) == 0)
    def _():
        gather_units(places_ref, pieces, w_ref)

    x = x_ref[...].astype(F32)
    inverse = lax.rsqrt(jnp.mean(x * x, axis=-1, keepdims=True) + EPSILON)
    unit = (x * inverse).astype(LOW)
    unit_ref[...] = unit
    cos, sin = cos_ref[...], sin_ref[...]
    for part in range(3):
        columns = slice(part * width, (part + 1) * width)
        value = dot(unit, w_ref[:, columns], 1, 0)
        if part < 2:
            value = value * cos + swap_halves(value) * sin
        out_ref[:, columns] = value.astype(LOW)


def project(places, x_all, pieces, cos, sin):
    count, features = x_all.shape
    wide = pieces[0].shape[1]
    width = wide // 3
    return pl.pallas_call(
        functools.partial(project_kernel, len(pieces)),
        grid_spec=pltpu.PrefetchScalarGridSpec(
            num_scalar_prefetch=1,
            grid=(count // BLOCK,),
            in_specs=[
                pl.BlockSpec((BLOCK, features), lambda i, p: (i, 0)),
                pl.BlockSpec((BLOCK, width), lambda i, p: (i, 0)),
                pl.BlockSpec((BLOCK, width), lambda i, p: (i, 0)),
            ]
            + [pl.BlockSpec(piece.shape, lambda i, p: (0, 0)) for piece in pieces],
            out_specs=[
                pl.BlockSpec((BLOCK, features), lambda i, p: (i, 0)),
                pl.BlockSpec((BLOCK, wide), lambda i, p: (i, 0)),
            ],
            scratch_shapes=[pltpu.VMEM((features, wide), LOW)],
        ),
        out_shape=[
            jax.ShapeDtypeStruct((count, features), LOW),
            jax.ShapeDtypeStruct((count, wide), LOW),
        ],
        compiler_params=pltpu.CompilerParams(vmem_limit_bytes=VMEM_LIMIT),
        cost_estimate=pl.CostEstimate(flops=9 * GIGA, bytes_accessed=0, transcendentals=0),
        name="project",
    )(places, x_all, cos, sin, *pieces)


def open_kernel(count, places_ref, left_ref, *refs):
    gate_pieces, up_pieces = refs[:count], refs[count : 2 * count]
    gate_ref, up_ref, hidden_ref, w_gate_ref, w_up_ref = refs[2 * count :]
    gather_units(places_ref, gate_pieces, w_gate_ref)
    gather_units(places_ref, up_pieces, w_up_ref)
    left = left_ref[...]
    gate = dot(left, w_gate_ref[...], 1, 0)
    gate_ref[...] = gate
    up = dot(left, w_up_ref[...], 1, 0)
    up_ref[...] = up
    hidden_ref[...] = (gate * jax.nn.sigmoid(gate) * up).astype(LOW)


def open_units(places, left, pieces):
    count, features = left.shape
    hidden = pieces[0].shape[1] // 2
    blocks = hidden // UNIT
    column = pl.BlockSpec((count, UNIT), lambda j, p: (0, j))
    return pl.pallas_call(
        functools.partial(open_kernel, len(pieces)),
        grid_spec=pltpu.PrefetchScalarGridSpec(
            num_scalar_prefetch=1,
            grid=(blocks,),
            in_specs=[pl.BlockSpec((count, features), lambda j, p: (0, 0))]
            + [pl.BlockSpec((w.shape[0], UNIT), lambda j, p: (0, j)) for w in pieces]
            + [pl.BlockSpec((w.shape[0], UNIT), lambda j, p: (0, j + blocks)) for w in pieces],
            out_specs=[column] * 3,
            scratch_shapes=[pltpu.VMEM((features, UNIT), LOW)] * 2,
        ),
        out_shape=[
            jax.ShapeDtypeStruct((count, hidden), F32),
            jax.ShapeDtypeStruct((count, hidden), F32),
            jax.ShapeDtypeStruct((count, hidden), LOW),
        ],
        compiler_params=pltpu.CompilerParams(vmem_limit_bytes=VMEM_LIMIT),
        cost_estimate=pl.CostEstimate(flops=12 * GIGA, bytes_accessed=0, transcendentals=0),
        name="open_units",
    )(places, left, *pieces, *pieces)


def close_kernel(count, places_ref, back_ref, gate_ref, up_ref, *refs):
    pieces = refs[:count]
    out_ref, w_ref = refs[count:]
    gather_units(places_ref, pieces, w_ref)
    d_hidden = dot(back_ref[...], w_ref[...], 1, 0)
    gate = gate_ref[...]
    sigmoid = jax.nn.sigmoid(gate)
    scaled = d_hidden * sigmoid
    out_ref[0] = (scaled * up_ref[...] * (1.0 + gate * (1.0 - sigmoid))).astype(LOW)
    out_ref[1] = (scaled * gate).astype(LOW)


def close_units(places, back, gate, up, pieces):
    count, features = back.shape
    hidden = gate.shape[1]
    column = pl.BlockSpec((count, UNIT), lambda j, p: (0, j))
    return pl.pallas_call(
        functools.partial(close_kernel, len(pieces)),
        grid_spec=pltpu.PrefetchScalarGridSpec(
            num_scalar_prefetch=1,
            grid=(hidden // UNIT,),
            in_specs=[pl.BlockSpec((count, features), lambda j, p: (0, 0)), column, column]
            + [pl.BlockSpec((w.shape[0], UNIT), lambda j, p: (0, j)) for w in pieces],
            out_specs=pl.BlockSpec((2, count, UNIT), lambda j, p: (0, 0, j)),
            scratch_shapes=[pltpu.VMEM((features, UNIT), LOW)],
        ),
        out_shape=jax.ShapeDtypeStruct((2, count, hidden), LOW),
        compiler_params=pltpu.CompilerParams(vmem_limit_bytes=VMEM_LIMIT),
        cost_estimate=pl.CostEstimate(flops=7 * GIGA, bytes_accessed=0, transcendentals=0),
        name="close_units",
    )(places, back, gate, up, *pieces)


def times_rows_kernel(pieces, places_ref, left_ref, *refs):
    out_ref, w_ref = refs[len(pieces) :]
    step = pl.program_id(0)
    first = 0
    for ref, units in zip(refs, pieces):

        @pl.when((step >= first) & (step < first + units))
        def _():
            w_ref[...] = ref[...]

        first += units
    parts, unused, width = left_ref.shape
    total_ = dot(left_ref[0], w_ref[:, :width], 1, 1)
    for part in range(1, parts):
        total_ += dot(left_ref[part], w_ref[:, part * width : (part + 1) * width], 1, 1)
    out_ref[...] = total_.astype(LOW)


def times_rows(places, left, pieces):
    parts, count, width = left.shape
    units = [piece.shape[0] // UNIT for piece in pieces]
    firsts = [sum(units[:index]) for index in range(len(units))]

    def spec(first, held):
        return pl.BlockSpec(
            (UNIT, parts * width), lambda s, p: (jnp.clip(s - first, 0, held - 1), 0)
        )

    return pl.pallas_call(
        functools.partial(times_rows_kernel, units),
        grid_spec=pltpu.PrefetchScalarGridSpec(
            num_scalar_prefetch=1,
            grid=(sum(units),),
            in_specs=[pl.BlockSpec(left.shape, lambda s, p: (0, 0, 0))]
            + [spec(first, held) for first, held in zip(firsts, units)],
            out_specs=pl.BlockSpec((count, UNIT), lambda s, p: (0, p[s])),
            scratch_shapes=[pltpu.VMEM((UNIT, parts * width), LOW)],
        ),
        out_shape=jax.ShapeDtypeStruct((count, sum(units) * UNIT), LOW),
        compiler_params=pltpu.CompilerParams(vmem_limit_bytes=VMEM_LIMIT),
        cost_estimate=pl.CostEstimate(
            flops=2 * parts * count * width * sum(units) * UNIT, bytes_accessed=0, transcendentals=0
        ),
        name="times_rows",
    )(places, left, *pieces)


def weight_grad_kernel(outs, pairs, order_ref, *refs):
    step = pl.program_id(0)
    values = []
    for left_ref, right_ref in zip(refs[:pairs], refs[pairs : 2 * pairs]):
        left = left_ref[...]
        for part in range(right_ref.shape[0]):
            values.append(dot(left, right_ref[part], 0, 0).astype(LOW))
    value = values[0] if len(values) == 1 else jnp.concatenate(values, axis=1)
    first = 0
    for ref, units in zip(refs[2 * pairs :], outs):

        @pl.when((step >= first) & (step < first + units))
        def _():
            ref[...] = value

        first += units


def weight_grad(order, outs, *pairs):
    lefts = [left for left, unused in pairs]
    rights = [right for unused, right in pairs]
    count, features = lefts[0].shape
    wide = sum(right.shape[0] * right.shape[2] for right in rights)
    firsts = [sum(outs[:index]) for index in range(len(outs))]

    def spec(first, held):
        return pl.BlockSpec((UNIT, wide), lambda s, p: (jnp.clip(s - first, 0, held - 1), 0))

    return pl.pallas_call(
        functools.partial(weight_grad_kernel, outs, len(pairs)),
        grid_spec=pltpu.PrefetchScalarGridSpec(
            num_scalar_prefetch=1,
            grid=(features // UNIT,),
            in_specs=[pl.BlockSpec((count, UNIT), lambda s, p: (0, p[s]))] * len(pairs)
            + [pl.BlockSpec(right.shape, lambda s, p: (0, 0, 0)) for right in rights],
            out_specs=[spec(first, held) for first, held in zip(firsts, outs)],
        ),
        out_shape=[jax.ShapeDtypeStruct((held * UNIT, wide), LOW) for held in outs],
        compiler_params=pltpu.CompilerParams(vmem_limit_bytes=VMEM_LIMIT),
        cost_estimate=pl.CostEstimate(
            flops=2 * count * wide * features, bytes_accessed=0, transcendentals=0
        ),
        name="weight_grad",
    )(order, *lefts, *rights)


def masked_scores(key, query, key_block, query_block, starts):
    scores = dot(key, query, 1, 1) * (HD**-0.5)
    at_key = key_block * BLOCK + lax.broadcasted_iota(jnp.int32, scores.shape, 0)
    at_query = query_block * BLOCK + lax.broadcasted_iota(jnp.int32, scores.shape, 1)
    return jnp.where((at_key <= at_query) & (at_key >= starts), scores, -1e30)


def attend_kernel(heads, lo_ref, start_ref, q_ref, k_ref, v_ref, out_ref, score_ref):
    block = pl.program_id(0)
    starts = start_ref[...]
    lanes = [slice(h * HD, (h + 1) * HD) for h in range(heads)]
    queries = [q_ref[:, lane] for lane in lanes]

    def score(key_block, tops):
        rows = pl.ds(pl.multiple_of(key_block * BLOCK, BLOCK), BLOCK)
        fresh = []
        for h in range(heads):
            s = masked_scores(k_ref[rows, lanes[h]], queries[h], key_block, block, starts)
            score_ref[h, rows, :] = s
            fresh.append(jnp.maximum(tops[h], jnp.max(s, axis=0, keepdims=True)))
        return tuple(fresh)

    lo = lo_ref[block]
    tops = lax.fori_loop(lo, block + 1, score, (jnp.full((1, BLOCK), -1e30, F32),) * heads)

    def weigh(key_block, carried):
        sums, totals = carried
        rows = pl.ds(pl.multiple_of(key_block * BLOCK, BLOCK), BLOCK)
        new_sums, new_totals = [], []
        for h in range(heads):
            p = jnp.exp(score_ref[h, rows, :] - tops[h])
            new_sums.append(sums[h] + jnp.sum(p, axis=0, keepdims=True))
            new_totals.append(totals[h] + dot(v_ref[rows, lanes[h]], p.astype(LOW), 0, 0))
        return tuple(new_sums), tuple(new_totals)

    sums, totals = lax.fori_loop(
        lo,
        block + 1,
        weigh,
        ((jnp.zeros((1, BLOCK), F32),) * heads, (jnp.zeros((HD, BLOCK), F32),) * heads),
    )
    turned = jnp.concatenate([totals[h] / sums[h] for h in range(heads)], axis=0)
    out_ref[...] = turned.T.astype(LOW)


def attend(lows, starts, qkv):
    count = qkv.shape[0]
    width = qkv.shape[1] // 3
    heads = width // HD
    return pl.pallas_call(
        functools.partial(attend_kernel, heads),
        grid_spec=pltpu.PrefetchScalarGridSpec(
            num_scalar_prefetch=1,
            grid=(count // BLOCK,),
            in_specs=[
                pl.BlockSpec((1, BLOCK), lambda i, lo: (0, i)),
                pl.BlockSpec((BLOCK, width), lambda i, lo: (i, 0)),
                pl.BlockSpec((count, width), lambda i, lo: (0, 1)),
                pl.BlockSpec((count, width), lambda i, lo: (0, 2)),
            ],
            out_specs=pl.BlockSpec((BLOCK, width), lambda i, lo: (i, 0)),
            scratch_shapes=[pltpu.VMEM((heads, count, BLOCK), F32)],
        ),
        out_shape=jax.ShapeDtypeStruct((count, width), LOW),
        compiler_params=pltpu.CompilerParams(vmem_limit_bytes=VMEM_LIMIT),
        cost_estimate=pl.CostEstimate(flops=10 * GIGA, bytes_accessed=0, transcendentals=0),
        name="attend",
    )(lows, starts, qkv, qkv, qkv)


def attend_back_kernel(
    heads,
    lo_ref,
    start_ref,
    q_ref,
    k_ref,
    v_ref,
    back_ref,
    cos_ref,
    sin_ref,
    out_ref,
    weight_ref,
    slope_ref,
    dk_ref,
    dv_ref,
):
    block = pl.program_id(0)
    width = heads * HD
    starts = start_ref[...]
    lanes = [slice(h * HD, (h + 1) * HD) for h in range(heads)]
    queries = [q_ref[:, lane] for lane in lanes]
    backs = [back_ref[:, lane] for lane in lanes]

    @pl.when(block == 0)
    def _():
        dk_ref[...] = jnp.zeros_like(dk_ref)
        dv_ref[...] = jnp.zeros_like(dv_ref)

    def score(key_block, tops):
        rows = pl.ds(pl.multiple_of(key_block * BLOCK, BLOCK), BLOCK)
        fresh = []
        for h in range(heads):
            s = masked_scores(k_ref[rows, lanes[h]], queries[h], key_block, block, starts)
            weight_ref[h, rows, :] = s
            slope_ref[h, rows, :] = dot(v_ref[rows, lanes[h]], backs[h], 1, 1)
            fresh.append(jnp.maximum(tops[h], jnp.max(s, axis=0, keepdims=True)))
        return tuple(fresh)

    lo = lo_ref[block]
    tops = lax.fori_loop(lo, block + 1, score, (jnp.full((1, BLOCK), -1e30, F32),) * heads)

    def weigh(key_block, carried):
        sums, deltas = carried
        rows = pl.ds(pl.multiple_of(key_block * BLOCK, BLOCK), BLOCK)
        new_sums, new_deltas = [], []
        for h in range(heads):
            p = jnp.exp(weight_ref[h, rows, :] - tops[h])
            weight_ref[h, rows, :] = p
            new_sums.append(sums[h] + jnp.sum(p, axis=0, keepdims=True))
            new_deltas.append(
                deltas[h] + jnp.sum(p * slope_ref[h, rows, :], axis=0, keepdims=True)
            )
        return tuple(new_sums), tuple(new_deltas)

    zero_row = (jnp.zeros((1, BLOCK), F32),) * heads
    sums, deltas = lax.fori_loop(lo, block + 1, weigh, (zero_row, zero_row))
    inverses = [1.0 / sums[h] for h in range(heads)]
    deltas = [deltas[h] * inverses[h] for h in range(heads)]

    def spread(key_block, totals):
        rows = pl.ds(pl.multiple_of(key_block * BLOCK, BLOCK), BLOCK)
        fresh, dks, dvs = [], [], []
        for h in range(heads):
            p = weight_ref[h, rows, :] * inverses[h]
            ds = (p * (slope_ref[h, rows, :] - deltas[h])).astype(LOW)
            dvs.append(dot(p.astype(LOW), backs[h], 1, 0))
            dks.append(dot(ds, queries[h], 1, 0))
            fresh.append(totals[h] + dot(k_ref[rows, lanes[h]], ds, 0, 0))
        dk_ref[rows, :] += jnp.concatenate(dks, axis=1)
        dv_ref[rows, :] += jnp.concatenate(dvs, axis=1)
        return tuple(fresh)

    totals = lax.fori_loop(lo, block + 1, spread, (jnp.zeros((HD, BLOCK), F32),) * heads)
    here = pl.ds(pl.multiple_of(block * BLOCK, BLOCK), BLOCK)
    dq = jnp.concatenate(totals, axis=0).T * (HD**-0.5)
    dq = dq * cos_ref[here, :] - swap_halves(dq) * sin_ref[here, :]
    out_ref[here, 0:width] = dq.astype(LOW)

    @pl.when(block == pl.num_programs(0) - 1)
    def _():
        def finish(index, carried):
            rows = pl.ds(pl.multiple_of(index * BLOCK, BLOCK), BLOCK)
            dk = dk_ref[rows, :] * (HD**-0.5)
            dk = dk * cos_ref[rows, :] - swap_halves(dk) * sin_ref[rows, :]
            out_ref[rows, width : 2 * width] = dk.astype(LOW)
            out_ref[rows, 2 * width : 3 * width] = dv_ref[rows, :].astype(LOW)
            return carried

        lax.fori_loop(0, dk_ref.shape[0] // BLOCK, finish, 0)


def attend_back(lows, starts, qkv, back, cos, sin):
    count = qkv.shape[0]
    width = qkv.shape[1] // 3
    heads = width // HD
    return pl.pallas_call(
        functools.partial(attend_back_kernel, heads),
        grid_spec=pltpu.PrefetchScalarGridSpec(
            num_scalar_prefetch=1,
            grid=(count // BLOCK,),
            in_specs=[
                pl.BlockSpec((1, BLOCK), lambda i, lo: (0, i)),
                pl.BlockSpec((BLOCK, width), lambda i, lo: (i, 0)),
                pl.BlockSpec((count, width), lambda i, lo: (0, 1)),
                pl.BlockSpec((count, width), lambda i, lo: (0, 2)),
                pl.BlockSpec((BLOCK, width), lambda i, lo: (i, 0)),
                pl.BlockSpec((count, width), lambda i, lo: (0, 0)),
                pl.BlockSpec((count, width), lambda i, lo: (0, 0)),
            ],
            out_specs=pl.BlockSpec((count, 3 * width), lambda i, lo: (0, 0)),
            scratch_shapes=[
                pltpu.VMEM((heads, count, BLOCK), F32),
                pltpu.VMEM((heads, count, BLOCK), F32),
                pltpu.VMEM((count, width), F32),
                pltpu.VMEM((count, width), F32),
            ],
        ),
        out_shape=jax.ShapeDtypeStruct((count, 3 * width), LOW),
        compiler_params=pltpu.CompilerParams(vmem_limit_bytes=VMEM_LIMIT),
        cost_estimate=pl.CostEstimate(flops=20 * GIGA, bytes_accessed=0, transcendentals=0),
        name="attend_back",
    )(lows, starts, qkv, qkv, qkv, back, cos, sin)


def blend_kernel(core_ref, x_ref, own_ref, other_ref, w_ref, unit_ref, mixed_ref):
    core = core_ref[0]
    pieces = []
    for chip in range(own_ref.shape[0]):
        own, other = own_ref[chip], other_ref[chip]
        pieces.append(jnp.where(core == 0, own, other))
        pieces.append(jnp.where(core == 0, other, own))
    attended = jnp.concatenate(pieces, axis=1)
    mixed = x_ref[...].astype(F32) + dot(attended, w_ref[...], 1, 1)
    mixed_ref[...] = mixed
    inverse = lax.rsqrt(jnp.mean(mixed * mixed, axis=-1, keepdims=True) + EPSILON)
    unit_ref[...] = (mixed * inverse).astype(LOW)


def blend(core, x_all, own, other, w_out):
    count, features = x_all.shape
    chips, unused, width = own.shape
    return pl.pallas_call(
        blend_kernel,
        grid_spec=pltpu.PrefetchScalarGridSpec(
            num_scalar_prefetch=1,
            grid=(count // BLOCK,),
            in_specs=[
                pl.BlockSpec((BLOCK, features), lambda i, core: (i, 0)),
                pl.BlockSpec((chips, BLOCK, width), lambda i, core: (0, i, 0)),
                pl.BlockSpec((chips, BLOCK, width), lambda i, core: (0, i, 0)),
                pl.BlockSpec((features, features), lambda i, core: (0, 0)),
            ],
            out_specs=[
                pl.BlockSpec((BLOCK, features), lambda i, core: (i, 0)),
                pl.BlockSpec((BLOCK, features), lambda i, core: (i, 0)),
            ],
        ),
        out_shape=[
            jax.ShapeDtypeStruct((count, features), LOW),
            jax.ShapeDtypeStruct((count, features), F32),
        ],
        compiler_params=pltpu.CompilerParams(vmem_limit_bytes=VMEM_LIMIT),
        cost_estimate=pl.CostEstimate(flops=15 * GIGA, bytes_accessed=0, transcendentals=0),
        name="blend",
    )(core, x_all, own, other, w_out)


def finish_kernel(parts, scaled_parts, rows_ref, gain_ref, *refs):
    weights = refs[:scaled_parts]
    grads = refs[scaled_parts : scaled_parts + parts]
    gain_grad_ref = refs[scaled_parts + parts]
    width = rows_ref.shape[2] // parts

    @pl.when(pl.program_id(0) == 0)
    def _():
        gain_grad_ref[...] = jnp.zeros_like(gain_grad_ref)

    gain = gain_ref[...]
    for part in range(parts):
        raw = rows_ref[0, :, part * width : (part + 1) * width].astype(F32)
        if part < scaled_parts:
            product = raw * weights[part][...].astype(F32)
            gain_grad_ref[...] += jnp.sum(product, axis=1, keepdims=True)
            raw = raw * gain
        grads[part][...] = raw


def finish(rows, gain, weights, parts):
    size, share, wide = rows.shape
    width = wide // parts
    column = pl.BlockSpec((share, 1), lambda i: (0, 0))
    block = pl.BlockSpec((share, width), lambda i: (0, i))
    out = pl.pallas_call(
        functools.partial(finish_kernel, parts, len(weights)),
        grid=(size,),
        in_specs=[pl.BlockSpec((1, share, wide), lambda i: (i, 0, 0)), column]
        + [block] * len(weights),
        out_specs=[block] * parts + [column],
        out_shape=[jax.ShapeDtypeStruct((share, size * width), F32)] * parts
        + [jax.ShapeDtypeStruct((share, 1), F32)],
        compiler_params=pltpu.CompilerParams(vmem_limit_bytes=VMEM_LIMIT),
        name="finish",
    )(rows, gain, *weights)
    return out[:parts], out[parts][:, 0]


def local(
    tokens,
    cotangent,
    doc_lengths,
    gain_attn,
    w_query,
    w_key,
    w_value,
    w_out,
    gain_mlp,
    w_gate,
    w_up,
    w_down,
):
    rows, features = tokens.shape
    n_c = lax.axis_size("ctx")
    group = rows * n_c
    width = features // n_c
    here = lax.axis_index("ctx") * rows
    share = w_query.shape[0]

    core = (lax.axis_index("ctx") % 2).astype(jnp.int32).reshape(1)
    square = lax.axis_size("fsdp") == 4

    def pull_near(block, *others):
        return near(after(block, *others)) if square else ()

    def pull_far(pieces):
        return far(pieces) if square else ()

    def pulled(block, near_pieces, far_pieces):
        if square:
            return (block,) + tuple(near_pieces) + tuple(far_pieces)
        return (lax.all_gather(block, "fsdp", axis=0, tiled=True),)

    def push_near(part):
        return reduce_near(part) if square else ()

    def push_far(part, landed):
        return reduce_far(part, landed) if square else ()

    def pushed(part, landed, last):
        if square:
            return reduce_own(part, landed, last).astype(LOW)
        return lax.psum_scatter(part[0], "fsdp", scatter_dimension=0, tiled=True)

    def to_rows(value):
        value = value.reshape(n_c, share, -1)
        return lax.all_to_all(value, "ctx", split_axis=0, concat_axis=0, tiled=True)

    me = lax.axis_index("fsdp")
    if square:
        places = [(me ^ bits) * 2 + low for bits in range(4) for low in range(2)]
        order = [
            (me ^ bits) * 2 + low
            for bits, low in ((3, 0), (1, 0), (3, 1), (2, 1), (2, 0), (1, 1), (0, 0), (0, 1))
        ]
        outs = (2, 2, 4)
    else:
        places = order = range(features // UNIT)
        outs = (features // UNIT,)
    places, order = (jnp.stack([jnp.int32(place) for place in p]) for p in (places, order))

    gain_a = gain_attn.astype(F32)[:, None]
    gain_m = gain_mlp.astype(F32)[:, None]

    def scaled(weight, gain):
        return (weight.astype(F32) * gain).astype(LOW)


    def paired(left, right):
        return jnp.concatenate(
            [left.reshape(share, n_c, -1), right.reshape(share, n_c, -1)], axis=2
        ).reshape(share, -1)

    x_all = lax.all_gather(tokens, "ctx", axis=0, tiled=True)
    stacked = jnp.concatenate(
        [
            scaled(w, gain_a).reshape(share, n_c, width)
            for w in (w_query, w_key, w_value)
        ],
        axis=2,
    ).reshape(share, 3 * features)
    out_all = lax.all_gather(after(w_out, stacked), ("fsdp", "ctx"), axis=0, tiled=True)
    qkv_rows = to_columns(stacked)
    qkv_near = pull_near(qkv_rows)
    two_rows = to_columns(after(paired(scaled(w_gate, gain_m), scaled(w_up, gain_m)), qkv_rows))
    qkv_far = pull_far(qkv_near)
    w_qkv = pulled(qkv_rows, qkv_near, qkv_far)

    position = jnp.arange(group, dtype=jnp.int32)
    doc_ends = jnp.cumsum(doc_lengths[0])
    doc_starts = doc_ends - doc_lengths[0]
    starts = jnp.max(
        jnp.where(position[:, None] >= doc_starts[None, :], doc_starts[None, :], 0), axis=1
    ).astype(jnp.int32)
    turns = (position - starts).astype(F32)
    half = HD // 2
    lane = jnp.arange(128, dtype=jnp.int32)
    inv_freq = ROPE_BASE ** (-2.0 * (lane % half).astype(F32) / HD)
    angles = turns[:, None] * inv_freq[None, :]
    sign = jnp.where(lane % HD < half, -1.0, 1.0).astype(F32)
    cos = jnp.tile(jnp.cos(angles), (1, width // 128))
    sin = jnp.tile(jnp.sin(angles) * sign[None, :], (1, width // 128))
    lows = starts[::BLOCK] // BLOCK
    starts_row = starts[None, :]

    unit, qkv = project(places, x_all, w_qkv, cos, sin)
    attended = attend(lows, starts_row, qkv)
    down_rows = to_columns(after(w_down, two_rows, attended))
    two_near = pull_near(two_rows)
    attended_mine = spread_cores(after(attended, down_rows))
    two_far = pull_far(two_near)
    down_near = pull_near(down_rows, *two_near)
    attended_mine = after(attended_mine, *two_far)
    back_all = lax.all_gather(after(cotangent, attended_mine), "ctx", axis=0, tiled=True)
    attended_other = other_core(attended_mine)
    unit_mlp, mixed = blend(core, x_all, attended_mine, attended_other, out_all)
    col_two = pulled(two_rows, two_near, two_far)
    down_near = tuple(after(piece, unit_mlp) for piece in down_near)
    down_far = pull_far(down_near)
    col_down = pulled(down_rows, down_near, down_far)

    gate, up, hidden = open_units(places, unit_mlp, col_two)
    d_both = close_units(places, back_all, gate, up, col_down)
    d_unit_sums = pair_sums(times_rows(places, d_both, col_two))
    d_unit_landed = swap_chips(d_unit_sums)
    part_down = weight_grad(order, outs, (after(back_all, d_unit_sums), hidden[None]))
    down_landed = push_near(part_down)
    part_gate = weight_grad(order, outs, (after(unit_mlp, part_down[0]), d_both[:1]))
    part_up = weight_grad(order, outs, (after(unit_mlp, part_gate[0]), d_both[1:]))
    mixed_own = lax.dynamic_slice_in_dim(mixed, here, rows, 0)
    d_unit = total(after(d_unit_landed, *down_landed, part_up[0]))

    inverse_own = lax.rsqrt(jnp.mean(mixed_own * mixed_own, axis=-1, keepdims=True) + EPSILON)
    unit_own = mixed_own * inverse_own
    d_mixed = cotangent.astype(F32) + inverse_own * (
        d_unit - unit_own * jnp.mean(d_unit * unit_own, axis=-1, keepdims=True)
    )
    d_mixed_low = d_mixed.astype(LOW)
    d_att = dot(d_mixed_low, out_all, 1, 0).astype(LOW)
    gate_landed = push_near(part_gate)
    branch = times_rows(places, after(hidden, d_att)[None], col_down)
    down_landed = tuple(after(piece, d_att) for piece in down_landed)
    d_att_own = lax.all_to_all(d_att, "ctx", split_axis=1, concat_axis=0, tiled=True)
    down_last = push_far(part_down, down_landed)
    gate_last = push_far(part_gate, gate_landed)
    d_att_own = after(d_att_own, branch, *down_last, *gate_landed)
    d_mixed_all = lax.all_gather(after(d_mixed_low, d_att_own), "ctx", axis=0, tiled=True)
    part_up = [after(part_up[0], d_att_own)] + list(part_up[1:])
    if square:
        part_up[1] = after(part_up[1], d_att_own)
    up_landed = push_near(part_up)
    up_last = push_far(part_up, up_landed)
    rows_down = to_rows(after(pushed(part_down, down_landed, down_last), d_att_own))

    d_qkv = attend_back(lows, starts_row, qkv, d_att_own, cos, sin)
    first_part = times_rows(places, d_qkv[None], w_qkv)
    d_first = lax.psum_scatter(first_part, "ctx", scatter_dimension=0, tiled=True).astype(F32)
    part_qkv = weight_grad(
        order, outs, (unit, after(d_qkv, first_part, *up_landed, *gate_last)[None]), (d_mixed_all, attended[None])
    )
    part_qkv = [after(part, rows_down, *up_last) for part in part_qkv]
    qkv_landed = push_near(part_qkv)
    two_mine = jnp.concatenate(
        [pushed(part_gate, gate_landed, gate_last), pushed(part_up, up_landed, up_last)], axis=1
    )
    rows_two = after(to_rows(after(two_mine, rows_down)), *qkv_landed)
    branch_own = lax.psum_scatter(
        after(branch, part_qkv[0]), "ctx", scatter_dimension=0, tiled=True
    ).astype(F32)
    qkv_last = push_far(part_qkv, qkv_landed)
    rows_qkv = to_rows(after(pushed(part_qkv, qkv_landed, qkv_last), rows_two))

    layer_out = (mixed_own + after(branch_own, rows_two)).astype(LOW)
    x_own = tokens.astype(F32)
    inverse = lax.rsqrt(jnp.mean(x_own * x_own, axis=-1, keepdims=True) + EPSILON)
    first_own = x_own * inverse
    grad_tokens = d_mixed + inverse * (
        d_first - first_own * jnp.mean(d_first * first_own, axis=-1, keepdims=True)
    )

    (grad_down,), unused = finish(rows_down, gain_m, (), 1)
    (grad_gate, grad_up), grad_gain_mlp = finish(rows_two, gain_m, (w_gate, w_up), 2)
    (grad_query, grad_key, grad_value, grad_out), grad_gain_attn = finish(
        rows_qkv, gain_a, (w_query, w_key, w_value), 4
    )
    return (
        layer_out,
        grad_tokens,
        grad_gain_attn,
        grad_query,
        grad_key,
        grad_value,
        grad_out,
        grad_gain_mlp,
        grad_gate,
        grad_up,
        grad_down,
    )


def solution(mesh):
    split = P(("fsdp", "ctx"))
    rows = P(("fsdp", "ctx"), None)
    in_specs = (rows, rows, P("fsdp", None), split, rows, rows, rows, rows, split, rows, rows, rows)
    out_specs = (rows, rows, split, rows, rows, rows, rows, split, rows, rows, rows)
    return jax.shard_map(local, mesh=mesh, in_specs=in_specs, out_specs=out_specs, check_vma=False)
```

```python
import functools

import jax
import jax.numpy as jnp
from jax import lax
from jax.experimental import pallas as pl
from jax.experimental.pallas import tpu as pltpu
from jax.sharding import PartitionSpec as P

H = 32
HD = 64
EPSILON = 1e-05
ROPE_BASE = 130000.0
BLOCK = 256
UNIT = 256
VMEM_LIMIT = 56 * 1024 * 1024
GIGA = 1000 * 1000 * 1000
LOW = jnp.bfloat16
F32 = jnp.float32


def dot(left, right, left_dim, right_dim):
    return lax.dot_general(
        left, right, (((left_dim,), (right_dim,)), ((), ())), preferred_element_type=F32
    )


def flip(axis, size, bit):
    return [(i, i ^ bit) for i in range(size)]


def same_core_groups(size):
    return [[2 * i + core for i in range(size // 2)] for core in (0, 1)]


def after(value, *others):
    return lax.optimization_barrier((value,) + others)[0]


def near(block):
    return (
        lax.ppermute(block, "fsdp", flip("fsdp", 4, 1)),
        lax.ppermute(block, "fsdp", flip("fsdp", 4, 2)),
    )


def far(pieces):
    from_x, from_y = pieces
    half = from_x.shape[0] // 2
    return (
        lax.ppermute(from_x[:half], "fsdp", flip("fsdp", 4, 2)),
        lax.ppermute(from_y[half:], "fsdp", flip("fsdp", 4, 1)),
    )


def reduce_near(part):
    return (
        lax.ppermute(part[0], "fsdp", flip("fsdp", 4, 1)),
        lax.ppermute(part[1], "fsdp", flip("fsdp", 4, 2)),
    )


def reduce_far(part, landed):
    over_x, over_y = landed
    unit = over_x.shape[0] // 2
    send_y = (part[2][:unit].astype(F32) + over_x[:unit].astype(F32)).astype(LOW)
    send_x = (part[2][unit : 2 * unit].astype(F32) + over_y[:unit].astype(F32)).astype(LOW)
    return (
        lax.ppermute(send_y, "fsdp", flip("fsdp", 4, 2)),
        lax.ppermute(send_x, "fsdp", flip("fsdp", 4, 1)),
    )


def reduce_own(part, landed, last):
    over_x, over_y = landed
    unit = over_x.shape[0] // 2
    top = part[2][2 * unit : 3 * unit].astype(F32) + over_x[unit:].astype(F32)
    low = part[2][3 * unit :].astype(F32) + over_y[unit:].astype(F32)
    return jnp.concatenate([top + last[0].astype(F32), low + last[1].astype(F32)])


def spread_cores(copies):
    return lax.all_to_all(
        copies,
        "ctx",
        0,
        0,
        axis_index_groups=same_core_groups(lax.axis_size("ctx")),
        tiled=True,
    )


def other_core(value):
    return lax.ppermute(value, "ctx", flip("ctx", lax.axis_size("ctx"), 1))


def pair_sums(part):
    got = other_core(part[1])
    return (part[0].astype(F32) + got.astype(F32)).astype(part.dtype)


def swap_chips(sums):
    return lax.all_to_all(
        sums,
        "ctx",
        0,
        0,
        axis_index_groups=same_core_groups(lax.axis_size("ctx")),
        tiled=True,
    )


def total(landed):
    return jnp.sum(landed.astype(F32), axis=0)


def by_owner(rows_block):
    size = lax.axis_size("ctx")
    shaped = rows_block.reshape(rows_block.shape[0], size, -1)
    return lax.optimization_barrier(jnp.swapaxes(shaped, 0, 1))


def to_columns(pieces):
    landed = lax.all_to_all(pieces, "ctx", 0, 0, tiled=True)
    return landed.reshape(-1, landed.shape[2])


def swap_halves(values):
    width = values.shape[1]
    lane = lax.broadcasted_iota(jnp.int32, values.shape, 1)
    down = pltpu.roll(values, width - HD // 2, 1)
    up = pltpu.roll(values, HD // 2, 1)
    return jnp.where(lane % HD < HD // 2, down, up)


def units_of(pieces):
    return [
        (index, unit)
        for index, piece in enumerate(pieces)
        for unit in range(piece.shape[0] // UNIT)
    ]


def gather_units(places_ref, pieces, out_ref):
    for step, (index, unit) in enumerate(units_of(pieces)):
        rows = pl.ds(pl.multiple_of(places_ref[step] * UNIT, UNIT), UNIT)
        out_ref[rows, :] = pieces[index][unit * UNIT : (unit + 1) * UNIT, :]


def project_kernel(count, places_ref, x_ref, cos_ref, sin_ref, *refs):
    pieces = refs[:count]
    unit_ref, out_ref, w_ref = refs[count:]
    width = out_ref.shape[1] // 3

    @pl.when(pl.program_id(0) == 0)
    def _():
        gather_units(places_ref, pieces, w_ref)

    x = x_ref[...].astype(F32)
    inverse = lax.rsqrt(jnp.mean(x * x, axis=-1, keepdims=True) + EPSILON)
    unit = (x * inverse).astype(LOW)
    unit_ref[...] = unit
    cos, sin = cos_ref[...], sin_ref[...]
    for part in range(3):
        columns = slice(part * width, (part + 1) * width)
        value = dot(unit, w_ref[:, columns], 1, 0)
        if part < 2:
            value = value * cos + swap_halves(value) * sin
        out_ref[:, columns] = value.astype(LOW)


def project(places, x_all, pieces, cos, sin):
    count, features = x_all.shape
    wide = pieces[0].shape[1]
    width = wide // 3
    return pl.pallas_call(
        functools.partial(project_kernel, len(pieces)),
        grid_spec=pltpu.PrefetchScalarGridSpec(
            num_scalar_prefetch=1,
            grid=(count // BLOCK,),
            in_specs=[
                pl.BlockSpec((BLOCK, features), lambda i, p: (i, 0)),
                pl.BlockSpec((BLOCK, width), lambda i, p: (i, 0)),
                pl.BlockSpec((BLOCK, width), lambda i, p: (i, 0)),
            ]
            + [pl.BlockSpec(piece.shape, lambda i, p: (0, 0)) for piece in pieces],
            out_specs=[
                pl.BlockSpec((BLOCK, features), lambda i, p: (i, 0)),
                pl.BlockSpec((BLOCK, wide), lambda i, p: (i, 0)),
            ],
            scratch_shapes=[pltpu.VMEM((features, wide), LOW)],
        ),
        out_shape=[
            jax.ShapeDtypeStruct((count, features), LOW),
            jax.ShapeDtypeStruct((count, wide), LOW),
        ],
        compiler_params=pltpu.CompilerParams(vmem_limit_bytes=VMEM_LIMIT),
        cost_estimate=pl.CostEstimate(flops=9 * GIGA, bytes_accessed=0, transcendentals=0),
        name="project",
    )(places, x_all, cos, sin, *pieces)


def open_kernel(count, places_ref, left_ref, *refs):
    gate_pieces, up_pieces = refs[:count], refs[count : 2 * count]
    gate_ref, up_ref, hidden_ref, w_gate_ref, w_up_ref = refs[2 * count :]
    gather_units(places_ref, gate_pieces, w_gate_ref)
    gather_units(places_ref, up_pieces, w_up_ref)
    left = left_ref[...]
    gate = dot(left, w_gate_ref[...], 1, 0)
    gate_ref[...] = gate
    up = dot(left, w_up_ref[...], 1, 0)
    up_ref[...] = up
    hidden_ref[...] = (gate * jax.nn.sigmoid(gate) * up).astype(LOW)


def open_units(places, left, pieces):
    count, features = left.shape
    hidden = pieces[0].shape[1] // 2
    blocks = hidden // UNIT
    column = pl.BlockSpec((count, UNIT), lambda j, p: (0, j))
    return pl.pallas_call(
        functools.partial(open_kernel, len(pieces)),
        grid_spec=pltpu.PrefetchScalarGridSpec(
            num_scalar_prefetch=1,
            grid=(blocks,),
            in_specs=[pl.BlockSpec((count, features), lambda j, p: (0, 0))]
            + [pl.BlockSpec((w.shape[0], UNIT), lambda j, p: (0, j)) for w in pieces]
            + [pl.BlockSpec((w.shape[0], UNIT), lambda j, p: (0, j + blocks)) for w in pieces],
            out_specs=[column] * 3,
            scratch_shapes=[pltpu.VMEM((features, UNIT), LOW)] * 2,
        ),
        out_shape=[
            jax.ShapeDtypeStruct((count, hidden), F32),
            jax.ShapeDtypeStruct((count, hidden), F32),
            jax.ShapeDtypeStruct((count, hidden), LOW),
        ],
        compiler_params=pltpu.CompilerParams(vmem_limit_bytes=VMEM_LIMIT),
        cost_estimate=pl.CostEstimate(flops=12 * GIGA, bytes_accessed=0, transcendentals=0),
        name="open_units",
    )(places, left, *pieces, *pieces)


def close_kernel(count, places_ref, back_ref, gate_ref, up_ref, *refs):
    pieces = refs[:count]
    out_ref, w_ref = refs[count:]
    gather_units(places_ref, pieces, w_ref)
    d_hidden = dot(back_ref[...], w_ref[...], 1, 0)
    gate = gate_ref[...]
    sigmoid = jax.nn.sigmoid(gate)
    scaled = d_hidden * sigmoid
    out_ref[0] = (scaled * up_ref[...] * (1.0 + gate * (1.0 - sigmoid))).astype(LOW)
    out_ref[1] = (scaled * gate).astype(LOW)


def close_units(places, back, gate, up, pieces):
    count, features = back.shape
    hidden = gate.shape[1]
    column = pl.BlockSpec((count, UNIT), lambda j, p: (0, j))
    return pl.pallas_call(
        functools.partial(close_kernel, len(pieces)),
        grid_spec=pltpu.PrefetchScalarGridSpec(
            num_scalar_prefetch=1,
            grid=(hidden // UNIT,),
            in_specs=[pl.BlockSpec((count, features), lambda j, p: (0, 0)), column, column]
            + [pl.BlockSpec((w.shape[0], UNIT), lambda j, p: (0, j)) for w in pieces],
            out_specs=pl.BlockSpec((2, count, UNIT), lambda j, p: (0, 0, j)),
            scratch_shapes=[pltpu.VMEM((features, UNIT), LOW)],
        ),
        out_shape=jax.ShapeDtypeStruct((2, count, hidden), LOW),
        compiler_params=pltpu.CompilerParams(vmem_limit_bytes=VMEM_LIMIT),
        cost_estimate=pl.CostEstimate(flops=7 * GIGA, bytes_accessed=0, transcendentals=0),
        name="close_units",
    )(places, back, gate, up, *pieces)


def times_rows_kernel(pieces, chips, places_ref, core_ref, left_ref, *refs):
    out_ref = refs[len(pieces)]
    step = pl.program_id(0)
    parts, count, width = left_ref.shape

    def put(ref):
        value = dot(left_ref[0], ref[:, :width], 1, 1)
        for part in range(1, parts):
            value += dot(left_ref[part], ref[:, part * width : (part + 1) * width], 1, 1)
        low = value.astype(LOW)
        if not chips:
            out_ref[...] = low
            return
        rows = count // (2 * chips)
        for chip in range(chips):
            first = low[2 * chip * rows : (2 * chip + 1) * rows]
            second = low[(2 * chip + 1) * rows : (2 * chip + 2) * rows]
            out_ref[0, chip] = jnp.where(core_ref[0] == 0, first, second)
            out_ref[1, chip] = jnp.where(core_ref[0] == 0, second, first)

    first_step = 0
    for ref, units in zip(refs, pieces):

        @pl.when((step >= first_step) & (step < first_step + units))
        def _():
            put(ref)

        first_step += units


def times_rows(places, core, left, pieces, chips=0):
    parts, count, width = left.shape
    units = [piece.shape[0] // UNIT for piece in pieces]
    firsts = [sum(units[:index]) for index in range(len(units))]

    def spec(first, held):
        return pl.BlockSpec(
            (UNIT, parts * width), lambda s, p, c: (jnp.clip(s - first, 0, held - 1), 0)
        )

    features = sum(units) * UNIT
    if chips:
        rows = count // (2 * chips)
        out_spec = pl.BlockSpec((2, chips, rows, UNIT), lambda s, p, c: (0, 0, 0, p[s]))
        shape = (2, chips, rows, features)
    else:
        out_spec = pl.BlockSpec((count, UNIT), lambda s, p, c: (0, p[s]))
        shape = (count, features)
    return pl.pallas_call(
        functools.partial(times_rows_kernel, units, chips),
        grid_spec=pltpu.PrefetchScalarGridSpec(
            num_scalar_prefetch=2,
            grid=(sum(units),),
            in_specs=[pl.BlockSpec(left.shape, lambda s, p, c: (0, 0, 0))]
            + [spec(first, held) for first, held in zip(firsts, units)],
            out_specs=out_spec,
        ),
        out_shape=jax.ShapeDtypeStruct(shape, LOW),
        compiler_params=pltpu.CompilerParams(vmem_limit_bytes=VMEM_LIMIT),
        cost_estimate=pl.CostEstimate(
            flops=2 * parts * count * width * features, bytes_accessed=0, transcendentals=0
        ),
        name="times_rows",
    )(places, core, left, *pieces)


def weight_grad_kernel(outs, pairs, order_ref, *refs):
    step = pl.program_id(0)
    values = []
    for left_ref, right_ref in zip(refs[:pairs], refs[pairs : 2 * pairs]):
        left = left_ref[...]
        for part in range(right_ref.shape[0]):
            values.append(dot(left, right_ref[part], 0, 0).astype(LOW))
    value = values[0] if len(values) == 1 else jnp.concatenate(values, axis=1)
    first = 0
    for ref, units in zip(refs[2 * pairs :], outs):

        @pl.when((step >= first) & (step < first + units))
        def _():
            ref[...] = value

        first += units


def weight_grad(order, outs, *pairs):
    lefts = [left for left, unused in pairs]
    rights = [right for unused, right in pairs]
    count, features = lefts[0].shape
    wide = sum(right.shape[0] * right.shape[2] for right in rights)
    firsts = [sum(outs[:index]) for index in range(len(outs))]

    def spec(first, held):
        return pl.BlockSpec((UNIT, wide), lambda s, p: (jnp.clip(s - first, 0, held - 1), 0))

    return pl.pallas_call(
        functools.partial(weight_grad_kernel, outs, len(pairs)),
        grid_spec=pltpu.PrefetchScalarGridSpec(
            num_scalar_prefetch=1,
            grid=(features // UNIT,),
            in_specs=[pl.BlockSpec((count, UNIT), lambda s, p: (0, p[s]))] * len(pairs)
            + [pl.BlockSpec(right.shape, lambda s, p: (0, 0, 0)) for right in rights],
            out_specs=[spec(first, held) for first, held in zip(firsts, outs)],
        ),
        out_shape=[jax.ShapeDtypeStruct((held * UNIT, wide), LOW) for held in outs],
        compiler_params=pltpu.CompilerParams(vmem_limit_bytes=VMEM_LIMIT),
        cost_estimate=pl.CostEstimate(
            flops=2 * count * wide * features, bytes_accessed=0, transcendentals=0
        ),
        name="weight_grad",
    )(order, *lefts, *rights)


def masked_scores(key, query, key_block, query_block, starts):
    scores = dot(key, query, 1, 1) * (HD**-0.5)
    at_key = key_block * BLOCK + lax.broadcasted_iota(jnp.int32, scores.shape, 0)
    at_query = query_block * BLOCK + lax.broadcasted_iota(jnp.int32, scores.shape, 1)
    return jnp.where((at_key <= at_query) & (at_key >= starts), scores, -1e30)


def attend_kernel(heads, lo_ref, start_ref, q_ref, k_ref, v_ref, out_ref, score_ref):
    block = pl.program_id(0)
    starts = start_ref[...]
    lanes = [slice(h * HD, (h + 1) * HD) for h in range(heads)]
    queries = [q_ref[:, lane] for lane in lanes]

    def score(key_block, tops):
        rows = pl.ds(pl.multiple_of(key_block * BLOCK, BLOCK), BLOCK)
        fresh = []
        for h in range(heads):
            s = masked_scores(k_ref[rows, lanes[h]], queries[h], key_block, block, starts)
            score_ref[h, rows, :] = s
            fresh.append(jnp.maximum(tops[h], jnp.max(s, axis=0, keepdims=True)))
        return tuple(fresh)

    lo = lo_ref[block]
    tops = lax.fori_loop(lo, block + 1, score, (jnp.full((1, BLOCK), -1e30, F32),) * heads)

    def weigh(key_block, carried):
        sums, totals = carried
        rows = pl.ds(pl.multiple_of(key_block * BLOCK, BLOCK), BLOCK)
        new_sums, new_totals = [], []
        for h in range(heads):
            p = jnp.exp(score_ref[h, rows, :] - tops[h])
            new_sums.append(sums[h] + jnp.sum(p, axis=0, keepdims=True))
            new_totals.append(totals[h] + dot(v_ref[rows, lanes[h]], p.astype(LOW), 0, 0))
        return tuple(new_sums), tuple(new_totals)

    sums, totals = lax.fori_loop(
        lo,
        block + 1,
        weigh,
        ((jnp.zeros((1, BLOCK), F32),) * heads, (jnp.zeros((HD, BLOCK), F32),) * heads),
    )
    turned = jnp.concatenate([totals[h] / sums[h] for h in range(heads)], axis=0)
    low = turned.T.astype(LOW)
    for chip in range(out_ref.shape[0]):
        out_ref[chip] = low


def attend(lows, starts, qkv, chips):
    count = qkv.shape[0]
    width = qkv.shape[1] // 3
    heads = width // HD
    return pl.pallas_call(
        functools.partial(attend_kernel, heads),
        grid_spec=pltpu.PrefetchScalarGridSpec(
            num_scalar_prefetch=1,
            grid=(count // BLOCK,),
            in_specs=[
                pl.BlockSpec((1, BLOCK), lambda i, lo: (0, i)),
                pl.BlockSpec((BLOCK, width), lambda i, lo: (i, 0)),
                pl.BlockSpec((count, width), lambda i, lo: (0, 1)),
                pl.BlockSpec((count, width), lambda i, lo: (0, 2)),
            ],
            out_specs=pl.BlockSpec((chips, BLOCK, width), lambda i, lo: (0, i, 0)),
            scratch_shapes=[pltpu.VMEM((heads, count, BLOCK), F32)],
        ),
        out_shape=jax.ShapeDtypeStruct((chips, count, width), LOW),
        compiler_params=pltpu.CompilerParams(vmem_limit_bytes=VMEM_LIMIT),
        cost_estimate=pl.CostEstimate(flops=10 * GIGA, bytes_accessed=0, transcendentals=0),
        name="attend",
    )(lows, starts, qkv, qkv, qkv)


def attend_back_kernel(
    heads,
    lo_ref,
    start_ref,
    q_ref,
    k_ref,
    v_ref,
    back_ref,
    cos_ref,
    sin_ref,
    out_ref,
    weight_ref,
    slope_ref,
    dk_ref,
    dv_ref,
):
    block = pl.program_id(0)
    width = heads * HD
    starts = start_ref[...]
    lanes = [slice(h * HD, (h + 1) * HD) for h in range(heads)]
    queries = [q_ref[:, lane] for lane in lanes]
    backs = [back_ref[:, lane] for lane in lanes]

    @pl.when(block == 0)
    def _():
        dk_ref[...] = jnp.zeros_like(dk_ref)
        dv_ref[...] = jnp.zeros_like(dv_ref)

    def score(key_block, tops):
        rows = pl.ds(pl.multiple_of(key_block * BLOCK, BLOCK), BLOCK)
        fresh = []
        for h in range(heads):
            s = masked_scores(k_ref[rows, lanes[h]], queries[h], key_block, block, starts)
            weight_ref[h, rows, :] = s
            slope_ref[h, rows, :] = dot(v_ref[rows, lanes[h]], backs[h], 1, 1)
            fresh.append(jnp.maximum(tops[h], jnp.max(s, axis=0, keepdims=True)))
        return tuple(fresh)

    lo = lo_ref[block]
    tops = lax.fori_loop(lo, block + 1, score, (jnp.full((1, BLOCK), -1e30, F32),) * heads)

    def weigh(key_block, carried):
        sums, deltas = carried
        rows = pl.ds(pl.multiple_of(key_block * BLOCK, BLOCK), BLOCK)
        new_sums, new_deltas = [], []
        for h in range(heads):
            p = jnp.exp(weight_ref[h, rows, :] - tops[h])
            weight_ref[h, rows, :] = p
            new_sums.append(sums[h] + jnp.sum(p, axis=0, keepdims=True))
            new_deltas.append(
                deltas[h] + jnp.sum(p * slope_ref[h, rows, :], axis=0, keepdims=True)
            )
        return tuple(new_sums), tuple(new_deltas)

    zero_row = (jnp.zeros((1, BLOCK), F32),) * heads
    sums, deltas = lax.fori_loop(lo, block + 1, weigh, (zero_row, zero_row))
    inverses = [1.0 / sums[h] for h in range(heads)]
    deltas = [deltas[h] * inverses[h] for h in range(heads)]

    def spread(key_block, totals):
        rows = pl.ds(pl.multiple_of(key_block * BLOCK, BLOCK), BLOCK)
        fresh, dks, dvs = [], [], []
        for h in range(heads):
            p = weight_ref[h, rows, :] * inverses[h]
            ds = (p * (slope_ref[h, rows, :] - deltas[h])).astype(LOW)
            dvs.append(dot(p.astype(LOW), backs[h], 1, 0))
            dks.append(dot(ds, queries[h], 1, 0))
            fresh.append(totals[h] + dot(k_ref[rows, lanes[h]], ds, 0, 0))
        dk_ref[rows, :] += jnp.concatenate(dks, axis=1)
        dv_ref[rows, :] += jnp.concatenate(dvs, axis=1)
        return tuple(fresh)

    totals = lax.fori_loop(lo, block + 1, spread, (jnp.zeros((HD, BLOCK), F32),) * heads)
    here = pl.ds(pl.multiple_of(block * BLOCK, BLOCK), BLOCK)
    dq = jnp.concatenate(totals, axis=0).T * (HD**-0.5)
    dq = dq * cos_ref[here, :] - swap_halves(dq) * sin_ref[here, :]
    out_ref[here, 0:width] = dq.astype(LOW)

    @pl.when(block == pl.num_programs(0) - 1)
    def _():
        def finish(index, carried):
            rows = pl.ds(pl.multiple_of(index * BLOCK, BLOCK), BLOCK)
            dk = dk_ref[rows, :] * (HD**-0.5)
            dk = dk * cos_ref[rows, :] - swap_halves(dk) * sin_ref[rows, :]
            out_ref[rows, width : 2 * width] = dk.astype(LOW)
            out_ref[rows, 2 * width : 3 * width] = dv_ref[rows, :].astype(LOW)
            return carried

        lax.fori_loop(0, dk_ref.shape[0] // BLOCK, finish, 0)


def attend_back(lows, starts, qkv, back, cos, sin):
    count = qkv.shape[0]
    width = qkv.shape[1] // 3
    heads = width // HD
    return pl.pallas_call(
        functools.partial(attend_back_kernel, heads),
        grid_spec=pltpu.PrefetchScalarGridSpec(
            num_scalar_prefetch=1,
            grid=(count // BLOCK,),
            in_specs=[
                pl.BlockSpec((1, BLOCK), lambda i, lo: (0, i)),
                pl.BlockSpec((BLOCK, width), lambda i, lo: (i, 0)),
                pl.BlockSpec((count, width), lambda i, lo: (0, 1)),
                pl.BlockSpec((count, width), lambda i, lo: (0, 2)),
                pl.BlockSpec((BLOCK, width), lambda i, lo: (i, 0)),
                pl.BlockSpec((count, width), lambda i, lo: (0, 0)),
                pl.BlockSpec((count, width), lambda i, lo: (0, 0)),
            ],
            out_specs=pl.BlockSpec((count, 3 * width), lambda i, lo: (0, 0)),
            scratch_shapes=[
                pltpu.VMEM((heads, count, BLOCK), F32),
                pltpu.VMEM((heads, count, BLOCK), F32),
                pltpu.VMEM((count, width), F32),
                pltpu.VMEM((count, width), F32),
            ],
        ),
        out_shape=jax.ShapeDtypeStruct((count, 3 * width), LOW),
        compiler_params=pltpu.CompilerParams(vmem_limit_bytes=VMEM_LIMIT),
        cost_estimate=pl.CostEstimate(flops=20 * GIGA, bytes_accessed=0, transcendentals=0),
        name="attend_back",
    )(lows, starts, qkv, qkv, qkv, back, cos, sin)


def blend_kernel(core_ref, x_ref, own_ref, other_ref, w_ref, unit_ref, mixed_ref):
    core = core_ref[0]
    pieces = []
    for chip in range(own_ref.shape[0]):
        own, other = own_ref[chip], other_ref[chip]
        pieces.append(jnp.where(core == 0, own, other))
        pieces.append(jnp.where(core == 0, other, own))
    attended = jnp.concatenate(pieces, axis=1)
    mixed = x_ref[...].astype(F32) + dot(attended, w_ref[...], 1, 1)
    mixed_ref[...] = mixed
    inverse = lax.rsqrt(jnp.mean(mixed * mixed, axis=-1, keepdims=True) + EPSILON)
    unit_ref[...] = (mixed * inverse).astype(LOW)


def blend(core, x_all, own, other, w_out):
    count, features = x_all.shape
    chips, unused, width = own.shape
    return pl.pallas_call(
        blend_kernel,
        grid_spec=pltpu.PrefetchScalarGridSpec(
            num_scalar_prefetch=1,
            grid=(count // BLOCK,),
            in_specs=[
                pl.BlockSpec((BLOCK, features), lambda i, core: (i, 0)),
                pl.BlockSpec((chips, BLOCK, width), lambda i, core: (0, i, 0)),
                pl.BlockSpec((chips, BLOCK, width), lambda i, core: (0, i, 0)),
                pl.BlockSpec((features, features), lambda i, core: (0, 0)),
            ],
            out_specs=[
                pl.BlockSpec((BLOCK, features), lambda i, core: (i, 0)),
                pl.BlockSpec((BLOCK, features), lambda i, core: (i, 0)),
            ],
        ),
        out_shape=[
            jax.ShapeDtypeStruct((count, features), LOW),
            jax.ShapeDtypeStruct((count, features), F32),
        ],
        compiler_params=pltpu.CompilerParams(vmem_limit_bytes=VMEM_LIMIT),
        cost_estimate=pl.CostEstimate(flops=15 * GIGA, bytes_accessed=0, transcendentals=0),
        name="blend",
    )(core, x_all, own, other, w_out)


def finish_kernel(parts, scaled_parts, rows_ref, gain_ref, *refs):
    weights = refs[:scaled_parts]
    grads = refs[scaled_parts : scaled_parts + parts]
    gain_grad_ref = refs[scaled_parts + parts]
    width = rows_ref.shape[2] // parts

    @pl.when(pl.program_id(0) == 0)
    def _():
        gain_grad_ref[...] = jnp.zeros_like(gain_grad_ref)

    gain = gain_ref[...]
    for part in range(parts):
        for index in range(rows_ref.shape[0]):
            lane = slice(index * width, (index + 1) * width)
            raw = rows_ref[index, :, part * width : (part + 1) * width].astype(F32)
            if part < scaled_parts:
                product = raw * weights[part][:, lane].astype(F32)
                gain_grad_ref[...] += jnp.sum(product, axis=1, keepdims=True)
                raw = raw * gain
            grads[part][:, lane] = raw


def finish(rows, gain, weights, parts):
    size, share, wide = rows.shape
    width = wide // parts
    column = pl.BlockSpec((share, 1), lambda i: (0, 0))
    held = min(size, max(1, 2048 // width))
    block = pl.BlockSpec((share, held * width), lambda i: (0, i))
    out = pl.pallas_call(
        functools.partial(finish_kernel, parts, len(weights)),
        grid=(size // held,),
        in_specs=[pl.BlockSpec((held, share, wide), lambda i: (i, 0, 0)), column]
        + [block] * len(weights),
        out_specs=[block] * parts + [column],
        out_shape=[jax.ShapeDtypeStruct((share, size * width), F32)] * parts
        + [jax.ShapeDtypeStruct((share, 1), F32)],
        compiler_params=pltpu.CompilerParams(vmem_limit_bytes=VMEM_LIMIT),
        name="finish",
    )(rows, gain, *weights)
    return out[:parts], out[parts][:, 0]


def local(
    tokens,
    cotangent,
    doc_lengths,
    gain_attn,
    w_query,
    w_key,
    w_value,
    w_out,
    gain_mlp,
    w_gate,
    w_up,
    w_down,
):
    rows, features = tokens.shape
    n_c = lax.axis_size("ctx")
    group = rows * n_c
    width = features // n_c
    here = lax.axis_index("ctx") * rows
    share = w_query.shape[0]

    core = (lax.axis_index("ctx") % 2).astype(jnp.int32).reshape(1)
    square = lax.axis_size("fsdp") == 4

    def pull_near(block, *others):
        return near(after(block, *others)) if square else ()

    def pull_far(pieces):
        return far(pieces) if square else ()

    def pulled(block, near_pieces, far_pieces):
        if square:
            return (block,) + tuple(near_pieces) + tuple(far_pieces)
        return (lax.all_gather(block, "fsdp", axis=0, tiled=True),)

    def push_near(part):
        return reduce_near(part) if square else ()

    def push_far(part, landed):
        return reduce_far(part, landed) if square else ()

    def pushed(part, landed, last):
        if square:
            return reduce_own(part, landed, last).astype(LOW)
        return lax.psum_scatter(part[0], "fsdp", scatter_dimension=0, tiled=True)

    def to_rows(value):
        value = value.reshape(n_c, share, -1)
        return lax.all_to_all(value, "ctx", split_axis=0, concat_axis=0, tiled=True)

    me = lax.axis_index("fsdp")
    if square:
        places = [(me ^ bits) * 2 + low for bits in range(4) for low in range(2)]
        order = [
            (me ^ bits) * 2 + low
            for bits, low in ((3, 0), (1, 0), (3, 1), (2, 1), (2, 0), (1, 1), (0, 0), (0, 1))
        ]
        outs = (2, 2, 4)
    else:
        places = order = range(features // UNIT)
        outs = (features // UNIT,)
    places, order = (jnp.stack([jnp.int32(place) for place in p]) for p in (places, order))

    gain_a = gain_attn.astype(F32)[:, None]
    gain_m = gain_mlp.astype(F32)[:, None]

    def scaled(weight, gain):
        return (weight.astype(F32) * gain).astype(LOW)


    def paired(left, right):
        return jnp.concatenate(
            [left.reshape(share, n_c, -1), right.reshape(share, n_c, -1)], axis=2
        ).reshape(share, -1)

    x_all = lax.all_gather(tokens, "ctx", axis=0, tiled=True)
    stacked = jnp.concatenate(
        [
            scaled(w, gain_a).reshape(share, n_c, width)
            for w in (w_query, w_key, w_value)
        ],
        axis=2,
    ).reshape(share, 3 * features)
    out_all = lax.all_gather(after(w_out, stacked), ("fsdp", "ctx"), axis=0, tiled=True)
    qkv_rows = to_columns(by_owner(stacked))
    qkv_near = pull_near(qkv_rows)
    two_rows = to_columns(
        after(by_owner(paired(scaled(w_gate, gain_m), scaled(w_up, gain_m))), qkv_rows)
    )
    qkv_far = pull_far(qkv_near)
    w_qkv = pulled(qkv_rows, qkv_near, qkv_far)

    position = jnp.arange(group, dtype=jnp.int32)
    doc_ends = jnp.cumsum(doc_lengths[0])
    doc_starts = doc_ends - doc_lengths[0]
    starts = jnp.max(
        jnp.where(position[:, None] >= doc_starts[None, :], doc_starts[None, :], 0), axis=1
    ).astype(jnp.int32)
    turns = (position - starts).astype(F32)
    half = HD // 2
    lane = jnp.arange(128, dtype=jnp.int32)
    inv_freq = ROPE_BASE ** (-2.0 * (lane % half).astype(F32) / HD)
    angles = turns[:, None] * inv_freq[None, :]
    sign = jnp.where(lane % HD < half, -1.0, 1.0).astype(F32)
    cos = jnp.tile(jnp.cos(angles), (1, width // 128))
    sin = jnp.tile(jnp.sin(angles) * sign[None, :], (1, width // 128))
    lows = starts[::BLOCK] // BLOCK
    starts_row = starts[None, :]

    unit, qkv = project(places, x_all, w_qkv, cos, sin)
    attended = attend(lows, starts_row, qkv, n_c // 2)
    down_rows = to_columns(after(by_owner(w_down), two_rows, attended))
    two_near = pull_near(two_rows)
    attended_mine = spread_cores(after(attended, down_rows))
    two_far = pull_far(two_near)
    down_near = pull_near(down_rows, *two_near)
    attended_mine = after(attended_mine, *two_far)
    back_all = lax.all_gather(after(cotangent, attended_mine), "ctx", axis=0, tiled=True)
    attended_other = other_core(attended_mine)
    unit_mlp, mixed = blend(core, x_all, attended_mine, attended_other, out_all)
    col_two = pulled(two_rows, two_near, two_far)
    down_near = tuple(after(piece, unit_mlp) for piece in down_near)
    down_far = pull_far(down_near)
    col_down = pulled(down_rows, down_near, down_far)

    gate, up, hidden = open_units(places, unit_mlp, col_two)
    d_both = close_units(places, back_all, gate, up, col_down)
    d_unit_sums = pair_sums(times_rows(places, core, d_both, col_two, n_c // 2))
    d_unit_landed = swap_chips(d_unit_sums)
    part_down = weight_grad(order, outs, (after(back_all, d_unit_sums), hidden[None]))
    down_landed = push_near(part_down)
    part_gate = weight_grad(order, outs, (after(unit_mlp, part_down[0]), d_both[:1]))
    part_up = weight_grad(order, outs, (after(unit_mlp, part_gate[0]), d_both[1:]))
    mixed_own = lax.dynamic_slice_in_dim(mixed, here, rows, 0)
    d_unit = total(after(d_unit_landed, *down_landed, part_up[0]))

    inverse_own = lax.rsqrt(jnp.mean(mixed_own * mixed_own, axis=-1, keepdims=True) + EPSILON)
    unit_own = mixed_own * inverse_own
    d_mixed = cotangent.astype(F32) + inverse_own * (
        d_unit - unit_own * jnp.mean(d_unit * unit_own, axis=-1, keepdims=True)
    )
    d_mixed_low = d_mixed.astype(LOW)
    d_att = dot(d_mixed_low, out_all, 1, 0).astype(LOW)
    gate_landed = push_near(part_gate)
    branch = times_rows(places, core, after(hidden, d_att)[None], col_down)
    down_landed = tuple(after(piece, d_att) for piece in down_landed)
    d_att_own = lax.all_to_all(d_att, "ctx", split_axis=1, concat_axis=0, tiled=True)
    down_last = push_far(part_down, down_landed)
    gate_last = push_far(part_gate, gate_landed)
    d_att_own = after(d_att_own, branch, *down_last, *gate_landed)
    d_mixed_all = lax.all_gather(after(d_mixed_low, d_att_own), "ctx", axis=0, tiled=True)
    part_up = [after(part_up[0], d_att_own)] + list(part_up[1:])
    if square:
        part_up[1] = after(part_up[1], d_att_own)
    up_landed = push_near(part_up)
    up_last = push_far(part_up, up_landed)
    rows_down = to_rows(after(pushed(part_down, down_landed, down_last), d_att_own))

    d_qkv = attend_back(lows, starts_row, qkv, d_att_own, cos, sin)
    first_part = times_rows(places, core, d_qkv[None], w_qkv)
    d_first = lax.psum_scatter(first_part, "ctx", scatter_dimension=0, tiled=True).astype(F32)
    part_qkv = weight_grad(
        order, outs, (unit, after(d_qkv, first_part, *up_landed, *gate_last)[None]), (d_mixed_all, attended[:1])
    )
    part_qkv = [after(part, rows_down, *up_last) for part in part_qkv]
    qkv_landed = push_near(part_qkv)
    two_mine = jnp.concatenate(
        [pushed(part_gate, gate_landed, gate_last), pushed(part_up, up_landed, up_last)], axis=1
    )
    rows_two = after(to_rows(after(two_mine, rows_down)), *qkv_landed)
    branch_own = lax.psum_scatter(
        after(branch, part_qkv[0]), "ctx", scatter_dimension=0, tiled=True
    ).astype(F32)
    qkv_last = push_far(part_qkv, qkv_landed)
    rows_qkv = to_rows(after(pushed(part_qkv, qkv_landed, qkv_last), rows_two))

    layer_out = (mixed_own + after(branch_own, rows_two)).astype(LOW)
    x_own = tokens.astype(F32)
    inverse = lax.rsqrt(jnp.mean(x_own * x_own, axis=-1, keepdims=True) + EPSILON)
    first_own = x_own * inverse
    grad_tokens = d_mixed + inverse * (
        d_first - first_own * jnp.mean(d_first * first_own, axis=-1, keepdims=True)
    )

    (grad_down,), unused = finish(rows_down, gain_m, (), 1)
    (grad_gate, grad_up), grad_gain_mlp = finish(rows_two, gain_m, (w_gate, w_up), 2)
    (grad_query, grad_key, grad_value, grad_out), grad_gain_attn = finish(
        rows_qkv, gain_a, (w_query, w_key, w_value), 4
    )
    return (
        layer_out,
        grad_tokens,
        grad_gain_attn,
        grad_query,
        grad_key,
        grad_value,
        grad_out,
        grad_gain_mlp,
        grad_gate,
        grad_up,
        grad_down,
    )


def solution(mesh):
    split = P(("fsdp", "ctx"))
    rows = P(("fsdp", "ctx"), None)
    in_specs = (rows, rows, P("fsdp", None), split, rows, rows, rows, rows, split, rows, rows, rows)
    out_specs = (rows, rows, split, rows, rows, rows, rows, split, rows, rows, rows)
    return jax.shard_map(local, mesh=mesh, in_specs=in_specs, out_specs=out_specs, check_vma=False)
```

```python
import functools

import jax
import jax.numpy as jnp
from jax import lax
from jax.experimental import pallas as pl
from jax.experimental.pallas import tpu as pltpu
from jax.sharding import PartitionSpec as P

H = 32
HD = 64
EPSILON = 1e-05
ROPE_BASE = 130000.0
BLOCK = 256
UNIT = 256
CHUNK = 512
VMEM_LIMIT = 56 * 1024 * 1024
GIGA = 1000 * 1000 * 1000
LOW = jnp.bfloat16
F32 = jnp.float32


def dot(left, right, left_dim, right_dim):
    return lax.dot_general(
        left, right, (((left_dim,), (right_dim,)), ((), ())), preferred_element_type=F32
    )


def flip(axis, size, bit):
    return [(i, i ^ bit) for i in range(size)]


def same_core_groups(size):
    return [[2 * i + core for i in range(size // 2)] for core in (0, 1)]


def after(value, *others):
    return lax.optimization_barrier((value,) + others)[0]


def near(block):
    return (
        lax.ppermute(block, "fsdp", flip("fsdp", 4, 1)),
        lax.ppermute(block, "fsdp", flip("fsdp", 4, 2)),
    )


def far(pieces):
    from_x, from_y = pieces
    half = from_x.shape[0] // 2
    return (
        lax.ppermute(from_x[:half], "fsdp", flip("fsdp", 4, 2)),
        lax.ppermute(from_y[half:], "fsdp", flip("fsdp", 4, 1)),
    )


def reduce_near(part):
    return (
        lax.ppermute(part[0], "fsdp", flip("fsdp", 4, 1)),
        lax.ppermute(part[1], "fsdp", flip("fsdp", 4, 2)),
    )


def reduce_far(part, landed):
    over_x, over_y = landed
    unit = over_x.shape[0] // 2
    send_y = (part[2][:unit].astype(F32) + over_x[:unit].astype(F32)).astype(LOW)
    send_x = (part[2][unit : 2 * unit].astype(F32) + over_y[:unit].astype(F32)).astype(LOW)
    return (
        lax.ppermute(send_y, "fsdp", flip("fsdp", 4, 2)),
        lax.ppermute(send_x, "fsdp", flip("fsdp", 4, 1)),
    )


def reduce_own(part, landed, last):
    over_x, over_y = landed
    unit = over_x.shape[0] // 2
    top = part[2][2 * unit : 3 * unit].astype(F32) + over_x[unit:].astype(F32)
    low = part[2][3 * unit :].astype(F32) + over_y[unit:].astype(F32)
    return jnp.concatenate([top + last[0].astype(F32), low + last[1].astype(F32)])


def spread_cores(copies):
    return lax.all_to_all(
        copies,
        "ctx",
        0,
        0,
        axis_index_groups=same_core_groups(lax.axis_size("ctx")),
        tiled=True,
    )


def other_core(value):
    return lax.ppermute(value, "ctx", flip("ctx", lax.axis_size("ctx"), 1))


def pair_sums(part):
    got = other_core(part[1])
    return (part[0].astype(F32) + got.astype(F32)).astype(part.dtype)


def swap_chips(sums):
    return lax.all_to_all(
        sums,
        "ctx",
        0,
        0,
        axis_index_groups=same_core_groups(lax.axis_size("ctx")),
        tiled=True,
    )


def total(landed):
    return jnp.sum(landed.astype(F32), axis=0)


def by_owner(rows_block):
    size = lax.axis_size("ctx")
    shaped = rows_block.reshape(rows_block.shape[0], size, -1)
    return lax.optimization_barrier(jnp.swapaxes(shaped, 0, 1))


def to_columns(pieces):
    landed = lax.all_to_all(pieces, "ctx", 0, 0, tiled=True)
    return landed.reshape(-1, landed.shape[2])


def swap_halves(values):
    width = values.shape[1]
    lane = lax.broadcasted_iota(jnp.int32, values.shape, 1)
    down = pltpu.roll(values, width - HD // 2, 1)
    up = pltpu.roll(values, HD // 2, 1)
    return jnp.where(lane % HD < HD // 2, down, up)


def units_of(pieces):
    return [
        (index, unit)
        for index, piece in enumerate(pieces)
        for unit in range(piece.shape[0] // UNIT)
    ]


def gather_units(places_ref, pieces, out_ref):
    for step, (index, unit) in enumerate(units_of(pieces)):
        rows = pl.ds(pl.multiple_of(places_ref[step] * UNIT, UNIT), UNIT)
        out_ref[rows, :] = pieces[index][unit * UNIT : (unit + 1) * UNIT, :]


def project_kernel(count, places_ref, x_ref, cos_ref, sin_ref, *refs):
    pieces = refs[:count]
    unit_ref, out_ref, w_ref = refs[count:]
    width = out_ref.shape[1] // 3

    @pl.when(pl.program_id(0) == 0)
    def _():
        gather_units(places_ref, pieces, w_ref)

    x = x_ref[...].astype(F32)
    inverse = lax.rsqrt(jnp.mean(x * x, axis=-1, keepdims=True) + EPSILON)
    unit = (x * inverse).astype(LOW)
    unit_ref[...] = unit
    cos, sin = cos_ref[...], sin_ref[...]
    for part in range(3):
        columns = slice(part * width, (part + 1) * width)
        value = dot(unit, w_ref[:, columns], 1, 0)
        if part < 2:
            value = value * cos + swap_halves(value) * sin
        out_ref[:, columns] = value.astype(LOW)


def project(places, x_all, pieces, cos, sin):
    count, features = x_all.shape
    wide = pieces[0].shape[1]
    width = wide // 3
    return pl.pallas_call(
        functools.partial(project_kernel, len(pieces)),
        grid_spec=pltpu.PrefetchScalarGridSpec(
            num_scalar_prefetch=1,
            grid=(count // BLOCK,),
            in_specs=[
                pl.BlockSpec((BLOCK, features), lambda i, p: (i, 0)),
                pl.BlockSpec((BLOCK, width), lambda i, p: (i, 0)),
                pl.BlockSpec((BLOCK, width), lambda i, p: (i, 0)),
            ]
            + [pl.BlockSpec(piece.shape, lambda i, p: (0, 0)) for piece in pieces],
            out_specs=[
                pl.BlockSpec((BLOCK, features), lambda i, p: (i, 0)),
                pl.BlockSpec((BLOCK, wide), lambda i, p: (i, 0)),
            ],
            scratch_shapes=[pltpu.VMEM((features, wide), LOW)],
        ),
        out_shape=[
            jax.ShapeDtypeStruct((count, features), LOW),
            jax.ShapeDtypeStruct((count, wide), LOW),
        ],
        compiler_params=pltpu.CompilerParams(vmem_limit_bytes=VMEM_LIMIT),
        cost_estimate=pl.CostEstimate(flops=9 * GIGA, bytes_accessed=0, transcendentals=0),
        name="project",
    )(places, x_all, cos, sin, *pieces)


def open_kernel(count, places_ref, left_ref, *refs):
    gate_pieces, up_pieces = refs[:count], refs[count : 2 * count]
    gate_ref, up_ref, hidden_ref, w_gate_ref, w_up_ref = refs[2 * count :]
    gather_units(places_ref, gate_pieces, w_gate_ref)
    gather_units(places_ref, up_pieces, w_up_ref)
    for first in range(0, left_ref.shape[0], CHUNK):
        rows = slice(first, first + CHUNK)
        left = left_ref[rows, :]
        gate = dot(left, w_gate_ref[...], 1, 0)
        gate_ref[rows, :] = gate
        up = dot(left, w_up_ref[...], 1, 0)
        up_ref[rows, :] = up
        hidden_ref[rows, :] = (gate * jax.nn.sigmoid(gate) * up).astype(LOW)


def open_units(places, left, pieces):
    count, features = left.shape
    hidden = pieces[0].shape[1] // 2
    blocks = hidden // UNIT
    column = pl.BlockSpec((count, UNIT), lambda j, p: (0, j))
    return pl.pallas_call(
        functools.partial(open_kernel, len(pieces)),
        grid_spec=pltpu.PrefetchScalarGridSpec(
            num_scalar_prefetch=1,
            grid=(blocks,),
            in_specs=[pl.BlockSpec((count, features), lambda j, p: (0, 0))]
            + [pl.BlockSpec((w.shape[0], UNIT), lambda j, p: (0, j)) for w in pieces]
            + [pl.BlockSpec((w.shape[0], UNIT), lambda j, p: (0, j + blocks)) for w in pieces],
            out_specs=[column] * 3,
            scratch_shapes=[pltpu.VMEM((features, UNIT), LOW)] * 2,
        ),
        out_shape=[
            jax.ShapeDtypeStruct((count, hidden), F32),
            jax.ShapeDtypeStruct((count, hidden), F32),
            jax.ShapeDtypeStruct((count, hidden), LOW),
        ],
        compiler_params=pltpu.CompilerParams(vmem_limit_bytes=VMEM_LIMIT),
        cost_estimate=pl.CostEstimate(flops=12 * GIGA, bytes_accessed=0, transcendentals=0),
        name="open_units",
    )(places, left, *pieces, *pieces)


def close_kernel(count, places_ref, back_ref, gate_ref, up_ref, *refs):
    pieces = refs[:count]
    out_ref, w_ref = refs[count:]
    gather_units(places_ref, pieces, w_ref)
    for first in range(0, back_ref.shape[0], CHUNK):
        rows = slice(first, first + CHUNK)
        d_hidden = dot(back_ref[rows, :], w_ref[...], 1, 0)
        gate = gate_ref[rows, :]
        sigmoid = jax.nn.sigmoid(gate)
        scaled = d_hidden * sigmoid
        out_ref[0, rows, :] = (scaled * up_ref[rows, :] * (1.0 + gate * (1.0 - sigmoid))).astype(LOW)
        out_ref[1, rows, :] = (scaled * gate).astype(LOW)


def close_units(places, back, gate, up, pieces):
    count, features = back.shape
    hidden = gate.shape[1]
    column = pl.BlockSpec((count, UNIT), lambda j, p: (0, j))
    return pl.pallas_call(
        functools.partial(close_kernel, len(pieces)),
        grid_spec=pltpu.PrefetchScalarGridSpec(
            num_scalar_prefetch=1,
            grid=(hidden // UNIT,),
            in_specs=[pl.BlockSpec((count, features), lambda j, p: (0, 0)), column, column]
            + [pl.BlockSpec((w.shape[0], UNIT), lambda j, p: (0, j)) for w in pieces],
            out_specs=pl.BlockSpec((2, count, UNIT), lambda j, p: (0, 0, j)),
            scratch_shapes=[pltpu.VMEM((features, UNIT), LOW)],
        ),
        out_shape=jax.ShapeDtypeStruct((2, count, hidden), LOW),
        compiler_params=pltpu.CompilerParams(vmem_limit_bytes=VMEM_LIMIT),
        cost_estimate=pl.CostEstimate(flops=7 * GIGA, bytes_accessed=0, transcendentals=0),
        name="close_units",
    )(places, back, gate, up, *pieces)


def times_rows_kernel(pieces, chips, places_ref, core_ref, left_ref, *refs):
    out_ref = refs[len(pieces)]
    step = pl.program_id(0)
    parts, count, width = left_ref.shape

    def put(ref):
        value = dot(left_ref[0], ref[:, :width], 1, 1)
        for part in range(1, parts):
            value += dot(left_ref[part], ref[:, part * width : (part + 1) * width], 1, 1)
        low = value.astype(LOW)
        if not chips:
            out_ref[...] = low
            return
        rows = count // (2 * chips)
        for chip in range(chips):
            first = low[2 * chip * rows : (2 * chip + 1) * rows]
            second = low[(2 * chip + 1) * rows : (2 * chip + 2) * rows]
            out_ref[0, chip] = jnp.where(core_ref[0] == 0, first, second)
            out_ref[1, chip] = jnp.where(core_ref[0] == 0, second, first)

    first_step = 0
    for ref, units in zip(refs, pieces):

        @pl.when((step >= first_step) & (step < first_step + units))
        def _():
            put(ref)

        first_step += units


def times_rows(places, core, left, pieces, chips=0):
    parts, count, width = left.shape
    units = [piece.shape[0] // UNIT for piece in pieces]
    firsts = [sum(units[:index]) for index in range(len(units))]

    def spec(first, held):
        return pl.BlockSpec(
            (UNIT, parts * width), lambda s, p, c: (jnp.clip(s - first, 0, held - 1), 0)
        )

    features = sum(units) * UNIT
    if chips:
        rows = count // (2 * chips)
        out_spec = pl.BlockSpec((2, chips, rows, UNIT), lambda s, p, c: (0, 0, 0, p[s]))
        shape = (2, chips, rows, features)
    else:
        out_spec = pl.BlockSpec((count, UNIT), lambda s, p, c: (0, p[s]))
        shape = (count, features)
    return pl.pallas_call(
        functools.partial(times_rows_kernel, units, chips),
        grid_spec=pltpu.PrefetchScalarGridSpec(
            num_scalar_prefetch=2,
            grid=(sum(units),),
            in_specs=[pl.BlockSpec(left.shape, lambda s, p, c: (0, 0, 0))]
            + [spec(first, held) for first, held in zip(firsts, units)],
            out_specs=out_spec,
        ),
        out_shape=jax.ShapeDtypeStruct(shape, LOW),
        compiler_params=pltpu.CompilerParams(vmem_limit_bytes=VMEM_LIMIT),
        cost_estimate=pl.CostEstimate(
            flops=2 * parts * count * width * features, bytes_accessed=0, transcendentals=0
        ),
        name="times_rows",
    )(places, core, left, *pieces)


def weight_grad_kernel(outs, pairs, order_ref, *refs):
    step = pl.program_id(0)
    values = []
    for index, right_ref in enumerate(refs[2 * pairs : 3 * pairs]):
        left = jnp.concatenate([refs[2 * index][...], refs[2 * index + 1][...]], axis=1)
        for part in range(right_ref.shape[0]):
            values.append(dot(left, right_ref[part], 0, 0).astype(LOW))
    value = values[0] if len(values) == 1 else jnp.concatenate(values, axis=1)
    first = 0
    for ref, units in zip(refs[3 * pairs :], outs):

        @pl.when((step >= first // 2) & (step < (first + units) // 2))
        def _():
            ref[...] = value

        first += units


def weight_grad(order, outs, *pairs):
    lefts = [left for left, unused in pairs]
    rights = [right for unused, right in pairs]
    count, features = lefts[0].shape
    wide = sum(right.shape[0] * right.shape[2] for right in rights)
    firsts = [sum(outs[:index]) for index in range(len(outs))]

    def spec(first, held):
        return pl.BlockSpec(
            (2 * UNIT, wide), lambda s, p: (jnp.clip(s - first // 2, 0, held // 2 - 1), 0)
        )

    return pl.pallas_call(
        functools.partial(weight_grad_kernel, outs, len(pairs)),
        grid_spec=pltpu.PrefetchScalarGridSpec(
            num_scalar_prefetch=1,
            grid=(features // (2 * UNIT),),
            in_specs=[
                pl.BlockSpec((count, UNIT), lambda s, p: (0, p[2 * s])),
                pl.BlockSpec((count, UNIT), lambda s, p: (0, p[2 * s + 1])),
            ]
            * len(pairs)
            + [pl.BlockSpec(right.shape, lambda s, p: (0, 0, 0)) for right in rights],
            out_specs=[spec(first, held) for first, held in zip(firsts, outs)],
        ),
        out_shape=[jax.ShapeDtypeStruct((held * UNIT, wide), LOW) for held in outs],
        compiler_params=pltpu.CompilerParams(vmem_limit_bytes=VMEM_LIMIT),
        cost_estimate=pl.CostEstimate(
            flops=2 * count * wide * features, bytes_accessed=0, transcendentals=0
        ),
        name="weight_grad",
    )(order, *[left for left in lefts for unused in range(2)], *rights)


def masked_scores(key, query, key_block, query_block, starts):
    scores = dot(key, query, 1, 1) * (HD**-0.5)
    at_key = key_block * BLOCK + lax.broadcasted_iota(jnp.int32, scores.shape, 0)
    at_query = query_block * BLOCK + lax.broadcasted_iota(jnp.int32, scores.shape, 1)
    return jnp.where((at_key <= at_query) & (at_key >= starts), scores, -1e30)


def attend_kernel(heads, lo_ref, start_ref, q_ref, k_ref, v_ref, out_ref, score_ref):
    block = pl.program_id(0)
    starts = start_ref[...]
    lanes = [slice(h * HD, (h + 1) * HD) for h in range(heads)]
    queries = [q_ref[:, lane] for lane in lanes]

    def score(key_block, tops):
        rows = pl.ds(pl.multiple_of(key_block * BLOCK, BLOCK), BLOCK)
        fresh = []
        for h in range(heads):
            s = masked_scores(k_ref[rows, lanes[h]], queries[h], key_block, block, starts)
            score_ref[h, rows, :] = s
            fresh.append(jnp.maximum(tops[h], jnp.max(s, axis=0, keepdims=True)))
        return tuple(fresh)

    lo = lo_ref[block]
    tops = lax.fori_loop(lo, block + 1, score, (jnp.full((1, BLOCK), -1e30, F32),) * heads)

    def weigh(key_block, carried):
        sums, totals = carried
        rows = pl.ds(pl.multiple_of(key_block * BLOCK, BLOCK), BLOCK)
        new_sums, new_totals = [], []
        for h in range(heads):
            p = jnp.exp(score_ref[h, rows, :] - tops[h])
            new_sums.append(sums[h] + jnp.sum(p, axis=0, keepdims=True))
            new_totals.append(totals[h] + dot(v_ref[rows, lanes[h]], p.astype(LOW), 0, 0))
        return tuple(new_sums), tuple(new_totals)

    sums, totals = lax.fori_loop(
        lo,
        block + 1,
        weigh,
        ((jnp.zeros((1, BLOCK), F32),) * heads, (jnp.zeros((HD, BLOCK), F32),) * heads),
    )
    turned = jnp.concatenate([totals[h] / sums[h] for h in range(heads)], axis=0)
    low = turned.T.astype(LOW)
    for chip in range(out_ref.shape[0]):
        out_ref[chip] = low


def attend(lows, starts, qkv, chips):
    count = qkv.shape[0]
    width = qkv.shape[1] // 3
    heads = width // HD
    return pl.pallas_call(
        functools.partial(attend_kernel, heads),
        grid_spec=pltpu.PrefetchScalarGridSpec(
            num_scalar_prefetch=1,
            grid=(count // BLOCK,),
            in_specs=[
                pl.BlockSpec((1, BLOCK), lambda i, lo: (0, i)),
                pl.BlockSpec((BLOCK, width), lambda i, lo: (i, 0)),
                pl.BlockSpec((count, width), lambda i, lo: (0, 1)),
                pl.BlockSpec((count, width), lambda i, lo: (0, 2)),
            ],
            out_specs=pl.BlockSpec((chips, BLOCK, width), lambda i, lo: (0, i, 0)),
            scratch_shapes=[pltpu.VMEM((heads, count, BLOCK), F32)],
        ),
        out_shape=jax.ShapeDtypeStruct((chips, count, width), LOW),
        compiler_params=pltpu.CompilerParams(vmem_limit_bytes=VMEM_LIMIT),
        cost_estimate=pl.CostEstimate(flops=10 * GIGA, bytes_accessed=0, transcendentals=0),
        name="attend",
    )(lows, starts, qkv, qkv, qkv)


def attend_back_kernel(
    heads,
    lo_ref,
    start_ref,
    q_ref,
    k_ref,
    v_ref,
    back_ref,
    cos_ref,
    sin_ref,
    out_ref,
    weight_ref,
    slope_ref,
    dk_ref,
    dv_ref,
):
    block = pl.program_id(0)
    width = heads * HD
    starts = start_ref[...]
    lanes = [slice(h * HD, (h + 1) * HD) for h in range(heads)]
    queries = [q_ref[:, lane] for lane in lanes]
    backs = [back_ref[:, lane] for lane in lanes]

    @pl.when(block == 0)
    def _():
        dk_ref[...] = jnp.zeros_like(dk_ref)
        dv_ref[...] = jnp.zeros_like(dv_ref)

    def score(key_block, tops):
        rows = pl.ds(pl.multiple_of(key_block * BLOCK, BLOCK), BLOCK)
        fresh = []
        for h in range(heads):
            s = masked_scores(k_ref[rows, lanes[h]], queries[h], key_block, block, starts)
            weight_ref[h, rows, :] = s
            slope_ref[h, rows, :] = dot(v_ref[rows, lanes[h]], backs[h], 1, 1)
            fresh.append(jnp.maximum(tops[h], jnp.max(s, axis=0, keepdims=True)))
        return tuple(fresh)

    lo = lo_ref[block]
    tops = lax.fori_loop(lo, block + 1, score, (jnp.full((1, BLOCK), -1e30, F32),) * heads)

    def weigh(key_block, carried):
        sums, deltas = carried
        rows = pl.ds(pl.multiple_of(key_block * BLOCK, BLOCK), BLOCK)
        new_sums, new_deltas = [], []
        for h in range(heads):
            p = jnp.exp(weight_ref[h, rows, :] - tops[h])
            weight_ref[h, rows, :] = p
            new_sums.append(sums[h] + jnp.sum(p, axis=0, keepdims=True))
            new_deltas.append(
                deltas[h] + jnp.sum(p * slope_ref[h, rows, :], axis=0, keepdims=True)
            )
        return tuple(new_sums), tuple(new_deltas)

    zero_row = (jnp.zeros((1, BLOCK), F32),) * heads
    sums, deltas = lax.fori_loop(lo, block + 1, weigh, (zero_row, zero_row))
    inverses = [1.0 / sums[h] for h in range(heads)]
    deltas = [deltas[h] * inverses[h] for h in range(heads)]

    def spread(key_block, totals):
        rows = pl.ds(pl.multiple_of(key_block * BLOCK, BLOCK), BLOCK)
        fresh, dks, dvs = [], [], []
        for h in range(heads):
            p = weight_ref[h, rows, :] * inverses[h]
            ds = (p * (slope_ref[h, rows, :] - deltas[h])).astype(LOW)
            dvs.append(dot(p.astype(LOW), backs[h], 1, 0))
            dks.append(dot(ds, queries[h], 1, 0))
            fresh.append(totals[h] + dot(k_ref[rows, lanes[h]], ds, 0, 0))
        dk_ref[rows, :] += jnp.concatenate(dks, axis=1)
        dv_ref[rows, :] += jnp.concatenate(dvs, axis=1)
        return tuple(fresh)

    totals = lax.fori_loop(lo, block + 1, spread, (jnp.zeros((HD, BLOCK), F32),) * heads)
    here = pl.ds(pl.multiple_of(block * BLOCK, BLOCK), BLOCK)
    dq = jnp.concatenate(totals, axis=0).T * (HD**-0.5)
    dq = dq * cos_ref[here, :] - swap_halves(dq) * sin_ref[here, :]
    out_ref[here, 0:width] = dq.astype(LOW)

    @pl.when(block == pl.num_programs(0) - 1)
    def _():
        def finish(index, carried):
            rows = pl.ds(pl.multiple_of(index * BLOCK, BLOCK), BLOCK)
            dk = dk_ref[rows, :] * (HD**-0.5)
            dk = dk * cos_ref[rows, :] - swap_halves(dk) * sin_ref[rows, :]
            out_ref[rows, width : 2 * width] = dk.astype(LOW)
            out_ref[rows, 2 * width : 3 * width] = dv_ref[rows, :].astype(LOW)
            return carried

        lax.fori_loop(0, dk_ref.shape[0] // BLOCK, finish, 0)


def attend_back(lows, starts, qkv, back, cos, sin):
    count = qkv.shape[0]
    width = qkv.shape[1] // 3
    heads = width // HD
    return pl.pallas_call(
        functools.partial(attend_back_kernel, heads),
        grid_spec=pltpu.PrefetchScalarGridSpec(
            num_scalar_prefetch=1,
            grid=(count // BLOCK,),
            in_specs=[
                pl.BlockSpec((1, BLOCK), lambda i, lo: (0, i)),
                pl.BlockSpec((BLOCK, width), lambda i, lo: (i, 0)),
                pl.BlockSpec((count, width), lambda i, lo: (0, 1)),
                pl.BlockSpec((count, width), lambda i, lo: (0, 2)),
                pl.BlockSpec((BLOCK, width), lambda i, lo: (i, 0)),
                pl.BlockSpec((count, width), lambda i, lo: (0, 0)),
                pl.BlockSpec((count, width), lambda i, lo: (0, 0)),
            ],
            out_specs=pl.BlockSpec((count, 3 * width), lambda i, lo: (0, 0)),
            scratch_shapes=[
                pltpu.VMEM((heads, count, BLOCK), F32),
                pltpu.VMEM((heads, count, BLOCK), F32),
                pltpu.VMEM((count, width), F32),
                pltpu.VMEM((count, width), F32),
            ],
        ),
        out_shape=jax.ShapeDtypeStruct((count, 3 * width), LOW),
        compiler_params=pltpu.CompilerParams(vmem_limit_bytes=VMEM_LIMIT),
        cost_estimate=pl.CostEstimate(flops=20 * GIGA, bytes_accessed=0, transcendentals=0),
        name="attend_back",
    )(lows, starts, qkv, qkv, qkv, back, cos, sin)


def blend_kernel(core_ref, x_ref, own_ref, other_ref, w_ref, unit_ref, mixed_ref, attended_ref):
    core = core_ref[0]
    pieces = []
    for chip in range(own_ref.shape[0]):
        own, other = own_ref[chip], other_ref[chip]
        pieces.append(jnp.where(core == 0, own, other))
        pieces.append(jnp.where(core == 0, other, own))
    attended = jnp.concatenate(pieces, axis=1)
    attended_ref[...] = attended
    mixed = x_ref[...].astype(F32) + dot(attended, w_ref[...], 1, 1)
    mixed_ref[...] = mixed
    inverse = lax.rsqrt(jnp.mean(mixed * mixed, axis=-1, keepdims=True) + EPSILON)
    unit_ref[...] = (mixed * inverse).astype(LOW)


def blend(core, x_all, own, other, w_out):
    count, features = x_all.shape
    chips, unused, width = own.shape
    return pl.pallas_call(
        blend_kernel,
        grid_spec=pltpu.PrefetchScalarGridSpec(
            num_scalar_prefetch=1,
            grid=(count // BLOCK,),
            in_specs=[
                pl.BlockSpec((BLOCK, features), lambda i, core: (i, 0)),
                pl.BlockSpec((chips, BLOCK, width), lambda i, core: (0, i, 0)),
                pl.BlockSpec((chips, BLOCK, width), lambda i, core: (0, i, 0)),
                pl.BlockSpec((features, features), lambda i, core: (0, 0)),
            ],
            out_specs=[
                pl.BlockSpec((BLOCK, features), lambda i, core: (i, 0)),
                pl.BlockSpec((BLOCK, features), lambda i, core: (i, 0)),
                pl.BlockSpec((BLOCK, features), lambda i, core: (i, 0)),
            ],
        ),
        out_shape=[
            jax.ShapeDtypeStruct((count, features), LOW),
            jax.ShapeDtypeStruct((count, features), F32),
            jax.ShapeDtypeStruct((count, features), LOW),
        ],
        compiler_params=pltpu.CompilerParams(vmem_limit_bytes=VMEM_LIMIT),
        cost_estimate=pl.CostEstimate(flops=15 * GIGA, bytes_accessed=0, transcendentals=0),
        name="blend",
    )(core, x_all, own, other, w_out)


def finish_kernel(parts, scaled_parts, rows_ref, gain_ref, *refs):
    weights = refs[:scaled_parts]
    grads = refs[scaled_parts : scaled_parts + parts]
    gain_grad_ref = refs[scaled_parts + parts]
    width = rows_ref.shape[2] // parts

    @pl.when(pl.program_id(0) == 0)
    def _():
        gain_grad_ref[...] = jnp.zeros_like(gain_grad_ref)

    gain = gain_ref[...]
    for part in range(parts):
        for index in range(rows_ref.shape[0]):
            lane = slice(index * width, (index + 1) * width)
            raw = rows_ref[index, :, part * width : (part + 1) * width].astype(F32)
            if part < scaled_parts:
                product = raw * weights[part][:, lane].astype(F32)
                gain_grad_ref[...] += jnp.sum(product, axis=1, keepdims=True)
                raw = raw * gain
            grads[part][:, lane] = raw


def finish(rows, gain, weights, parts):
    size, share, wide = rows.shape
    width = wide // parts
    column = pl.BlockSpec((share, 1), lambda i: (0, 0))
    held = min(size, max(1, 2048 // width))
    block = pl.BlockSpec((share, held * width), lambda i: (0, i))
    out = pl.pallas_call(
        functools.partial(finish_kernel, parts, len(weights)),
        grid=(size // held,),
        in_specs=[pl.BlockSpec((held, share, wide), lambda i: (i, 0, 0)), column]
        + [block] * len(weights),
        out_specs=[block] * parts + [column],
        out_shape=[jax.ShapeDtypeStruct((share, size * width), F32)] * parts
        + [jax.ShapeDtypeStruct((share, 1), F32)],
        compiler_params=pltpu.CompilerParams(vmem_limit_bytes=VMEM_LIMIT),
        name="finish",
    )(rows, gain, *weights)
    return out[:parts], out[parts][:, 0]


def local(
    tokens,
    cotangent,
    doc_lengths,
    gain_attn,
    w_query,
    w_key,
    w_value,
    w_out,
    gain_mlp,
    w_gate,
    w_up,
    w_down,
):
    rows, features = tokens.shape
    n_c, n_f = lax.axis_size("ctx"), lax.axis_size("fsdp")
    group = rows * n_c
    width = features // n_c
    here = lax.axis_index("ctx") * rows
    share = w_query.shape[0]

    core = (lax.axis_index("ctx") % 2).astype(jnp.int32).reshape(1)
    square = lax.axis_size("fsdp") == 4

    def pull_near(block, *others):
        return near(after(block, *others)) if square else ()

    def pull_far(pieces):
        return far(pieces) if square else ()

    def pulled(block, near_pieces, far_pieces):
        if square:
            return (block,) + tuple(near_pieces) + tuple(far_pieces)
        return (lax.all_gather(block, "fsdp", axis=0, tiled=True),)

    def push_near(part):
        return reduce_near(part) if square else ()

    def push_far(part, landed):
        return reduce_far(part, landed) if square else ()

    def pushed(part, landed, last):
        if square:
            return reduce_own(part, landed, last).astype(LOW)
        return lax.psum_scatter(part[0], "fsdp", scatter_dimension=0, tiled=True)

    def to_rows(value):
        value = value.reshape(n_c, share, -1)
        return lax.all_to_all(value, "ctx", split_axis=0, concat_axis=0, tiled=True)

    me = lax.axis_index("fsdp")
    if square:
        places = [(me ^ bits) * 2 + low for bits in range(4) for low in range(2)]
        order = [
            (me ^ bits) * 2 + low
            for bits, low in ((3, 0), (1, 0), (3, 1), (2, 1), (2, 0), (1, 1), (0, 0), (0, 1))
        ]
        outs = (2, 2, 4)
    else:
        places = order = range(features // UNIT)
        outs = (features // UNIT,)
    places, order = (jnp.stack([jnp.int32(place) for place in p]) for p in (places, order))

    gain_a = gain_attn.astype(F32)[:, None]
    gain_m = gain_mlp.astype(F32)[:, None]

    def scaled(weight, gain):
        return (weight.astype(F32) * gain).astype(LOW)


    def paired(left, right):
        return jnp.concatenate(
            [left.reshape(share, n_c, -1), right.reshape(share, n_c, -1)], axis=2
        ).reshape(share, -1)

    x_all = lax.all_gather(tokens, "ctx", axis=0, tiled=True)
    stacked = jnp.concatenate(
        [
            scaled(w, gain_a).reshape(share, n_c, width)
            for w in (w_query, w_key, w_value)
        ],
        axis=2,
    ).reshape(share, 3 * features)
    out_all = lax.all_gather(after(w_out, stacked), ("fsdp", "ctx"), axis=0, tiled=True)
    qkv_rows = to_columns(by_owner(stacked))
    qkv_near = pull_near(qkv_rows)
    two_rows = to_columns(
        after(by_owner(paired(scaled(w_gate, gain_m), scaled(w_up, gain_m))), qkv_rows)
    )
    qkv_far = pull_far(qkv_near)
    w_qkv = pulled(qkv_rows, qkv_near, qkv_far)

    position = jnp.arange(group, dtype=jnp.int32)
    doc_ends = jnp.cumsum(doc_lengths[0])
    doc_starts = doc_ends - doc_lengths[0]
    starts = jnp.max(
        jnp.where(position[:, None] >= doc_starts[None, :], doc_starts[None, :], 0), axis=1
    ).astype(jnp.int32)
    turns = (position - starts).astype(F32)
    half = HD // 2
    lane = jnp.arange(128, dtype=jnp.int32)
    inv_freq = ROPE_BASE ** (-2.0 * (lane % half).astype(F32) / HD)
    angles = turns[:, None] * inv_freq[None, :]
    sign = jnp.where(lane % HD < half, -1.0, 1.0).astype(F32)
    cos = jnp.tile(jnp.cos(angles), (1, width // 128))
    sin = jnp.tile(jnp.sin(angles) * sign[None, :], (1, width // 128))
    lows = starts[::BLOCK] // BLOCK
    starts_row = starts[None, :]

    unit, qkv = project(places, x_all, w_qkv, cos, sin)
    attended = attend(lows, starts_row, qkv, n_c // 2)
    down_rows = to_columns(after(by_owner(w_down), two_rows, attended))
    two_near = pull_near(two_rows)
    attended_mine = spread_cores(after(attended, down_rows))
    two_far = pull_far(two_near)
    down_near = pull_near(down_rows, *two_near)
    attended_mine = after(attended_mine, *two_far)
    back_all = lax.all_gather(after(cotangent, attended_mine), "ctx", axis=0, tiled=True)
    attended_other = other_core(attended_mine)
    unit_mlp, mixed, attended_all = blend(core, x_all, attended_mine, attended_other, out_all)
    col_two = pulled(two_rows, two_near, two_far)
    down_near = tuple(after(piece, unit_mlp) for piece in down_near)
    down_far = pull_far(down_near)
    col_down = pulled(down_rows, down_near, down_far)

    gate, up, hidden = open_units(places, unit_mlp, col_two)
    d_both = close_units(places, back_all, gate, up, col_down)
    d_unit_sums = pair_sums(times_rows(places, core, d_both, col_two, n_c // 2))
    d_unit_landed = swap_chips(d_unit_sums)
    part_down = weight_grad(order, outs, (after(back_all, d_unit_sums), hidden[None]))
    down_landed = push_near(part_down)
    part_gate = weight_grad(order, outs, (after(unit_mlp, part_down[0]), d_both[:1]))
    part_up = weight_grad(order, outs, (after(unit_mlp, part_gate[0]), d_both[1:]))
    mixed_own = lax.dynamic_slice_in_dim(mixed, here, rows, 0)
    d_unit = total(after(d_unit_landed, *down_landed, part_up[0]))

    inverse_own = lax.rsqrt(jnp.mean(mixed_own * mixed_own, axis=-1, keepdims=True) + EPSILON)
    unit_own = mixed_own * inverse_own
    d_mixed = cotangent.astype(F32) + inverse_own * (
        d_unit - unit_own * jnp.mean(d_unit * unit_own, axis=-1, keepdims=True)
    )
    d_mixed_low = d_mixed.astype(LOW)
    d_att = dot(d_mixed_low, out_all, 1, 0).astype(LOW)
    branch = times_rows(places, core, after(hidden, d_att)[None], col_down)
    down_landed = tuple(after(piece, d_att) for piece in down_landed)
    owners = jnp.swapaxes(d_mixed_low.reshape(rows, n_f, n_c, share), 1, 2)
    both_ways = jnp.concatenate(
        [d_att.reshape(rows, n_c, width), owners.reshape(rows, n_c, n_f * share)], axis=2
    ).reshape(rows, -1)
    d_att_own = lax.all_to_all(both_ways, "ctx", split_axis=1, concat_axis=0, tiled=True)
    down_last = push_far(part_down, down_landed)
    part_gate = [after(part, *down_last) for part in part_gate]
    gate_landed = push_near(part_gate)
    gate_last = push_far(part_gate, gate_landed)
    d_att_own = after(d_att_own, branch, *down_last)
    branch_own = lax.psum_scatter(
        after(branch, d_att_own), "ctx", scatter_dimension=0, tiled=True
    )
    part_up = [after(part_up[0], d_att_own)] + list(part_up[1:])
    if square:
        part_up[1] = after(part_up[1], d_att_own)
    up_landed = push_near(part_up)
    up_last = push_far(part_up, up_landed)
    rows_down = to_rows(after(pushed(part_down, down_landed, down_last), d_att_own))

    d_qkv = attend_back(lows, starts_row, qkv, d_att_own, cos, sin)
    first_part = times_rows(places, core, d_qkv[None], w_qkv)
    first_part = after(first_part, rows_down, *gate_landed, *up_landed)
    d_first = lax.psum_scatter(first_part, "ctx", scatter_dimension=0, tiled=True).astype(F32)
    part_qkv = weight_grad(
        order, outs, (unit, after(d_qkv, first_part)[None])
    )
    part_out = dot(after(d_att_own, part_qkv[0])[:, width:], attended_all, 0, 0).astype(LOW)
    if square:
        part_out = part_out.reshape(n_f, share, features)
        terms = [lax.dynamic_index_in_dim(part_out, me ^ bits, 0, False) for bits in range(4)]
        for bits in range(1, 4):
            terms[bits] = lax.ppermute(terms[bits], "fsdp", flip("fsdp", 4, bits))
        grad_out = sum(term.astype(F32) for term in terms)
    else:
        grad_out = lax.psum_scatter(part_out, "fsdp", scatter_dimension=0, tiled=True).astype(F32)
    part_qkv = [after(part, *up_last, *gate_last) for part in part_qkv]
    qkv_landed = push_near(part_qkv)
    two_mine = jnp.concatenate(
        [pushed(part_gate, gate_landed, gate_last), pushed(part_up, up_landed, up_last)], axis=1
    )
    rows_two = after(to_rows(after(two_mine, rows_down)), grad_out, *qkv_landed)
    qkv_last = push_far(part_qkv, qkv_landed)
    rows_qkv = to_rows(after(pushed(part_qkv, qkv_landed, qkv_last), rows_two))

    layer_out = (mixed_own + after(branch_own, rows_two).astype(F32)).astype(LOW)
    x_own = tokens.astype(F32)
    inverse = lax.rsqrt(jnp.mean(x_own * x_own, axis=-1, keepdims=True) + EPSILON)
    first_own = x_own * inverse
    grad_tokens = d_mixed + inverse * (
        d_first - first_own * jnp.mean(d_first * first_own, axis=-1, keepdims=True)
    )

    (grad_down,), unused = finish(rows_down, gain_m, (), 1)
    (grad_gate, grad_up), grad_gain_mlp = finish(rows_two, gain_m, (w_gate, w_up), 2)
    (grad_query, grad_key, grad_value), grad_gain_attn = finish(
        rows_qkv, gain_a, (w_query, w_key, w_value), 3
    )
    return (
        layer_out,
        grad_tokens,
        grad_gain_attn,
        grad_query,
        grad_key,
        grad_value,
        grad_out,
        grad_gain_mlp,
        grad_gate,
        grad_up,
        grad_down,
    )


def solution(mesh):
    split = P(("fsdp", "ctx"))
    rows = P(("fsdp", "ctx"), None)
    in_specs = (rows, rows, P("fsdp", None), split, rows, rows, rows, rows, split, rows, rows, rows)
    out_specs = (rows, rows, split, rows, rows, rows, rows, split, rows, rows, rows)
    return jax.shard_map(local, mesh=mesh, in_specs=in_specs, out_specs=out_specs, check_vma=False)
```

```python
import functools

import jax
import jax.numpy as jnp
from jax import lax
from jax.experimental import pallas as pl
from jax.experimental.pallas import tpu as pltpu
from jax.sharding import PartitionSpec as P

H = 32
HD = 64
EPSILON = 1e-05
ROPE_BASE = 130000.0
BLOCK = 256
UNIT = 256
CHUNK = 512
VMEM_LIMIT = 56 * 1024 * 1024
GIGA = 1000 * 1000 * 1000
LOW = jnp.bfloat16
F32 = jnp.float32


def dot(left, right, left_dim, right_dim):
    return lax.dot_general(
        left, right, (((left_dim,), (right_dim,)), ((), ())), preferred_element_type=F32
    )


def flip(axis, size, bit):
    return [(i, i ^ bit) for i in range(size)]


def same_core_groups(size):
    return [[2 * i + core for i in range(size // 2)] for core in (0, 1)]


def after(value, *others):
    return lax.optimization_barrier((value,) + others)[0]


def near(block):
    return (
        lax.ppermute(block, "fsdp", flip("fsdp", 4, 1)),
        lax.ppermute(block, "fsdp", flip("fsdp", 4, 2)),
    )


def far(pieces):
    from_x, from_y = pieces
    half = from_x.shape[0] // 2
    return (
        lax.ppermute(from_x[:half], "fsdp", flip("fsdp", 4, 2)),
        lax.ppermute(from_y[half:], "fsdp", flip("fsdp", 4, 1)),
    )


def reduce_near(part):
    return (
        lax.ppermute(part[0], "fsdp", flip("fsdp", 4, 1)),
        lax.ppermute(part[1], "fsdp", flip("fsdp", 4, 2)),
    )


def reduce_far(part, landed):
    over_x, over_y = landed
    unit = over_x.shape[0] // 2
    send_y = (part[2][:unit].astype(F32) + over_x[:unit].astype(F32)).astype(LOW)
    send_x = (part[2][unit : 2 * unit].astype(F32) + over_y[:unit].astype(F32)).astype(LOW)
    return (
        lax.ppermute(send_y, "fsdp", flip("fsdp", 4, 2)),
        lax.ppermute(send_x, "fsdp", flip("fsdp", 4, 1)),
    )


def reduce_own(part, landed, last):
    over_x, over_y = landed
    unit = over_x.shape[0] // 2
    top = part[2][2 * unit : 3 * unit].astype(F32) + over_x[unit:].astype(F32)
    low = part[2][3 * unit :].astype(F32) + over_y[unit:].astype(F32)
    return jnp.concatenate([top + last[0].astype(F32), low + last[1].astype(F32)])


def spread_cores(copies):
    return lax.all_to_all(
        copies,
        "ctx",
        0,
        0,
        axis_index_groups=same_core_groups(lax.axis_size("ctx")),
        tiled=True,
    )


def other_core(value):
    return lax.ppermute(value, "ctx", flip("ctx", lax.axis_size("ctx"), 1))


def pair_sums(part):
    got = other_core(part[1])
    return (part[0].astype(F32) + got.astype(F32)).astype(part.dtype)


def swap_chips(sums):
    return lax.all_to_all(
        sums,
        "ctx",
        0,
        0,
        axis_index_groups=same_core_groups(lax.axis_size("ctx")),
        tiled=True,
    )


def total(landed):
    return jnp.sum(landed.astype(F32), axis=0)


def by_owner(rows_block):
    size = lax.axis_size("ctx")
    shaped = rows_block.reshape(rows_block.shape[0], size, -1)
    return lax.optimization_barrier(jnp.swapaxes(shaped, 0, 1))


def to_columns(pieces):
    landed = lax.all_to_all(pieces, "ctx", 0, 0, tiled=True)
    return landed.reshape(-1, landed.shape[2])


def swap_halves(values):
    width = values.shape[1]
    lane = lax.broadcasted_iota(jnp.int32, values.shape, 1)
    down = pltpu.roll(values, width - HD // 2, 1)
    up = pltpu.roll(values, HD // 2, 1)
    return jnp.where(lane % HD < HD // 2, down, up)


def units_of(pieces):
    return [
        (index, unit)
        for index, piece in enumerate(pieces)
        for unit in range(piece.shape[0] // UNIT)
    ]


def gather_units(places_ref, pieces, out_ref):
    for step, (index, unit) in enumerate(units_of(pieces)):
        rows = pl.ds(pl.multiple_of(places_ref[step] * UNIT, UNIT), UNIT)
        out_ref[rows, :] = pieces[index][unit * UNIT : (unit + 1) * UNIT, :]


def project_kernel(count, places_ref, x_ref, cos_ref, sin_ref, *refs):
    pieces = refs[:count]
    unit_ref, out_ref, w_ref = refs[count:]
    width = out_ref.shape[1] // 3

    @pl.when(pl.program_id(0) == 0)
    def _():
        gather_units(places_ref, pieces, w_ref)

    x = x_ref[...].astype(F32)
    inverse = lax.rsqrt(jnp.mean(x * x, axis=-1, keepdims=True) + EPSILON)
    unit = (x * inverse).astype(LOW)
    unit_ref[...] = unit
    cos, sin = cos_ref[...], sin_ref[...]
    for part in range(3):
        columns = slice(part * width, (part + 1) * width)
        value = dot(unit, w_ref[:, columns], 1, 0)
        if part < 2:
            value = value * cos + swap_halves(value) * sin
        out_ref[:, columns] = value.astype(LOW)


def project(places, x_all, pieces, cos, sin):
    count, features = x_all.shape
    wide = pieces[0].shape[1]
    width = wide // 3
    return pl.pallas_call(
        functools.partial(project_kernel, len(pieces)),
        grid_spec=pltpu.PrefetchScalarGridSpec(
            num_scalar_prefetch=1,
            grid=(count // BLOCK,),
            in_specs=[
                pl.BlockSpec((BLOCK, features), lambda i, p: (i, 0)),
                pl.BlockSpec((BLOCK, width), lambda i, p: (i, 0)),
                pl.BlockSpec((BLOCK, width), lambda i, p: (i, 0)),
            ]
            + [pl.BlockSpec(piece.shape, lambda i, p: (0, 0)) for piece in pieces],
            out_specs=[
                pl.BlockSpec((BLOCK, features), lambda i, p: (i, 0)),
                pl.BlockSpec((BLOCK, wide), lambda i, p: (i, 0)),
            ],
            scratch_shapes=[pltpu.VMEM((features, wide), LOW)],
        ),
        out_shape=[
            jax.ShapeDtypeStruct((count, features), LOW),
            jax.ShapeDtypeStruct((count, wide), LOW),
        ],
        compiler_params=pltpu.CompilerParams(vmem_limit_bytes=VMEM_LIMIT),
        cost_estimate=pl.CostEstimate(flops=9 * GIGA, bytes_accessed=0, transcendentals=0),
        name="project",
    )(places, x_all, cos, sin, *pieces)


def open_kernel(count, places_ref, left_ref, *refs):
    gate_pieces, up_pieces = refs[:count], refs[count : 2 * count]
    gate_ref, up_ref, hidden_ref, w_gate_ref, w_up_ref = refs[2 * count :]
    gather_units(places_ref, gate_pieces, w_gate_ref)
    gather_units(places_ref, up_pieces, w_up_ref)
    for first in range(0, left_ref.shape[0], CHUNK):
        rows = slice(first, first + CHUNK)
        left = left_ref[rows, :]
        gate = dot(left, w_gate_ref[...], 1, 0)
        gate_ref[rows, :] = gate
        up = dot(left, w_up_ref[...], 1, 0)
        up_ref[rows, :] = up
        hidden_ref[rows, :] = (gate * jax.nn.sigmoid(gate) * up).astype(LOW)


def open_units(places, left, pieces):
    count, features = left.shape
    hidden = pieces[0].shape[1] // 2
    blocks = hidden // UNIT
    column = pl.BlockSpec((count, UNIT), lambda j, p: (0, j))
    return pl.pallas_call(
        functools.partial(open_kernel, len(pieces)),
        grid_spec=pltpu.PrefetchScalarGridSpec(
            num_scalar_prefetch=1,
            grid=(blocks,),
            in_specs=[pl.BlockSpec((count, features), lambda j, p: (0, 0))]
            + [pl.BlockSpec((w.shape[0], UNIT), lambda j, p: (0, j)) for w in pieces]
            + [pl.BlockSpec((w.shape[0], UNIT), lambda j, p: (0, j + blocks)) for w in pieces],
            out_specs=[column] * 3,
            scratch_shapes=[pltpu.VMEM((features, UNIT), LOW)] * 2,
        ),
        out_shape=[
            jax.ShapeDtypeStruct((count, hidden), F32),
            jax.ShapeDtypeStruct((count, hidden), F32),
            jax.ShapeDtypeStruct((count, hidden), LOW),
        ],
        compiler_params=pltpu.CompilerParams(vmem_limit_bytes=VMEM_LIMIT),
        cost_estimate=pl.CostEstimate(flops=12 * GIGA, bytes_accessed=0, transcendentals=0),
        name="open_units",
    )(places, left, *pieces, *pieces)


def close_kernel(count, places_ref, back_ref, gate_ref, up_ref, *refs):
    pieces = refs[:count]
    out_ref, w_ref = refs[count:]
    gather_units(places_ref, pieces, w_ref)
    for first in range(0, back_ref.shape[0], CHUNK):
        rows = slice(first, first + CHUNK)
        d_hidden = dot(back_ref[rows, :], w_ref[...], 1, 0)
        gate = gate_ref[rows, :]
        sigmoid = jax.nn.sigmoid(gate)
        scaled = d_hidden * sigmoid
        out_ref[0, rows, :] = (scaled * up_ref[rows, :] * (1.0 + gate * (1.0 - sigmoid))).astype(LOW)
        out_ref[1, rows, :] = (scaled * gate).astype(LOW)


def close_units(places, back, gate, up, pieces):
    count, features = back.shape
    hidden = gate.shape[1]
    column = pl.BlockSpec((count, UNIT), lambda j, p: (0, j))
    return pl.pallas_call(
        functools.partial(close_kernel, len(pieces)),
        grid_spec=pltpu.PrefetchScalarGridSpec(
            num_scalar_prefetch=1,
            grid=(hidden // UNIT,),
            in_specs=[pl.BlockSpec((count, features), lambda j, p: (0, 0)), column, column]
            + [pl.BlockSpec((w.shape[0], UNIT), lambda j, p: (0, j)) for w in pieces],
            out_specs=pl.BlockSpec((2, count, UNIT), lambda j, p: (0, 0, j)),
            scratch_shapes=[pltpu.VMEM((features, UNIT), LOW)],
        ),
        out_shape=jax.ShapeDtypeStruct((2, count, hidden), LOW),
        compiler_params=pltpu.CompilerParams(vmem_limit_bytes=VMEM_LIMIT),
        cost_estimate=pl.CostEstimate(flops=7 * GIGA, bytes_accessed=0, transcendentals=0),
        name="close_units",
    )(places, back, gate, up, *pieces)


def times_rows_kernel(pieces, chips, places_ref, core_ref, left_ref, *refs):
    out_ref = refs[len(pieces)]
    step = pl.program_id(0)
    parts, count, width = left_ref.shape

    def put(ref):
        value = dot(left_ref[0], ref[:, :width], 1, 1)
        for part in range(1, parts):
            value += dot(left_ref[part], ref[:, part * width : (part + 1) * width], 1, 1)
        low = value.astype(LOW)
        if not chips:
            out_ref[...] = low
            return
        rows = count // (2 * chips)
        for chip in range(chips):
            first = low[2 * chip * rows : (2 * chip + 1) * rows]
            second = low[(2 * chip + 1) * rows : (2 * chip + 2) * rows]
            out_ref[0, chip] = jnp.where(core_ref[0] == 0, first, second)
            out_ref[1, chip] = jnp.where(core_ref[0] == 0, second, first)

    first_step = 0
    for ref, units in zip(refs, pieces):

        @pl.when((step >= first_step) & (step < first_step + units))
        def _():
            put(ref)

        first_step += units


def times_rows(places, core, left, pieces, chips=0):
    parts, count, width = left.shape
    units = [piece.shape[0] // UNIT for piece in pieces]
    firsts = [sum(units[:index]) for index in range(len(units))]

    def spec(first, held):
        return pl.BlockSpec(
            (UNIT, parts * width), lambda s, p, c: (jnp.clip(s - first, 0, held - 1), 0)
        )

    features = sum(units) * UNIT
    if chips:
        rows = count // (2 * chips)
        out_spec = pl.BlockSpec((2, chips, rows, UNIT), lambda s, p, c: (0, 0, 0, p[s]))
        shape = (2, chips, rows, features)
    else:
        out_spec = pl.BlockSpec((count, UNIT), lambda s, p, c: (0, p[s]))
        shape = (count, features)
    return pl.pallas_call(
        functools.partial(times_rows_kernel, units, chips),
        grid_spec=pltpu.PrefetchScalarGridSpec(
            num_scalar_prefetch=2,
            grid=(sum(units),),
            in_specs=[pl.BlockSpec(left.shape, lambda s, p, c: (0, 0, 0))]
            + [spec(first, held) for first, held in zip(firsts, units)],
            out_specs=out_spec,
        ),
        out_shape=jax.ShapeDtypeStruct(shape, LOW),
        compiler_params=pltpu.CompilerParams(vmem_limit_bytes=VMEM_LIMIT),
        cost_estimate=pl.CostEstimate(
            flops=2 * parts * count * width * features, bytes_accessed=0, transcendentals=0
        ),
        name="times_rows",
    )(places, core, left, *pieces)


def weight_grad_kernel(outs, pairs, order_ref, *refs):
    step = pl.program_id(0)
    values = []
    for index, right_ref in enumerate(refs[2 * pairs : 3 * pairs]):
        left = jnp.concatenate([refs[2 * index][...], refs[2 * index + 1][...]], axis=1)
        for part in range(right_ref.shape[0]):
            values.append(dot(left, right_ref[part], 0, 0).astype(LOW))
    value = values[0] if len(values) == 1 else jnp.concatenate(values, axis=1)
    first = 0
    for ref, units in zip(refs[3 * pairs :], outs):

        @pl.when((step >= first // 2) & (step < (first + units) // 2))
        def _():
            ref[...] = value

        first += units


def weight_grad(order, outs, *pairs):
    lefts = [left for left, unused in pairs]
    rights = [right for unused, right in pairs]
    count, features = lefts[0].shape
    wide = sum(right.shape[0] * right.shape[2] for right in rights)
    firsts = [sum(outs[:index]) for index in range(len(outs))]

    def spec(first, held):
        return pl.BlockSpec(
            (2 * UNIT, wide), lambda s, p: (jnp.clip(s - first // 2, 0, held // 2 - 1), 0)
        )

    return pl.pallas_call(
        functools.partial(weight_grad_kernel, outs, len(pairs)),
        grid_spec=pltpu.PrefetchScalarGridSpec(
            num_scalar_prefetch=1,
            grid=(features // (2 * UNIT),),
            in_specs=[
                pl.BlockSpec((count, UNIT), lambda s, p: (0, p[2 * s])),
                pl.BlockSpec((count, UNIT), lambda s, p: (0, p[2 * s + 1])),
            ]
            * len(pairs)
            + [pl.BlockSpec(right.shape, lambda s, p: (0, 0, 0)) for right in rights],
            out_specs=[spec(first, held) for first, held in zip(firsts, outs)],
        ),
        out_shape=[jax.ShapeDtypeStruct((held * UNIT, wide), LOW) for held in outs],
        compiler_params=pltpu.CompilerParams(vmem_limit_bytes=VMEM_LIMIT),
        cost_estimate=pl.CostEstimate(
            flops=2 * count * wide * features, bytes_accessed=0, transcendentals=0
        ),
        name="weight_grad",
    )(order, *[left for left in lefts for unused in range(2)], *rights)


def masked_scores(key, query, key_block, query_block, starts):
    scores = dot(key, query, 1, 1) * (HD**-0.5)
    at_key = key_block * BLOCK + lax.broadcasted_iota(jnp.int32, scores.shape, 0)
    at_query = query_block * BLOCK + lax.broadcasted_iota(jnp.int32, scores.shape, 1)
    return jnp.where((at_key <= at_query) & (at_key >= starts), scores, -1e30)


def attend_kernel(heads, lo_ref, start_ref, q_ref, k_ref, v_ref, out_ref, score_ref):
    block = pl.program_id(0)
    starts = start_ref[...]
    lanes = [slice(h * HD, (h + 1) * HD) for h in range(heads)]
    queries = [q_ref[:, lane] for lane in lanes]

    def score(key_block, tops):
        rows = pl.ds(pl.multiple_of(key_block * BLOCK, BLOCK), BLOCK)
        fresh = []
        for h in range(heads):
            s = masked_scores(k_ref[rows, lanes[h]], queries[h], key_block, block, starts)
            score_ref[h, rows, :] = s
            fresh.append(jnp.maximum(tops[h], jnp.max(s, axis=0, keepdims=True)))
        return tuple(fresh)

    lo = lo_ref[block]
    tops = lax.fori_loop(lo, block + 1, score, (jnp.full((1, BLOCK), -1e30, F32),) * heads)

    def weigh(key_block, carried):
        sums, totals = carried
        rows = pl.ds(pl.multiple_of(key_block * BLOCK, BLOCK), BLOCK)
        new_sums, new_totals = [], []
        for h in range(heads):
            p = jnp.exp(score_ref[h, rows, :] - tops[h])
            new_sums.append(sums[h] + jnp.sum(p, axis=0, keepdims=True))
            new_totals.append(totals[h] + dot(v_ref[rows, lanes[h]], p.astype(LOW), 0, 0))
        return tuple(new_sums), tuple(new_totals)

    sums, totals = lax.fori_loop(
        lo,
        block + 1,
        weigh,
        ((jnp.zeros((1, BLOCK), F32),) * heads, (jnp.zeros((HD, BLOCK), F32),) * heads),
    )
    turned = jnp.concatenate([totals[h] / sums[h] for h in range(heads)], axis=0)
    low = turned.T.astype(LOW)
    for chip in range(out_ref.shape[0]):
        out_ref[chip] = low


def attend(lows, starts, qkv, chips):
    count = qkv.shape[0]
    width = qkv.shape[1] // 3
    heads = width // HD
    return pl.pallas_call(
        functools.partial(attend_kernel, heads),
        grid_spec=pltpu.PrefetchScalarGridSpec(
            num_scalar_prefetch=1,
            grid=(count // BLOCK,),
            in_specs=[
                pl.BlockSpec((1, BLOCK), lambda i, lo: (0, i)),
                pl.BlockSpec((BLOCK, width), lambda i, lo: (i, 0)),
                pl.BlockSpec((count, width), lambda i, lo: (0, 1)),
                pl.BlockSpec((count, width), lambda i, lo: (0, 2)),
            ],
            out_specs=pl.BlockSpec((chips, BLOCK, width), lambda i, lo: (0, i, 0)),
            scratch_shapes=[pltpu.VMEM((heads, count, BLOCK), F32)],
        ),
        out_shape=jax.ShapeDtypeStruct((chips, count, width), LOW),
        compiler_params=pltpu.CompilerParams(vmem_limit_bytes=VMEM_LIMIT),
        cost_estimate=pl.CostEstimate(flops=10 * GIGA, bytes_accessed=0, transcendentals=0),
        name="attend",
    )(lows, starts, qkv, qkv, qkv)


def attend_back_kernel(
    heads,
    lo_ref,
    start_ref,
    q_ref,
    k_ref,
    v_ref,
    back_ref,
    cos_ref,
    sin_ref,
    out_ref,
    weight_ref,
    slope_ref,
    dk_ref,
    dv_ref,
):
    block = pl.program_id(0)
    width = heads * HD
    starts = start_ref[...]
    lanes = [slice(h * HD, (h + 1) * HD) for h in range(heads)]
    queries = [q_ref[:, lane] for lane in lanes]
    backs = [back_ref[:, lane] for lane in lanes]

    @pl.when(block == 0)
    def _():
        dk_ref[...] = jnp.zeros_like(dk_ref)
        dv_ref[...] = jnp.zeros_like(dv_ref)

    def score(key_block, tops):
        rows = pl.ds(pl.multiple_of(key_block * BLOCK, BLOCK), BLOCK)
        fresh = []
        for h in range(heads):
            s = masked_scores(k_ref[rows, lanes[h]], queries[h], key_block, block, starts)
            weight_ref[h, rows, :] = s
            slope_ref[h, rows, :] = dot(v_ref[rows, lanes[h]], backs[h], 1, 1)
            fresh.append(jnp.maximum(tops[h], jnp.max(s, axis=0, keepdims=True)))
        return tuple(fresh)

    lo = lo_ref[block]
    tops = lax.fori_loop(lo, block + 1, score, (jnp.full((1, BLOCK), -1e30, F32),) * heads)

    def weigh(key_block, carried):
        sums, deltas = carried
        rows = pl.ds(pl.multiple_of(key_block * BLOCK, BLOCK), BLOCK)
        new_sums, new_deltas = [], []
        for h in range(heads):
            p = jnp.exp(weight_ref[h, rows, :] - tops[h])
            weight_ref[h, rows, :] = p
            new_sums.append(sums[h] + jnp.sum(p, axis=0, keepdims=True))
            new_deltas.append(
                deltas[h] + jnp.sum(p * slope_ref[h, rows, :], axis=0, keepdims=True)
            )
        return tuple(new_sums), tuple(new_deltas)

    zero_row = (jnp.zeros((1, BLOCK), F32),) * heads
    sums, deltas = lax.fori_loop(lo, block + 1, weigh, (zero_row, zero_row))
    inverses = [1.0 / sums[h] for h in range(heads)]
    deltas = [deltas[h] * inverses[h] for h in range(heads)]

    def spread(key_block, totals):
        rows = pl.ds(pl.multiple_of(key_block * BLOCK, BLOCK), BLOCK)
        fresh, dks, dvs = [], [], []
        for h in range(heads):
            p = weight_ref[h, rows, :] * inverses[h]
            ds = (p * (slope_ref[h, rows, :] - deltas[h])).astype(LOW)
            dvs.append(dot(p.astype(LOW), backs[h], 1, 0))
            dks.append(dot(ds, queries[h], 1, 0))
            fresh.append(totals[h] + dot(k_ref[rows, lanes[h]], ds, 0, 0))
        dk_ref[rows, :] += jnp.concatenate(dks, axis=1)
        dv_ref[rows, :] += jnp.concatenate(dvs, axis=1)
        return tuple(fresh)

    totals = lax.fori_loop(lo, block + 1, spread, (jnp.zeros((HD, BLOCK), F32),) * heads)
    here = pl.ds(pl.multiple_of(block * BLOCK, BLOCK), BLOCK)
    dq = jnp.concatenate(totals, axis=0).T * (HD**-0.5)
    dq = dq * cos_ref[here, :] - swap_halves(dq) * sin_ref[here, :]
    out_ref[here, 0:width] = dq.astype(LOW)

    @pl.when(block == pl.num_programs(0) - 1)
    def _():
        def finish(index, carried):
            rows = pl.ds(pl.multiple_of(index * BLOCK, BLOCK), BLOCK)
            dk = dk_ref[rows, :] * (HD**-0.5)
            dk = dk * cos_ref[rows, :] - swap_halves(dk) * sin_ref[rows, :]
            out_ref[rows, width : 2 * width] = dk.astype(LOW)
            out_ref[rows, 2 * width : 3 * width] = dv_ref[rows, :].astype(LOW)
            return carried

        lax.fori_loop(0, dk_ref.shape[0] // BLOCK, finish, 0)


def attend_back(lows, starts, qkv, back, cos, sin):
    count = qkv.shape[0]
    width = qkv.shape[1] // 3
    heads = width // HD
    return pl.pallas_call(
        functools.partial(attend_back_kernel, heads),
        grid_spec=pltpu.PrefetchScalarGridSpec(
            num_scalar_prefetch=1,
            grid=(count // BLOCK,),
            in_specs=[
                pl.BlockSpec((1, BLOCK), lambda i, lo: (0, i)),
                pl.BlockSpec((BLOCK, width), lambda i, lo: (i, 0)),
                pl.BlockSpec((count, width), lambda i, lo: (0, 1)),
                pl.BlockSpec((count, width), lambda i, lo: (0, 2)),
                pl.BlockSpec((BLOCK, width), lambda i, lo: (i, 0)),
                pl.BlockSpec((count, width), lambda i, lo: (0, 0)),
                pl.BlockSpec((count, width), lambda i, lo: (0, 0)),
            ],
            out_specs=pl.BlockSpec((count, 3 * width), lambda i, lo: (0, 0)),
            scratch_shapes=[
                pltpu.VMEM((heads, count, BLOCK), F32),
                pltpu.VMEM((heads, count, BLOCK), F32),
                pltpu.VMEM((count, width), F32),
                pltpu.VMEM((count, width), F32),
            ],
        ),
        out_shape=jax.ShapeDtypeStruct((count, 3 * width), LOW),
        compiler_params=pltpu.CompilerParams(vmem_limit_bytes=VMEM_LIMIT),
        cost_estimate=pl.CostEstimate(flops=20 * GIGA, bytes_accessed=0, transcendentals=0),
        name="attend_back",
    )(lows, starts, qkv, qkv, qkv, back, cos, sin)


def blend_kernel(core_ref, x_ref, own_ref, other_ref, w_ref, unit_ref, mixed_ref, attended_ref):
    core = core_ref[0]
    pieces = []
    for chip in range(own_ref.shape[0]):
        own, other = own_ref[chip], other_ref[chip]
        pieces.append(jnp.where(core == 0, own, other))
        pieces.append(jnp.where(core == 0, other, own))
    attended = jnp.concatenate(pieces, axis=1)
    attended_ref[...] = attended
    mixed = x_ref[...].astype(F32) + dot(attended, w_ref[...], 1, 1)
    mixed_ref[...] = mixed
    inverse = lax.rsqrt(jnp.mean(mixed * mixed, axis=-1, keepdims=True) + EPSILON)
    unit_ref[...] = (mixed * inverse).astype(LOW)


def blend(core, x_all, own, other, w_out):
    count, features = x_all.shape
    chips, unused, width = own.shape
    return pl.pallas_call(
        blend_kernel,
        grid_spec=pltpu.PrefetchScalarGridSpec(
            num_scalar_prefetch=1,
            grid=(count // BLOCK,),
            in_specs=[
                pl.BlockSpec((BLOCK, features), lambda i, core: (i, 0)),
                pl.BlockSpec((chips, BLOCK, width), lambda i, core: (0, i, 0)),
                pl.BlockSpec((chips, BLOCK, width), lambda i, core: (0, i, 0)),
                pl.BlockSpec((features, features), lambda i, core: (0, 0)),
            ],
            out_specs=[
                pl.BlockSpec((BLOCK, features), lambda i, core: (i, 0)),
                pl.BlockSpec((BLOCK, features), lambda i, core: (i, 0)),
                pl.BlockSpec((BLOCK, features), lambda i, core: (i, 0)),
            ],
        ),
        out_shape=[
            jax.ShapeDtypeStruct((count, features), LOW),
            jax.ShapeDtypeStruct((count, features), F32),
            jax.ShapeDtypeStruct((count, features), LOW),
        ],
        compiler_params=pltpu.CompilerParams(vmem_limit_bytes=VMEM_LIMIT),
        cost_estimate=pl.CostEstimate(flops=15 * GIGA, bytes_accessed=0, transcendentals=0),
        name="blend",
    )(core, x_all, own, other, w_out)


def finish_kernel(parts, scaled_parts, rows_ref, gain_ref, *refs):
    weights = refs[:scaled_parts]
    grads = refs[scaled_parts : scaled_parts + parts]
    gain_grad_ref = refs[scaled_parts + parts]
    width = rows_ref.shape[2] // parts

    @pl.when(pl.program_id(0) == 0)
    def _():
        gain_grad_ref[...] = jnp.zeros_like(gain_grad_ref)

    gain = gain_ref[...]
    for part in range(parts):
        for index in range(rows_ref.shape[0]):
            lane = slice(index * width, (index + 1) * width)
            raw = rows_ref[index, :, part * width : (part + 1) * width].astype(F32)
            if part < scaled_parts:
                product = raw * weights[part][:, lane].astype(F32)
                gain_grad_ref[...] += jnp.sum(product, axis=1, keepdims=True)
                raw = raw * gain
            grads[part][:, lane] = raw


def finish(rows, gain, weights, parts):
    size, share, wide = rows.shape
    width = wide // parts
    column = pl.BlockSpec((share, 1), lambda i: (0, 0))
    held = min(size, max(1, 2048 // width))
    block = pl.BlockSpec((share, held * width), lambda i: (0, i))
    out = pl.pallas_call(
        functools.partial(finish_kernel, parts, len(weights)),
        grid=(size // held,),
        in_specs=[pl.BlockSpec((held, share, wide), lambda i: (i, 0, 0)), column]
        + [block] * len(weights),
        out_specs=[block] * parts + [column],
        out_shape=[jax.ShapeDtypeStruct((share, size * width), F32)] * parts
        + [jax.ShapeDtypeStruct((share, 1), F32)],
        compiler_params=pltpu.CompilerParams(vmem_limit_bytes=VMEM_LIMIT),
        name="finish",
    )(rows, gain, *weights)
    return out[:parts], out[parts][:, 0]


def local(
    tokens,
    cotangent,
    doc_lengths,
    gain_attn,
    w_query,
    w_key,
    w_value,
    w_out,
    gain_mlp,
    w_gate,
    w_up,
    w_down,
):
    rows, features = tokens.shape
    n_c, n_f = lax.axis_size("ctx"), lax.axis_size("fsdp")
    group = rows * n_c
    width = features // n_c
    here = lax.axis_index("ctx") * rows
    share = w_query.shape[0]

    core = (lax.axis_index("ctx") % 2).astype(jnp.int32).reshape(1)
    square = lax.axis_size("fsdp") == 4

    def pull_near(block, *others):
        return near(after(block, *others)) if square else ()

    def pull_far(pieces):
        return far(pieces) if square else ()

    def pulled(block, near_pieces, far_pieces):
        if square:
            return (block,) + tuple(near_pieces) + tuple(far_pieces)
        return (lax.all_gather(block, "fsdp", axis=0, tiled=True),)

    def push_near(part):
        return reduce_near(part) if square else ()

    def push_far(part, landed):
        return reduce_far(part, landed) if square else ()

    def pushed(part, landed, last):
        if square:
            return reduce_own(part, landed, last).astype(LOW)
        return lax.psum_scatter(part[0], "fsdp", scatter_dimension=0, tiled=True)

    def to_rows(value):
        value = value.reshape(n_c, share, -1)
        return lax.all_to_all(value, "ctx", split_axis=0, concat_axis=0, tiled=True)

    me = lax.axis_index("fsdp")
    if square:
        places = [(me ^ bits) * 2 + low for bits in range(4) for low in range(2)]
        order = [
            (me ^ bits) * 2 + low
            for bits, low in ((3, 0), (1, 0), (3, 1), (2, 1), (2, 0), (1, 1), (0, 0), (0, 1))
        ]
        outs = (2, 2, 4)
    else:
        places = order = range(features // UNIT)
        outs = (features // UNIT,)
    places, order = (jnp.stack([jnp.int32(place) for place in p]) for p in (places, order))

    gain_a = gain_attn.astype(F32)[:, None]
    gain_m = gain_mlp.astype(F32)[:, None]

    def scaled(weight, gain):
        return (weight.astype(F32) * gain).astype(LOW)


    def paired(left, right):
        return jnp.concatenate(
            [left.reshape(share, n_c, -1), right.reshape(share, n_c, -1)], axis=2
        ).reshape(share, -1)

    x_all = lax.all_gather(tokens, "ctx", axis=0, tiled=True)
    stacked = jnp.concatenate(
        [
            scaled(w, gain_a).reshape(share, n_c, width)
            for w in (w_query, w_key, w_value)
        ],
        axis=2,
    ).reshape(share, 3 * features)
    out_all = lax.all_gather(after(w_out, stacked), ("fsdp", "ctx"), axis=0, tiled=True)
    qkv_rows = to_columns(by_owner(stacked))
    qkv_near = pull_near(qkv_rows)
    two_rows = to_columns(
        after(by_owner(paired(scaled(w_gate, gain_m), scaled(w_up, gain_m))), qkv_rows)
    )
    qkv_far = pull_far(qkv_near)
    w_qkv = pulled(qkv_rows, qkv_near, qkv_far)

    position = jnp.arange(group, dtype=jnp.int32)
    doc_ends = jnp.cumsum(doc_lengths[0])
    doc_starts = doc_ends - doc_lengths[0]
    starts = jnp.max(
        jnp.where(position[:, None] >= doc_starts[None, :], doc_starts[None, :], 0), axis=1
    ).astype(jnp.int32)
    turns = (position - starts).astype(F32)
    half = HD // 2
    lane = jnp.arange(128, dtype=jnp.int32)
    inv_freq = ROPE_BASE ** (-2.0 * (lane % half).astype(F32) / HD)
    angles = turns[:, None] * inv_freq[None, :]
    sign = jnp.where(lane % HD < half, -1.0, 1.0).astype(F32)
    cos = jnp.tile(jnp.cos(angles), (1, width // 128))
    sin = jnp.tile(jnp.sin(angles) * sign[None, :], (1, width // 128))
    lows = starts[::BLOCK] // BLOCK
    starts_row = starts[None, :]

    unit, qkv = project(places, x_all, w_qkv, cos, sin)
    attended = attend(lows, starts_row, qkv, n_c // 2)
    down_rows = to_columns(after(by_owner(w_down), two_rows, attended))
    two_near = pull_near(two_rows)
    attended_mine = spread_cores(after(attended, down_rows))
    two_far = pull_far(two_near)
    down_near = pull_near(down_rows, *two_near)
    attended_mine = after(attended_mine, *two_far)
    back_all = lax.all_gather(after(cotangent, attended_mine), "ctx", axis=0, tiled=True)
    attended_other = other_core(attended_mine)
    unit_mlp, mixed, attended_all = blend(core, x_all, attended_mine, attended_other, out_all)
    col_two = pulled(two_rows, two_near, two_far)
    down_near = tuple(after(piece, unit_mlp) for piece in down_near)
    down_far = pull_far(down_near)
    col_down = pulled(down_rows, down_near, down_far)

    gate, up, hidden = open_units(places, unit_mlp, col_two)
    d_both = close_units(places, back_all, gate, up, col_down)
    d_unit_sums = pair_sums(times_rows(places, core, d_both, col_two, n_c // 2))
    d_unit_landed = swap_chips(d_unit_sums)
    part_down = weight_grad(order, outs, (after(back_all, d_unit_sums), hidden[None]))
    down_landed = push_near(part_down)
    part_gate = weight_grad(order, outs, (after(unit_mlp, part_down[0]), d_both[:1]))
    part_up = weight_grad(order, outs, (after(unit_mlp, part_gate[0]), d_both[1:]))
    mixed_own = lax.dynamic_slice_in_dim(mixed, here, rows, 0)
    d_unit = total(after(d_unit_landed, *down_landed, part_up[0]))

    inverse_own = lax.rsqrt(jnp.mean(mixed_own * mixed_own, axis=-1, keepdims=True) + EPSILON)
    unit_own = mixed_own * inverse_own
    d_mixed = cotangent.astype(F32) + inverse_own * (
        d_unit - unit_own * jnp.mean(d_unit * unit_own, axis=-1, keepdims=True)
    )
    d_mixed_low = d_mixed.astype(LOW)
    d_att = dot(d_mixed_low, out_all, 1, 0).astype(LOW)
    branch = times_rows(places, core, after(hidden, d_att)[None], col_down)
    down_landed = tuple(after(piece, d_att) for piece in down_landed)
    owners = jnp.swapaxes(d_mixed_low.reshape(rows, n_f, n_c, share), 1, 2)
    both_ways = jnp.concatenate(
        [d_att.reshape(rows, n_c, width), owners.reshape(rows, n_c, n_f * share)], axis=2
    ).reshape(rows, -1)
    d_att_own = lax.all_to_all(both_ways, "ctx", split_axis=1, concat_axis=0, tiled=True)
    down_last = push_far(part_down, down_landed)
    part_gate = [after(part, *down_last) for part in part_gate]
    gate_landed = push_near(part_gate)
    gate_last = push_far(part_gate, gate_landed)
    d_att_own = after(d_att_own, branch, *down_last)
    branch_own = lax.psum_scatter(
        after(branch, d_att_own), "ctx", scatter_dimension=0, tiled=True
    )
    part_up = [after(part_up[0], d_att_own)] + list(part_up[1:])
    if square:
        part_up[1] = after(part_up[1], d_att_own)
    up_landed = push_near(part_up)
    up_last = push_far(part_up, up_landed)
    rows_down = to_rows(after(pushed(part_down, down_landed, down_last), d_att_own))

    d_qkv = attend_back(lows, starts_row, qkv, d_att_own, cos, sin)
    first_part = times_rows(places, core, d_qkv[None], w_qkv)
    first_part = after(first_part, rows_down, *gate_landed, *up_landed)
    d_first = lax.psum_scatter(first_part, "ctx", scatter_dimension=0, tiled=True).astype(F32)
    part_qkv = weight_grad(
        order, outs, (unit, after(d_qkv, first_part)[None])
    )
    part_out = dot(after(d_att_own, part_qkv[0])[:, width:], attended_all, 0, 0).astype(LOW)
    if square:
        part_out = part_out.reshape(n_f, share, features)
        terms = [lax.dynamic_index_in_dim(part_out, me ^ bits, 0, False) for bits in range(4)]
        for bits in range(1, 4):
            terms[bits] = lax.ppermute(terms[bits], "fsdp", flip("fsdp", 4, bits))
        grad_out = sum(term.astype(F32) for term in terms)
    else:
        grad_out = lax.psum_scatter(part_out, "fsdp", scatter_dimension=0, tiled=True).astype(F32)
    part_qkv = [after(part, *up_last, *gate_last) for part in part_qkv]
    qkv_landed = push_near(part_qkv)
    two_mine = jnp.concatenate(
        [pushed(part_gate, gate_landed, gate_last), pushed(part_up, up_landed, up_last)], axis=1
    )
    rows_two = after(to_rows(after(two_mine, rows_down)), grad_out, *qkv_landed)
    qkv_last = push_far(part_qkv, qkv_landed)
    rows_qkv = to_rows(after(pushed(part_qkv, qkv_landed, qkv_last), rows_two))

    layer_out = (mixed_own + after(branch_own, rows_two).astype(F32)).astype(LOW)
    x_own = tokens.astype(F32)
    inverse = lax.rsqrt(jnp.mean(x_own * x_own, axis=-1, keepdims=True) + EPSILON)
    first_own = x_own * inverse
    grad_tokens = d_mixed + inverse * (
        d_first - first_own * jnp.mean(d_first * first_own, axis=-1, keepdims=True)
    )

    rows_qkv = after(rows_qkv, layer_out, grad_tokens)
    (grad_down,), unused = finish(rows_down, gain_m, (), 1)
    (grad_gate, grad_up), grad_gain_mlp = finish(rows_two, gain_m, (w_gate, w_up), 2)
    (grad_query, grad_key, grad_value), grad_gain_attn = finish(
        rows_qkv, gain_a, (w_query, w_key, w_value), 3
    )
    return (
        layer_out,
        grad_tokens,
        grad_gain_attn,
        grad_query,
        grad_key,
        grad_value,
        grad_out,
        grad_gain_mlp,
        grad_gate,
        grad_up,
        grad_down,
    )


def solution(mesh):
    split = P(("fsdp", "ctx"))
    rows = P(("fsdp", "ctx"), None)
    in_specs = (rows, rows, P("fsdp", None), split, rows, rows, rows, rows, split, rows, rows, rows)
    out_specs = (rows, rows, split, rows, rows, rows, rows, split, rows, rows, rows)
    return jax.shard_map(local, mesh=mesh, in_specs=in_specs, out_specs=out_specs, check_vma=False)
```
